512 devices in a mesh: tx: 32 (over x, y, core), ty: 16 (over z).
Axes of the slice: x: 4, y: 4, z: 16, core: 2. Of those that a mesh axis runs over, the one named last changes fastest.
Arguments:
- source: float32 [20, 512, 2048], P(None, 'tx', 'ty'), may hold values from -6 to 6
- kappa_sq: float32 [20, 512, 2048], P(None, 'tx', 'ty'), may hold values from 0.05 to 0.5
- lon_diff: float32 [20, 512, 2048], P(None, 'tx', 'ty'), may hold values from 8 to 64
- lat_diff: float32 [20, 512, 2048], P(None, 'tx', 'ty'), may hold values from 8 to 64
- sea_mask: int32 [20, 512, 2048], P(None, 'tx', 'ty'), may hold values 0 or 1
Outputs:
- solution: float32 [20, 512, 2048], P(None, 'tx', 'ty')
- residual: float32 [20, 512, 2048], P(None, 'tx', 'ty')
The draws below stay inside these ranges and needn't reach their ends.
All inputs are finite; a program needn't handle non-finite values. No bound on the sum of `sea_mask` on one device may be relied on, other than what follows from the above.
Results may differ from the reference program's by a relative error of at most 0.0003.
Values sent between devices are 32-bit elements; how exact they have to be, the bound alone decides.
A program may use at most 128 MiB of HBM per device.

```python
import math
import jax
import jax.numpy as jnp
from jax import lax

NZ = 20
LEVELS = 4
COARSE_SWEEPS = 20
NLON = 512
NLAT = 2048


def touch_ends(drawn, own_key, low, high):
    longest = drawn.shape.index(max(drawn.shape))
    spots = []
    for shift in (0, 1):
        where = [jax.random.randint(jax.random.fold_in(own_key, axis), (), 0, length) for axis, length in enumerate(drawn.shape)]
        where[longest] = (where[longest] + shift) % drawn.shape[longest]
        spots.append(tuple(where))
    return drawn.at[spots[0]].set(low).at[spots[1]].set(high)


def block_levels(rng, shape, shards, smallest, top_value):
    def one(axis_at, parts):
        heights = jax.random.uniform(jax.random.fold_in(jax.random.fold_in(rng, 6), axis_at), (parts,), jnp.float32, smallest / len(shards), top_value / len(shards))
        return jnp.repeat(jnp.exp(heights), shape[axis_at] // parts).reshape((-1,) + (1,) * (len(shape) - axis_at - 1))

    level = one(*shards[0])
    for cut in shards[1:]:
        level = level * one(*cut)
    return level


def gaussian(rng, extent, spread, bound, cuts=(), dtype=jnp.bfloat16):
    result = spread * jax.random.normal(rng, extent, jnp.float32)
    if cuts:
        result = result * block_levels(rng, extent, cuts, -0.22, 0.18)
    return jnp.clip(result, -bound, bound).astype(dtype)


def setup_inputs(seed: int = 0) -> dict:
    streams_of = jax.random.split(jax.random.key(seed), 6)
    source = gaussian(streams_of[0], (NZ, NLON, NLAT), 1.0, 6.0, ((1, 32), (2, 16)), jnp.float32)
    kappa_sq = jnp.clip(jnp.exp(math.log(0.5) - 2.3025851 * jax.random.uniform(streams_of[1], (NZ, NLON, NLAT), jnp.float32) ** block_levels(streams_of[1], (NZ, NLON, NLAT), ((1, 32), (2, 16)), -0.2, 0.2)), 0.05, 0.5)
    lon_diff = jnp.clip(jnp.exp(math.log(64.0) - 2.0794415 * jax.random.uniform(streams_of[2], (NZ, NLON, NLAT), jnp.float32) ** block_levels(streams_of[2], (NZ, NLON, NLAT), ((1, 32), (2, 16)), -0.2, 0.2)), 8.0, 64.0)
    lat_diff = jnp.clip(jnp.exp(math.log(64.0) - 2.0794415 * jax.random.uniform(streams_of[3], (NZ, NLON, NLAT), jnp.float32) ** block_levels(streams_of[3], (NZ, NLON, NLAT), ((1, 32), (2, 16)), -0.2, 0.2)), 8.0, 64.0)
    sea_mask = touch_ends((jax.random.randint(streams_of[4], (NZ, NLON, NLAT), 0, 5) < 4).astype(jnp.int32), jax.random.fold_in(streams_of[4], 1), 0, 1)
    return dict(source=source, kappa_sq=kappa_sq, lon_diff=lon_diff, lat_diff=lat_diff, sea_mask=sea_mask)


OMEGA = 0.8
VERT = 1.0


def shift_up(field):
    return jnp.concatenate([field[1:], jnp.zeros_like(field[:1])], axis=0)


def shift_down(field):
    return jnp.concatenate([jnp.zeros_like(field[:1]), field[:-1]], axis=0)


def east_of(field):
    return jnp.roll(field, -1, axis=1)


def west_of(field):
    return jnp.roll(field, 1, axis=1)


def north_of(field):
    return jnp.concatenate([field[:, :, 1:], jnp.zeros_like(field[:, :, :1])], axis=2)


def south_of(field):
    return jnp.concatenate([jnp.zeros_like(field[:, :, :1]), field[:, :, :-1]], axis=2)


def build_faces(kappa, lond, latd, sea):
    lon_weight = sea * lond
    lat_weight = sea * latd
    face_east = 0.5 * (lon_weight * east_of(sea) + sea * east_of(lon_weight))
    face_west = 0.5 * (lon_weight * west_of(sea) + sea * west_of(lon_weight))
    face_north = 0.5 * (lat_weight * north_of(sea) + sea * north_of(lat_weight))
    face_south = 0.5 * (lat_weight * south_of(sea) + sea * south_of(lat_weight))
    face_up = VERT * sea * shift_up(sea)
    face_down = VERT * sea * shift_down(sea)
    diagonal = sea * kappa + (face_west + face_east + face_south + face_north + face_down + face_up) + (1.0 - sea)
    return (face_west, face_east, face_south, face_north, face_down, face_up, diagonal)


def apply_op(field, faces):
    total = faces[0] * west_of(field) + faces[1] * east_of(field) + faces[2] * south_of(field) + faces[3] * north_of(field) + faces[4] * shift_down(field) + faces[5] * shift_up(field)
    return faces[6] * field - total


def sweep(field, right, faces):
    return field + OMEGA * (right - apply_op(field, faces)) / faces[6]


def block_mean(field):
    depth, wide, tall = field.shape
    return field.reshape(depth, wide // 2, 2, tall // 2, 2).mean(axis=(2, 4))


def block_max(field):
    depth, wide, tall = field.shape
    return field.reshape(depth, wide // 2, 2, tall // 2, 2).max(axis=(2, 4))


def prolong(field):
    return jnp.repeat(jnp.repeat(field, 2, axis=1), 2, axis=2)


def coarsen(params):
    kappa, lond, latd, sea = params
    return (block_mean(kappa), 0.25 * block_mean(lond), 0.25 * block_mean(latd), block_max(sea))


def cycle(level, right, params, faces_all):
    faces = faces_all[level]
    if level == LEVELS:
        field = OMEGA * right / faces[6]

        def step_fn(step, current):
            return sweep(current, right, faces)

        return lax.fori_loop(0, COARSE_SWEEPS - 1, step_fn, field)
    field = OMEGA * right / faces[6]
    field = sweep(field, right, faces)
    remain = right - apply_op(field, faces)
    correction = cycle(level + 1, block_mean(remain), params, faces_all)
    field = field + prolong(correction)
    field = sweep(field, right, faces)
    field = sweep(field, right, faces)
    return field


def reference(source, kappa_sq, lon_diff, lat_diff, sea_mask):
    sea = sea_mask.astype(jnp.float32)
    params = [(kappa_sq, lon_diff, lat_diff, sea)]
    for level in range(LEVELS):
        params.append(coarsen(params[-1]))
    faces_all = [build_faces(*params[level]) for level in range(LEVELS + 1)]
    solution = cycle(0, source, params, faces_all)
    residual = source - apply_op(solution, faces_all[0])
    return solution, residual
```

```python
import jax
import jax.numpy as jnp
from jax import lax
from jax.experimental import pallas as pl
from jax.experimental.pallas import tpu as pltpu
from jax.sharding import PartitionSpec as P

NZ = 20
HZ = 10
NTX = 32
NTY = 16
OMEGA = 0.8
UNROLL = 20
MESH = pl.DeviceIdType.MESH
F32 = jnp.float32

DIAGONALS = ((1, 1), (-1, 1), (1, -1), (-1, -1))


def iota(shape, dim):
    return lax.broadcasted_iota(jnp.int32, shape, dim)


def mm(x, m):
    high = x.astype(jnp.bfloat16)
    low = (x - high.astype(F32)).astype(jnp.bfloat16)
    m = m.astype(jnp.bfloat16)
    return lax.dot_general(
        jnp.concatenate([high, low], axis=1), jnp.concatenate([m, m], axis=0),
        (((1,), (0,)), ((), ())), preferred_element_type=F32,
    )


def roll(x, shift, axis):
    shift = shift % x.shape[axis]
    return x if shift == 0 else pltpu.roll(x, shift, axis)


def one_hot(shape, hit, value=1.0):
    row, col = iota(shape, 0), iota(shape, 1)
    return jnp.where(hit(row, col), F32(value), F32(0.0))


def restrict_0():
    return one_hot((128, 128), lambda n, m: m == 32 + (n >> 1), 0.25)


def restrict_1():
    return one_hot((256, 128), lambda n, m: m == n >> 1, 0.25)


def restrict_2():
    return one_hot((128, 128), lambda n, m: m == (n & 64) + 8 + ((n & 63) >> 1), 0.25)


def restrict_3():
    def hit(n, m):
        q = n & 63
        return (m == (n & 64) + 16 + (q >> 1)) & (q >= 16) & (q < 32)

    return one_hot((128, 128), hit, 0.25)


def restrict_all():
    return one_hot((256, 128), lambda n, m: m == ((n & 128) >> 1) + 24 + ((n & 127) >> 4), 1.0 / 256)


def prolong_3():
    return one_hot((128, 128), lambda m, n: m == (n & 64) + 16 + ((n & 63) >> 1))


def prolong_2():
    return one_hot((128, 128), lambda m, n: m == (n & 64) + 8 + ((n & 63) >> 1))


def prolong_1():
    return one_hot((128, 256), lambda m, n: m == n >> 1)


def prolong_0():
    def hit(m, n):
        rel = jnp.where(n >= 192, n - 256, n)
        return (m == 32 + (rel >> 1)) & (rel < 132) & (rel >= -4)

    return one_hot((128, 256), hit)


class Level:
    def __init__(self, slabs, folded, refs):
        self.slabs = slabs
        self.folded = folded
        self.e, self.n, self.v, self.g, self.d, self.c, self.u, self.w = refs

    def each(self, body, unroll):
        def step(z, carry):
            body(z)
            return carry

        lax.fori_loop(0, self.slabs, step, 0, unroll=min(unroll, self.slabs))

    def wrap(self, ref):
        if self.folded:
            ref[0] = roll(ref[self.slabs], 64, 1)
            ref[self.slabs + 1] = roll(ref[1], 64, 1)

    def clear_ends(self):
        if not self.folded:
            for ref in (self.u, self.w):
                ref[0] = jnp.zeros_like(ref[0])
                ref[self.slabs + 1] = jnp.zeros_like(ref[0])

    def faces(self, kap, lond, latd, sea, unroll):
        top = self.slabs - 1

        def vertical(z):
            here = sea(z)
            self.v[z + 1] = here * sea(z + 1)

        lax.fori_loop(0, top, lambda z, c: (vertical(z), c)[1], 0, unroll=min(unroll, top))
        if self.folded:
            low = iota(self.v.shape[1:], 1) < 64
            self.v[self.slabs] = jnp.where(low, sea(top) * roll(sea(0), 64, 1), 0.0)
            self.v[0] = roll(self.v[self.slabs], 64, 1)
        else:
            self.v[0] = jnp.zeros_like(self.v[0])
            self.v[self.slabs] = jnp.zeros_like(self.v[0])

        def horizontal(z):
            s = sea(z)
            lw = s * lond(z)
            tw = s * latd(z)
            east = 0.5 * (lw * roll(s, -1, 0) + s * roll(lw, -1, 0))
            north = 0.5 * (tw * roll(s, -1, 1) + s * roll(tw, -1, 1))
            west = roll(east, 1, 0)
            south = roll(north, 1, 1)
            diag = s * kap(z) + (west + east + south + north + self.v[z] + self.v[z + 1]) + (1.0 - s)
            self.e[z] = east
            self.n[z] = north
            self.d[z] = diag
            self.g[z] = OMEGA / diag

        self.each(horizontal, unroll)

    def total(self, src, z):
        u = src[z + 1]
        e = self.e[z]
        n = self.n[z]
        return u, (
            roll(e * u, 1, 0)
            + e * roll(u, -1, 0)
            + roll(n * u, 1, 1)
            + n * roll(u, -1, 1)
            + self.v[z] * src[z]
            + self.v[z + 1] * src[z + 2]
        )

    def sweep(self, src, dst, unroll):
        def body(z):
            u, total = self.total(src, z)
            dst[z + 1] = (1.0 - OMEGA) * u + self.c[z] + self.g[z] * total

        self.each(body, unroll)
        self.wrap(dst)

    def start(self, unroll):
        def body(z):
            self.u[z + 1] = self.c[z]

        self.each(body, unroll)
        self.wrap(self.u)

    def remain(self, src, z):
        u, total = self.total(src, z)
        return self.d[z] * (1.25 * self.c[z] - u) + total


def pack_edge(slabs, width, base, count):
    lane = iota(slabs[0].shape, 1)
    out = roll(slabs[0], -base, 1)
    for i in range(1, count):
        out = jnp.where(lane >= width * i, roll(slabs[i], width * i - base, 1), out)
    return out


def body(
    source_in, kappa_in, lon_in, lat_in, mask_in,
    sol_out, resid_out,
    sol, resid, out_sem, source, kappa, lon_diff, lat_diff, mask, in_sem,
    raw0, src0, l0, raw1, l1, raw2, l2, raw3, l3, raw4, l4, t0, t1, t2, t3, t4, q1,
    a_ew, a_ns, a_rew, a_rns, a_rd,
    b_pk, b_ns, b_nc, b_rpk, b_rns, b_rnc,
    f_p, f_rp,
    k_blk, k_z, k_ev, k_od,
    p_pk, p_ns, p_nc, p_rpk, p_rns, p_rnc, g_p, g_rp, h_blk, h_z, h_ev, h_od,
    o_ew, o_ns, o_rew, o_rns, o_rd,
    send_sem, recv_sem,
):
    mx, my = lax.axis_index("tx"), lax.axis_index("ty")
    odd = lax.rem(mx, 2) == 1
    counter = [0]
    pending = []

    def copy(src, dst, dx, dy):
        i = counter[0]
        counter[0] += 1
        made = pltpu.make_async_remote_copy(
            src_ref=src, dst_ref=dst, send_sem=send_sem.at[i], recv_sem=recv_sem.at[i],
            device_id=(lax.rem(mx + (dx + NTX), NTX), lax.rem(my + (dy + NTY), NTY)),
            device_id_type=MESH,
        )
        made.start()
        pending.append(made)
        return made

    def arrive(copies):
        for made in copies:
            made.wait_recv()

    lev0 = Level(NZ, False, l0)
    lev1 = Level(NZ, False, l1)
    lev2 = Level(HZ, True, l2)
    lev3 = Level(HZ, True, l3)
    lev4 = Level(HZ, True, l4)

    fetched = [
        pltpu.make_async_copy(src, dst, in_sem.at[i])
        for i, (src, dst) in enumerate((
            (mask_in, mask), (lon_in, lon_diff), (lat_in, lat_diff), (kappa_in, kappa), (source_in, source)
        ))
    ]
    for made in fetched:
        made.start()

    peers = [(2 * k, 0) for k in range(1, 16)] + [(1, 0), (-1, 0), (3, 0), (-3, 0)]
    peers += [(0, d) for d in (1, 2, 3, -1, -2, -3)] + list(DIAGONALS)
    barrier = pltpu.get_barrier_semaphore()
    for dx, dy in peers:
        pl.semaphore_signal(
            barrier, inc=1,
            device_id=(lax.rem(mx + (dx + NTX), NTX), lax.rem(my + (dy + NTY), NTY)),
            device_id_type=MESH,
        )

    for made in fetched:
        made.wait()

    def own0(z):
        s = mask[z].astype(F32)
        return (kappa[z], s * lon_diff[z], s * lat_diff[z], source[z])

    lane16 = iota((16, 128), 1)
    edge_n = [jnp.zeros((16, 128), F32)] * 4
    edge_s = [jnp.zeros((16, 128), F32)] * 4
    for z in range(NZ):
        for f, x in enumerate(own0(z)):
            raw0[f, z, 0:16, 0:128] = x
            a_ew[0, f * NZ + z] = x[0:2]
            a_ew[1, f * NZ + z] = x[14:16]
            if f == 1:
                a_ew[0, 4 * NZ + z // 2, z % 2:z % 2 + 1] = x[2:3]
                a_ew[1, 4 * NZ + z // 2, z % 2:z % 2 + 1] = x[13:14]
            edge_n[f] = jnp.where(lane16 >= 4 * z, roll(x, 4 * z - 124, 1), edge_n[f])
            edge_s[f] = jnp.where(lane16 >= 4 * z, roll(x, 4 * z, 1), edge_s[f])
    for f in range(4):
        a_ns[0, f] = edge_n[f]
        a_ns[1, f] = edge_s[f]

    pl.semaphore_wait(barrier, len(peers))

    def send_edges(ew, ns, rew, rns, rd):
        made = [copy(ew.at[0], rew.at[0], -1, 0), copy(ew.at[1], rew.at[1], 1, 0)]
        made += [copy(ns.at[0], rns.at[0], 0, 1), copy(ns.at[1], rns.at[1], 0, -1)]
        made.append(copy(ns.at[0, :, 8:16, :], rd.at[0], 1, 1))
        made.append(copy(ns.at[0, :, 0:8, :], rd.at[1], -1, 1))
        made.append(copy(ns.at[1, :, 8:16, :], rd.at[2], 1, -1))
        made.append(copy(ns.at[1, :, 0:8, :], rd.at[3], -1, -1))
        return made

    has_s, has_n = my > 0, my < NTY - 1

    def merge_edges(f, rows, rns, rd, put_rows, put_side):
        sub = iota((8, 128), 0)
        south = jnp.concatenate([rns[0, f], jnp.where(sub < 4, rd[1, f], rd[0, f])], axis=0)
        north = jnp.concatenate([rns[1, f], jnp.where(sub < 4, rd[3, f], rd[2, f])], axis=0)
        lane = iota((24, 128), 1)
        south = jnp.where(has_s, south, 0.0)
        north = jnp.where(has_n, north, 0.0)
        for z in range(NZ):
            put_rows(z, rows(z))
            side = jnp.where(lane < 4, roll(north, -4 * z, 1), roll(south, 124 - 4 * z, 1))
            put_side(z, jnp.where((lane < 4) | (lane >= 124), side, 0.0))

    sent_a = send_edges(a_ew, a_ns, a_rew, a_rns, a_rd)

    m0 = restrict_0()

    def down_0(x):
        t1[...] = mm(x.reshape(NZ * 16, 128), m0).reshape(NZ, 16, 128)
        return t1[:, pl.ds(0, 8, stride=2), :] + t1[:, pl.ds(1, 8, stride=2), :]

    def pack_1(x, f, pk, ns, nc):
        lane = iota((8, 128), 1)
        for k in range(HZ):
            pk[f * HZ + k] = jnp.where(lane < 64, roll(x[k], -32, 1), roll(x[k + HZ], 32, 1))
        for k in range(5):
            group = [x[k + 5 * j] for j in range(4)]
            for side, base in ((0, 64), (1, 32)):
                edge = pack_edge(group, 32, base, 4)
                ns[side, f * 5 + k] = edge
                nc[side, 0, f * 5 + k] = edge[0:4]
                nc[side, 1, f * 5 + k] = edge[4:8]

    def send_1(pk, ns, nc, rpk, rns, rnc):
        made = [copy(pk, rpk.at[0], -1, 0), copy(pk, rpk.at[1], 1, 0)]
        made += [copy(ns.at[0], rns.at[0], 0, 1), copy(ns.at[1], rns.at[1], 0, -1)]
        made.append(copy(nc.at[0, 1], rnc.at[0, 1], 1, 1))
        made.append(copy(nc.at[0, 0], rnc.at[0, 0], -1, 1))
        made.append(copy(nc.at[1, 1], rnc.at[1, 1], 1, -1))
        made.append(copy(nc.at[1, 0], rnc.at[1, 0], -1, -1))
        return made

    def merge_1(f, own, rpk, rns, rnc, put):
        lane = iota((8, 128), 1)
        blank = jnp.zeros((4, 128), F32)

        def edge(side, i, at):
            if i == 0:
                return rns[side, at]
            if i == 1:
                return jnp.concatenate([rnc[side, 0, at], blank], axis=0)
            return jnp.concatenate([blank, rnc[side, 1, at]], axis=0)

        for z in range(NZ):
            k, shift = (z, 32) if z < HZ else (z - HZ, -32)
            middle = (own(z), roll(rpk[0, f * HZ + k], shift, 1), roll(rpk[1, f * HZ + k], shift, 1))
            for i, start in ((0, 8), (1, 16), (2, 0)):
                south = jnp.where(has_s, roll(edge(0, i, f * 5 + z % 5), -32 * (z // 5), 1), 0.0)
                north = jnp.where(has_n, roll(edge(1, i, f * 5 + z % 5), 96 - 32 * (z // 5), 1), 0.0)
                put(z, start, jnp.where(lane < 32, south, jnp.where(lane < 96, middle[i], north)))

    own1 = [
        down_0(kappa[...]),
        0.25 * down_0(lon_diff[...]),
        0.25 * down_0(lat_diff[...]),
        (down_0(mask[...].astype(F32)) > 0.0).astype(F32),
    ]
    for f in range(4):
        pack_1(own1[f], f, p_pk, p_ns, p_nc)
        raw1[f, :, 8:16, :] = own1[f]
    sent_p1 = send_1(p_pk, p_ns, p_nc, p_rpk, p_rns, p_rnc)

    mall = restrict_all()

    def down_all(x):
        pair = jnp.concatenate([x[0:HZ], x[HZ:NZ]], axis=2).reshape(HZ * 16, 256)
        return jnp.sum(mm(pair, mall).reshape(HZ, 16, 128), axis=1)

    sea4 = (down_all(mask[...].astype(F32)) > 0.0).astype(F32)
    h_blk[0:10, :] = down_all(kappa[...])
    h_blk[10:20, :] = sea4 * (down_all(lon_diff[...]) * (1.0 / 256))
    h_blk[20:30, :] = sea4 * (down_all(lat_diff[...]) * (1.0 / 256))
    h_blk[30:32, :] = jnp.zeros((2, 128), F32)

    def send_z(blk, slots):
        slots[3] = blk[...]
        return [copy(blk, slots.at[3 - d], 0, d) for d in (1, -1, 2, -2, 3, -3)]

    def window_row(slots, count):
        row = jnp.zeros((count, 128), F32)
        for s in range(7):
            inside = (my + (s - 3) >= 0) & (my + (s - 3) < NTY)
            row = row + jnp.where(inside, roll(slots[s], 8 * (s - 3), 1), 0.0)
        return row

    def send_plane(row, ev, count):
        own = pl.ds(8 * count, count)
        ev[own, :] = row
        return [
            copy(ev.at[own], ev.at[pl.ds(((8 - k) % 16) * count, count)], 2 * k, 0)
            for k in (1, 15, 2, 14, 3, 13, 4, 12, 5, 11, 6, 10, 7, 9, 8)
        ]

    def send_sibling(ev, od):
        i = counter[0]
        counter[0] += 1
        made = pltpu.make_async_remote_copy(
            src_ref=ev, dst_ref=od, send_sem=send_sem.at[i], recv_sem=recv_sem.at[i],
            device_id=(mx + 1 - 2 * lax.rem(mx, 2), my), device_id_type=MESH,
        )
        made.start()
        pending.append(made)
        return [made]

    def window_slab(ev, od, index, count, put):
        put(pl.ds(0, 16, stride=2), ev[pl.ds(index, 16, stride=count), :])
        other = od[pl.ds(index, 16, stride=count), :]
        put(pl.ds(1, 16, stride=2), jnp.where(odd, roll(other, -1, 0), other))

    sent_hz = send_z(h_blk, h_z)

    arrive(sent_a)
    for f in range(4):
        def put_rows(z, x):
            raw0[f, z, 16:24, 0:128] = x

        def put_side(z, x):
            raw0[f, z, :, 128:256] = x

        def rows(z):
            pick = slice(z % 2, z % 2 + 1)
            blank = jnp.zeros((1, 128), F32)
            near, far = [blank], [blank]
            if f == 1:
                near, far = [a_rew[0, 4 * NZ + z // 2, pick]], [a_rew[1, 4 * NZ + z // 2, pick]]
            return jnp.concatenate(
                [a_rew[0, f * NZ + z]] + near + [blank, blank] + far + [a_rew[1, f * NZ + z]], axis=0
            )

        merge_edges(f, rows, a_rns, a_rd, put_rows, put_side)

    def sea0(z):
        return (raw0[1, z] > 0.0).astype(F32)

    lev0.faces(lambda z: raw0[0, z], lambda z: raw0[1, z], lambda z: raw0[2, z], sea0, UNROLL)
    lev0.clear_ends()

    def first0(z):
        c = lev0.g[z] * raw0[3, z]
        lev0.c[z] = c
        lev0.u[z + 1] = c

    lev0.each(first0, UNROLL)
    lev0.sweep(lev0.u, lev0.w, UNROLL)

    def remain0(z):
        u, total = lev0.total(lev0.w, z)
        r = raw0[3, z] - (lev0.d[z] * u - total)
        t0[z] = r[0:16, 0:128]

    lev0.each(remain0, UNROLL)
    b1 = down_0(t0[...])

    arrive(sent_p1)
    for f in range(4):
        def put1(z, start, x):
            raw1[f, z, start:start + 8, :] = x

        merge_1(f, lambda z: raw1[f, z, 8:16, :], p_rpk, p_rns, p_rnc, put1)
    lev1.faces(lambda z: raw1[0, z], lambda z: raw1[1, z], lambda z: raw1[2, z], lambda z: raw1[3, z], UNROLL)
    lev1.clear_ends()
    c1 = lev1.g[:, 8:16, :] * b1
    q1[...] = c1
    pack_1(c1, 0, b_pk, b_ns, b_nc)
    sent_b = send_1(b_pk, b_ns, b_nc, b_rpk, b_rns, b_rnc)

    edge_n = jnp.zeros((16, 128), F32)
    edge_s = jnp.zeros((16, 128), F32)
    for z in range(NZ):
        x = lev0.w[z + 1, 0:16, 0:128]
        o_ew[0, z] = x[0:4]
        o_ew[1, z] = x[12:16]
        edge_n = jnp.where(lane16 >= 4 * z, roll(x, 4 * z - 124, 1), edge_n)
        edge_s = jnp.where(lane16 >= 4 * z, roll(x, 4 * z, 1), edge_s)
    o_ns[0, 0] = edge_n
    o_ns[1, 0] = edge_s
    sent_o = send_edges(o_ew, o_ns, o_rew, o_rns, o_rd)

    m1 = restrict_1()

    def down_1(x):
        pair = jnp.concatenate([x[0:HZ], x[HZ:NZ]], axis=2).reshape(HZ * 8, 256)
        t2[...] = mm(pair, m1).reshape(HZ, 8, 128)
        return t2[:, pl.ds(0, 4, stride=2), :] + t2[:, pl.ds(1, 4, stride=2), :]

    own2 = [
        down_1(raw1[0, :, 8:16, :]),
        0.25 * down_1(raw1[1, :, 8:16, :]),
        0.25 * down_1(raw1[2, :, 8:16, :]),
        (down_1(raw1[3, :, 8:16, :]) > 0.0).astype(F32),
    ]

    def send_2(p, rp):
        return [copy(p, rp.at[3 - d], d, 0) for d in (1, -1, 2, -2, 3, -3)]

    for f in range(4):
        g_p[f * HZ:(f + 1) * HZ] = own2[f]
    sent_p2 = send_2(g_p, g_rp)

    arrive(sent_b)

    def put1c(z, start, x):
        lev1.c[z, start:start + 8, :] = x
        lev1.u[z + 1, start:start + 8, :] = x

    merge_1(0, lambda z: q1[z], b_rpk, b_rns, b_rnc, put1c)
    lev1.sweep(lev1.u, lev1.w, UNROLL)

    def remain1(z):
        q1[z] = lev1.remain(lev1.w, z)[8:16]

    lev1.each(remain1, UNROLL)
    b2 = down_1(q1[...])

    arrive(sent_p2)
    for f in range(4):
        for s in range(7):
            piece = g_p if s == 3 else g_rp.at[s]
            raw2[f, :, 4 * s:4 * s + 4, :] = piece[f * HZ:(f + 1) * HZ]
        raw2[f, :, 28:32, :] = jnp.zeros((HZ, 4, 128), F32)
    lev2.faces(lambda z: raw2[0, z], lambda z: raw2[1, z], lambda z: raw2[2, z], lambda z: raw2[3, z], UNROLL)
    f_p[...] = lev2.g[:, 12:16, :] * b2
    sent_c = send_2(f_p, f_rp)

    arrive(sent_hz)
    sent_hp = send_plane(window_row(h_z, 32), h_ev, 32)

    m2 = restrict_2()

    def down_2(x):
        t3[...] = mm(x.reshape(HZ * 32, 128), m2).reshape(HZ, 32, 128)
        return t3[:, pl.ds(0, 16, stride=2), :] + t3[:, pl.ds(1, 16, stride=2), :]

    raw3[0] = down_2(raw2[0])
    raw3[1] = 0.25 * down_2(raw2[1])
    raw3[2] = 0.25 * down_2(raw2[2])
    raw3[3] = (down_2(raw2[3]) > 0.0).astype(F32)
    lev3.faces(lambda z: raw3[0, z], lambda z: raw3[1, z], lambda z: raw3[2, z], lambda z: raw3[3, z], UNROLL)

    arrive(sent_c)
    for s in range(7):
        piece = f_p if s == 3 else f_rp.at[s]
        lev2.c[:, 4 * s:4 * s + 4, :] = piece[...]
    lev2.c[:, 28:32, :] = jnp.zeros((HZ, 4, 128), F32)
    lev2.start(UNROLL)
    lev2.sweep(lev2.u, lev2.w, UNROLL)

    def remain2(z):
        t4[z] = lev2.remain(lev2.w, z)

    lev2.each(remain2, UNROLL)

    lev3.c[...] = lev3.g[...] * down_2(t4[...])
    lev3.start(UNROLL)
    lev3.sweep(lev3.u, lev3.w, UNROLL)

    def remain3(z):
        t3[z, 0:16, :] = lev3.remain(lev3.w, z)

    lev3.each(remain3, UNROLL)
    m3 = restrict_3()
    t3[:, 0:16, :] = mm(t3[:, 0:16, :].reshape(HZ * 16, 128), m3).reshape(HZ, 16, 128)
    for z in range(HZ):
        k_blk[z:z + 1, :] = t3[z, 6:7, :] + t3[z, 7:8, :]
    k_blk[HZ:16, :] = jnp.zeros((16 - HZ, 128), F32)
    sent_kz = send_z(k_blk, k_z)

    arrive(sent_hp)
    sent_hs = send_sibling(h_ev, h_od)

    arrive(sent_hs)
    for f in range(3):
        for z in range(HZ):
            def put4(rows, x):
                raw4[f, z, rows, :] = x

            window_slab(h_ev, h_od, f * HZ + z, 32, put4)

    def sea_4(z):
        return (raw4[1, z] > 0.0).astype(F32)

    lev4.faces(lambda z: raw4[0, z], lambda z: raw4[1, z], lambda z: raw4[2, z], sea_4, UNROLL)

    arrive(sent_kz)
    sent_kp = send_plane(window_row(k_z, 16), k_ev, 16)
    arrive(sent_kp)
    arrive(send_sibling(k_ev, k_od))
    for z in range(HZ):
        def put4c(rows, x):
            lev4.c[z, rows, :] = x

        window_slab(k_ev, k_od, z, 16, put4c)
    for z in range(HZ):
        lev4.c[z] = lev4.g[z] * lev4.c[z]
    lev4.start(UNROLL)

    def two(step, carry):
        lev4.sweep(lev4.u, lev4.w, UNROLL)
        lev4.sweep(lev4.w, lev4.u, UNROLL)
        return carry

    lax.fori_loop(0, 9, two, 0)
    lev4.sweep(lev4.u, lev4.w, UNROLL)

    up = mm(lev4.w[1:HZ + 1, 13:21, :].reshape(HZ * 8, 128), prolong_3()).reshape(HZ, 8, 128)
    for start in range(2):
        t3[:, pl.ds(start, 8, stride=2), :] = up

    def add3(z):
        lev3.w[z + 1] = lev3.w[z + 1] + t3[z, 0:16, :]

    lev3.each(add3, UNROLL)
    lev3.wrap(lev3.w)
    lev3.sweep(lev3.w, lev3.u, UNROLL)
    lev3.sweep(lev3.u, lev3.w, UNROLL)

    up = mm(lev3.w[1:HZ + 1].reshape(HZ * 16, 128), prolong_2()).reshape(HZ, 16, 128)
    for start in range(2):
        t3[:, pl.ds(start, 16, stride=2), :] = up

    def add2(z):
        lev2.w[z + 1] = lev2.w[z + 1] + t3[z]

    lev2.each(add2, UNROLL)
    lev2.wrap(lev2.w)
    lev2.sweep(lev2.w, lev2.u, UNROLL)
    lev2.sweep(lev2.u, lev2.w, UNROLL)

    t3[:, 0:16, :] = lev2.w[1:HZ + 1, 8:24, :]
    up = mm(t3[:, 0:16, :].reshape(HZ * 16, 128), prolong_1()).reshape(HZ, 16, 256)
    for start in range(2):
        t1[0:HZ, :, :] = up[:, :, 0:128]
        t1[HZ:NZ, :, :] = up[:, :, 128:256]
    for z in range(NZ):
        for start in range(2):
            q = pl.ds(start, 12, stride=2)
            raw1[0, z, q, :] = t1[z, 0:12, :]

    def add1(z):
        lev1.w[z + 1] = lev1.w[z + 1] + raw1[0, z]

    lev1.each(add1, UNROLL)
    lev1.sweep(lev1.w, lev1.u, UNROLL)
    lev1.sweep(lev1.u, lev1.w, UNROLL)

    arrive(sent_o)

    def put_rows0(z, x):
        lev0.w[z + 1, 16:24, 0:128] = x

    def put_side0(z, x):
        lev0.w[z + 1, :, 128:256] = x

    def rows0(z):
        return jnp.concatenate([o_rew[0, z], o_rew[1, z]], axis=0)

    merge_edges(0, rows0, o_rns, o_rd, put_rows0, put_side0)
    for z in range(NZ):
        t1[z, 0:8, :] = lev1.w[z + 1, 8:16, :]
        t1[z, 8:10, :] = lev1.w[z + 1, 16:18, :]
        t1[z, 10:12, :] = lev1.w[z + 1, 6:8, :]
        t1[z, 12:16, :] = jnp.zeros((4, 128), F32)
    up = mm(t1[...].reshape(NZ * 16, 128), prolong_0()).reshape(NZ, 16, 256)
    for z in range(NZ):
        for half in range(2):
            part = up[z, 0:12, 128 * half:128 * half + 128]
            for start in range(2):
                raw1[half, z, pl.ds(start, 12, stride=2), :] = part

    def add0(z):
        for half in range(2):
            lanes = slice(128 * half, 128 * half + 128)
            lev0.w[z + 1, :, lanes] = lev0.w[z + 1, :, lanes] + raw1[half, z]

    lev0.each(add0, UNROLL)
    lev0.sweep(lev0.w, lev0.u, UNROLL)
    lev0.sweep(lev0.u, lev0.w, UNROLL)
    sol[...] = lev0.w[1:NZ + 1, 0:16, 0:128]
    out_sol = pltpu.make_async_copy(sol, sol_out, out_sem.at[0])
    out_sol.start()

    def last0(z):
        u, total = lev0.total(lev0.w, z)
        r = raw0[3, z] - (lev0.d[z] * u - total)
        resid[z] = r[0:16, 0:128]

    lev0.each(last0, UNROLL)
    out_resid = pltpu.make_async_copy(resid, resid_out, out_sem.at[1])
    out_resid.start()

    for made in pending:
        made.wait_send()
    out_sol.wait()
    out_resid.wait()


def deliver(sol_in, resid_in, sol_out, resid_out, sem):
    copies = [
        pltpu.make_async_copy(sol_in, sol_out, sem.at[0]),
        pltpu.make_async_copy(resid_in, resid_out, sem.at[1]),
    ]
    for made in copies:
        made.start()
    for made in copies:
        made.wait()


def level_scratch(slabs, rows, lanes):
    def vmem(count):
        return pltpu.VMEM((count, rows, lanes), F32)

    return [vmem(slabs), vmem(slabs), vmem(slabs + 1), vmem(slabs), vmem(slabs), vmem(slabs), vmem(slabs + 2), vmem(slabs + 2)]


def shards(source, kappa_sq, lon_diff, lat_diff, sea_mask):
    def vmem(*shape):
        return pltpu.VMEM(shape, F32)

    scratch = [
        vmem(NZ, 16, 128), vmem(NZ, 16, 128), pltpu.SemaphoreType.DMA((2,)),
        vmem(NZ, 16, 128), vmem(NZ, 16, 128), vmem(NZ, 16, 128), vmem(NZ, 16, 128),
        pltpu.VMEM((NZ, 16, 128), jnp.int32), pltpu.SemaphoreType.DMA((5,)),
        vmem(4, NZ, 24, 256), vmem(8, 128), level_scratch(NZ, 24, 256),
        vmem(4, NZ, 24, 128), level_scratch(NZ, 24, 128),
        vmem(4, HZ, 32, 128), level_scratch(HZ, 32, 128),
        vmem(4, HZ, 16, 128), level_scratch(HZ, 16, 128),
        vmem(3, HZ, 32, 128), level_scratch(HZ, 32, 128),
        vmem(NZ, 16, 128), vmem(NZ, 16, 128), vmem(HZ, 8, 128), vmem(HZ, 32, 128), vmem(HZ, 32, 128), vmem(NZ, 8, 128),
        vmem(2, 4 * NZ + HZ, 2, 128), vmem(2, 4, 16, 128), vmem(2, 4 * NZ + HZ, 2, 128), vmem(2, 4, 16, 128), vmem(4, 4, 8, 128),
        vmem(HZ, 8, 128), vmem(2, 5, 8, 128), vmem(2, 2, 5, 4, 128),
        vmem(2, HZ, 8, 128), vmem(2, 5, 8, 128), vmem(2, 2, 5, 4, 128),
        vmem(HZ, 4, 128), vmem(7, HZ, 4, 128),
        vmem(16, 128), vmem(7, 16, 128), vmem(16 * 16, 128), vmem(16 * 16, 128),
        vmem(4 * HZ, 8, 128), vmem(2, 20, 8, 128), vmem(2, 2, 20, 4, 128),
        vmem(2, 4 * HZ, 8, 128), vmem(2, 20, 8, 128), vmem(2, 2, 20, 4, 128),
        vmem(4 * HZ, 4, 128), vmem(7, 4 * HZ, 4, 128),
        vmem(32, 128), vmem(7, 32, 128), vmem(16 * 32, 128), vmem(16 * 32, 128),
        vmem(2, NZ, 4, 128), vmem(2, 1, 16, 128), vmem(2, NZ, 4, 128), vmem(2, 1, 16, 128), vmem(4, 1, 8, 128),
        pltpu.SemaphoreType.DMA((96,)), pltpu.SemaphoreType.DMA((96,)),
    ]
    shape = jax.ShapeDtypeStruct(source.shape, F32)
    anywhere = pl.BlockSpec(memory_space=pl.ANY)
    found = pl.pallas_call(
        body,
        out_shape=(shape, shape),
        in_specs=[anywhere] * 5,
        out_specs=[anywhere] * 2,
        scratch_shapes=scratch,
        compiler_params=pltpu.CompilerParams(
            collective_id=0, has_side_effects=True, vmem_limit_bytes=62 * 1024 * 1024
        ),
    )(source, kappa_sq, lon_diff, lat_diff, sea_mask)
    return pl.pallas_call(
        deliver,
        out_shape=(shape, shape),
        in_specs=[anywhere] * 2,
        out_specs=[anywhere] * 2,
        scratch_shapes=[pltpu.SemaphoreType.DMA((2,))],
        compiler_params=pltpu.CompilerParams(vmem_limit_bytes=62 * 1024 * 1024),
    )(*found)


def solution(mesh):
    spec = P(None, "tx", "ty")
    return jax.shard_map(
        shards, mesh=mesh, in_specs=(spec,) * 5, out_specs=(spec, spec), check_vma=False
    )
```

```python
import jax
import jax.numpy as jnp
from jax import lax
from jax.experimental import pallas as pl
from jax.experimental.pallas import tpu as pltpu
from jax.sharding import PartitionSpec as P

NZ = 20
HZ = 10
NTX = 32
NTY = 16
OMEGA = 0.8
UNROLL = 20
MESH = pl.DeviceIdType.MESH
F32 = jnp.float32

DIAGONALS = ((1, 1), (-1, 1), (1, -1), (-1, -1))


def iota(shape, dim):
    return lax.broadcasted_iota(jnp.int32, shape, dim)


def mm(x, m):
    high = x.astype(jnp.bfloat16)
    low = (x - high.astype(F32)).astype(jnp.bfloat16)
    m = m.astype(jnp.bfloat16)
    return lax.dot_general(
        jnp.concatenate([high, low], axis=1), jnp.concatenate([m, m], axis=0),
        (((1,), (0,)), ((), ())), preferred_element_type=F32,
    )


def roll(x, shift, axis):
    shift = shift % x.shape[axis]
    return x if shift == 0 else pltpu.roll(x, shift, axis)


def one_hot(shape, hit, value=1.0):
    row, col = iota(shape, 0), iota(shape, 1)
    return jnp.where(hit(row, col), F32(value), F32(0.0))


def restrict_0():
    return one_hot((128, 128), lambda n, m: m == 32 + (n >> 1), 0.25)


def restrict_1():
    return one_hot((256, 128), lambda n, m: m == n >> 1, 0.25)


def restrict_2():
    return one_hot((128, 128), lambda n, m: m == (n & 64) + 8 + ((n & 63) >> 1), 0.25)


def restrict_3():
    def hit(n, m):
        q = n & 63
        return (m == (n & 64) + 16 + (q >> 1)) & (q >= 16) & (q < 32)

    return one_hot((128, 128), hit, 0.25)


def restrict_all():
    return one_hot((256, 128), lambda n, m: m == ((n & 128) >> 1) + 24 + ((n & 127) >> 4), 1.0 / 256)


def prolong_3():
    return one_hot((128, 128), lambda m, n: m == (n & 64) + 16 + ((n & 63) >> 1))


def prolong_2():
    return one_hot((128, 128), lambda m, n: m == (n & 64) + 8 + ((n & 63) >> 1))


def prolong_1():
    return one_hot((128, 256), lambda m, n: m == n >> 1)


def prolong_0():
    def hit(m, n):
        rel = jnp.where(n >= 192, n - 256, n)
        return (m == 32 + (rel >> 1)) & (rel < 132) & (rel >= -4)

    return one_hot((128, 256), hit)


class Level:
    def __init__(self, slabs, folded, refs):
        self.slabs = slabs
        self.folded = folded
        self.e, self.n, self.v, self.g, self.d, self.c, self.u, self.w = refs

    def each(self, body, unroll):
        def step(z, carry):
            body(z)
            return carry

        lax.fori_loop(0, self.slabs, step, 0, unroll=min(unroll, self.slabs))

    def wrap(self, ref, rows=slice(None)):
        if self.folded:
            ref[0, rows] = roll(ref[self.slabs, rows], 64, 1)
            ref[self.slabs + 1, rows] = roll(ref[1, rows], 64, 1)

    def clear_ends(self):
        if not self.folded:
            for ref in (self.u, self.w):
                ref[0] = jnp.zeros_like(ref[0])
                ref[self.slabs + 1] = jnp.zeros_like(ref[0])

    def faces(self, kap, lond, latd, sea, unroll):
        top = self.slabs - 1

        def vertical(z):
            here = sea(z)
            self.v[z + 1] = here * sea(z + 1)

        lax.fori_loop(0, top, lambda z, c: (vertical(z), c)[1], 0, unroll=min(unroll, top))
        if self.folded:
            low = iota(self.v.shape[1:], 1) < 64
            self.v[self.slabs] = jnp.where(low, sea(top) * roll(sea(0), 64, 1), 0.0)
            self.v[0] = roll(self.v[self.slabs], 64, 1)
        else:
            self.v[0] = jnp.zeros_like(self.v[0])
            self.v[self.slabs] = jnp.zeros_like(self.v[0])

        def horizontal(z):
            s = sea(z)
            lw = s * lond(z)
            tw = s * latd(z)
            east = 0.5 * (lw * roll(s, -1, 0) + s * roll(lw, -1, 0))
            north = 0.5 * (tw * roll(s, -1, 1) + s * roll(tw, -1, 1))
            west = roll(east, 1, 0)
            south = roll(north, 1, 1)
            diag = s * kap(z) + (west + east + south + north + self.v[z] + self.v[z + 1]) + (1.0 - s)
            self.e[z] = east
            self.n[z] = north
            self.d[z] = diag
            self.g[z] = OMEGA / diag

        self.each(horizontal, unroll)

    def stencil(self, src, unroll, use, rows=slice(None)):
        def step(z, carry):
            below, u, face_below = carry
            above = src[z + 2, rows]
            face_above = self.v[z + 1, rows]
            e = self.e[z, rows]
            n = self.n[z, rows]
            use(z, u, (
                roll(e * u, 1, 0)
                + e * roll(u, -1, 0)
                + roll(n * u, 1, 1)
                + n * roll(u, -1, 1)
                + face_below * below
                + face_above * above
            ))
            return u, above, face_above

        lax.fori_loop(0, self.slabs, step, (src[0, rows], src[1, rows], self.v[0, rows]), unroll=min(unroll, self.slabs))

    def sweep(self, src, dst, unroll, rows=slice(None)):
        def use(z, u, total):
            dst[z + 1, rows] = (1.0 - OMEGA) * u + self.c[z, rows] + self.g[z, rows] * total

        self.stencil(src, unroll, use, rows)
        self.wrap(dst, rows)

    def start(self, unroll):
        def body(z):
            self.u[z + 1] = self.c[z]

        self.each(body, unroll)
        self.wrap(self.u)

    def remain(self, src, unroll, put):
        self.stencil(src, unroll, lambda z, u, total: put(z, self.d[z] * (1.25 * self.c[z] - u) + total))


def pack_edge(slabs, width, base, count):
    lane = iota(slabs[0].shape, 1)
    out = roll(slabs[0], -base, 1)
    for i in range(1, count):
        out = jnp.where(lane >= width * i, roll(slabs[i], width * i - base, 1), out)
    return out


def body(
    source_in, kappa_in, lon_in, lat_in, mask_in,
    sol, resid,
    source, kappa, lon_diff, lat_diff, mask, in_sem,
    raw0, src0, l0, raw1, l1, raw2, l2, raw3, l3, raw4, l4, t0, t1, t2, t3, t4, q1,
    a_ew, a_ns, a_rew, a_rns, a_rd,
    b_pk, b_ns, b_nc, b_rpk, b_rns, b_rnc,
    f_p, f_rp,
    k_blk, k_z, k_ev,
    p_pk, p_ns, p_nc, p_rpk, p_rns, p_rnc, q_p, q_rp, g_p, g_rp, h_blk, h_z, h_ev, h_od,
    o_ew, o_ns, o_rew, o_rns, o_rd,
    send_sem, recv_sem,
):
    mx, my = lax.axis_index("tx"), lax.axis_index("ty")
    odd = lax.rem(mx, 2) == 1
    counter = [0]
    pending = []
    places = {}

    def shifted(axis, here, shift, count):
        shift = shift % count
        if (axis, shift) not in places:
            there = here + shift
            places[axis, shift] = jnp.where(there >= count, there - count, there) if shift else here
        return places[axis, shift]

    def device(dx, dy):
        return (shifted(0, mx, dx, NTX), shifted(1, my, dy, NTY))

    def copy(src, dst, dx, dy):
        i = counter[0]
        counter[0] += 1
        made = pltpu.make_async_remote_copy(
            src_ref=src, dst_ref=dst, send_sem=send_sem.at[i], recv_sem=recv_sem.at[i],
            device_id=device(dx, dy),
            device_id_type=MESH,
        )
        made.start()
        pending.append(made)
        return made

    def arrive(copies):
        for made in copies:
            made.wait_recv()

    lev0 = Level(NZ, False, l0)
    lev1 = Level(NZ, False, l1)
    lev2 = Level(HZ, True, l2)
    lev3 = Level(HZ, True, l3)
    lev4 = Level(HZ, True, l4)

    fetched = [
        pltpu.make_async_copy(src, dst, in_sem.at[i])
        for i, (src, dst) in enumerate((
            (mask_in, mask), (lon_in, lon_diff), (lat_in, lat_diff), (kappa_in, kappa), (source_in, source)
        ))
    ]
    for made in fetched:
        made.start()

    peers = [(2 * k, 0) for k in range(1, 16)] + [(1, 0), (-1, 0), (3, 0), (-3, 0)]
    peers += [(0, d) for d in (1, 2, 3, -1, -2, -3)] + list(DIAGONALS)
    barrier = pltpu.get_barrier_semaphore()
    for dx, dy in peers:
        pl.semaphore_signal(
            barrier, inc=1,
            device_id=device(dx, dy),
            device_id_type=MESH,
        )

    lane16 = iota((16, 128), 1)
    place = ((1, 0), (0, 0), (0, 60), (1, 60))
    edge_n = [jnp.zeros((16, 128), F32)] * 4
    edge_s = [jnp.zeros((16, 128), F32)] * 4
    own0 = (
        lambda z: kappa[z],
        lambda z: mask[z].astype(F32) * lon_diff[z],
        lambda z: mask[z].astype(F32) * lat_diff[z],
        lambda z: source[z],
    )
    for f, needed in ((1, (0, 1)), (2, (2,)), (0, (3,)), (3, (4,))):
        for i in needed:
            fetched[i].wait()
        for z in range(NZ):
            x = own0[f](z)
            raw0[f, z, 0:16, 0:128] = x
            a_ew[0, f * NZ + z] = x[0:2]
            a_ew[1, f * NZ + z] = x[14:16]
            if f == 1:
                a_ew[0, 4 * NZ + z // 2, z % 2:z % 2 + 1] = x[2:3]
                a_ew[1, 4 * NZ + z // 2, z % 2:z % 2 + 1] = x[13:14]
            start = place[f][1] + 3 * z
            edge_n[f] = jnp.where(lane16 >= start, roll(x, start - 125, 1), edge_n[f])
            edge_s[f] = jnp.where(lane16 >= start, roll(x, start, 1), edge_s[f])
    for pair, (f, g) in enumerate(((1, 2), (0, 3))):
        a_ns[0, pair] = jnp.where(lane16 < 60, edge_n[f], edge_n[g])
        a_ns[1, pair] = jnp.where(lane16 < 60, edge_s[f], edge_s[g])

    pl.semaphore_wait(barrier, len(peers))

    def send_edges(ew, ns, rew, rns, rd):
        made = [copy(ns.at[0, :, 8:16, :], rd.at[0], 1, 1)]
        made.append(copy(ns.at[0, :, 0:8, :], rd.at[1], -1, 1))
        made.append(copy(ns.at[1, :, 8:16, :], rd.at[2], 1, -1))
        made.append(copy(ns.at[1, :, 0:8, :], rd.at[3], -1, -1))
        made += [copy(ew.at[0], rew.at[0], -1, 0), copy(ew.at[1], rew.at[1], 1, 0)]
        made += [copy(ns.at[0], rns.at[0], 0, 1), copy(ns.at[1], rns.at[1], 0, -1)]
        return made

    has_s, has_n = my > 0, my < NTY - 1

    def merge_edges(f, base, rns, rd, put_rows, put_side):
        sub = iota((8, 128), 0)
        south = jnp.concatenate([rns[0, f], jnp.where(sub < 4, rd[1, f], rd[0, f])], axis=0)
        north = jnp.concatenate([rns[1, f], jnp.where(sub < 4, rd[3, f], rd[2, f])], axis=0)
        lane = iota((24, 128), 1)
        south = jnp.where(has_s, south, 0.0)
        north = jnp.where(has_n, north, 0.0)
        for z in range(NZ):
            put_rows(z)
            start = base + 3 * z
            side = jnp.where(lane < 3, roll(north, -start, 1), roll(south, 125 - start, 1))
            put_side(z, jnp.where((lane < 3) | (lane >= 125), side, 0.0))

    sent_a = send_edges(a_ew, a_ns, a_rew, a_rns, a_rd)
    for f in range(4):
        for z in range(NZ):
            raw0[f, z, 16:24, 0:128] = jnp.zeros((8, 128), F32)

    m0 = restrict_0()

    def down_0(x):
        t1[...] = mm(x.reshape(NZ * 16, 128), m0).reshape(NZ, 16, 128)
        return t1[:, pl.ds(0, 8, stride=2), :] + t1[:, pl.ds(1, 8, stride=2), :]

    def pack_1(x, f, pk, ns, nc):
        lane = iota((8, 128), 1)
        for k in range(HZ):
            pk[f * HZ + k] = jnp.where(lane < 64, roll(x[k], -32, 1), roll(x[k + HZ], 32, 1))
        for k in range(5):
            group = [x[k + 5 * j] for j in range(4)]
            for side, base in ((0, 64), (1, 32)):
                edge = pack_edge(group, 32, base, 4)
                ns[side, f * 5 + k] = edge
                nc[side, 0, f * 5 + k] = edge[0:4]
                nc[side, 1, f * 5 + k] = edge[4:8]

    def send_1(pk, ns, nc, rpk, rns, rnc):
        made = [copy(nc.at[0, 1], rnc.at[0, 1], 1, 1)]
        made.append(copy(nc.at[0, 0], rnc.at[0, 0], -1, 1))
        made.append(copy(nc.at[1, 1], rnc.at[1, 1], 1, -1))
        made.append(copy(nc.at[1, 0], rnc.at[1, 0], -1, -1))
        made += [copy(pk, rpk.at[0], -1, 0), copy(pk, rpk.at[1], 1, 0)]
        made += [copy(ns.at[0], rns.at[0], 0, 1), copy(ns.at[1], rns.at[1], 0, -1)]
        return made

    def merge_1(f, own, rpk, rns, rnc, put):
        lane = iota((8, 128), 1)
        blank = jnp.zeros((4, 128), F32)

        def edge(side, i, at):
            if i == 0:
                return rns[side, at]
            if i == 1:
                return jnp.concatenate([rnc[side, 0, at], blank], axis=0)
            return jnp.concatenate([blank, rnc[side, 1, at]], axis=0)

        for z in range(NZ):
            k, shift = (z, 32) if z < HZ else (z - HZ, -32)
            middle = (own(z), roll(rpk[0, f * HZ + k], shift, 1), roll(rpk[1, f * HZ + k], shift, 1))
            for i, start in ((0, 8), (1, 16), (2, 0)):
                south = jnp.where(has_s, roll(edge(0, i, f * 5 + z % 5), -32 * (z // 5), 1), 0.0)
                north = jnp.where(has_n, roll(edge(1, i, f * 5 + z % 5), 96 - 32 * (z // 5), 1), 0.0)
                put(z, start, jnp.where(lane < 32, south, jnp.where(lane < 96, middle[i], north)))

    own1 = [
        down_0(kappa[...]),
        0.25 * down_0(lon_diff[...]),
        0.25 * down_0(lat_diff[...]),
        (down_0(mask[...].astype(F32)) > 0.0).astype(F32),
    ]

    m1 = restrict_1()

    def down_1(x):
        pair = jnp.concatenate([x[0:HZ], x[HZ:NZ]], axis=2).reshape(HZ * 8, 256)
        t2[...] = mm(pair, m1).reshape(HZ, 8, 128)
        return t2[:, pl.ds(0, 4, stride=2), :] + t2[:, pl.ds(1, 4, stride=2), :]

    own2 = [
        down_1(own1[0]),
        0.25 * down_1(own1[1]),
        0.25 * down_1(own1[2]),
        (down_1(own1[3]) > 0.0).astype(F32),
    ]
    for f in range(4):
        g_p[f * HZ:(f + 1) * HZ] = own2[f]
        for k in range(5):
            q_p[f * 5 + k] = own2[f][k] + roll(own2[f][k + 5], 32, 1)
    sent_q = [copy(q_p, q_rp.at[0], 0, 1), copy(q_p, q_rp.at[1], 0, -1)]

    for f, x in enumerate((own1[0], own1[3] * own1[1], own1[3] * own1[2])):
        pack_1(x, f, p_pk, p_ns, p_nc)
        raw1[f, :, 8:16, :] = x
    sent_p1 = send_1(p_pk, p_ns, p_nc, p_rpk, p_rns, p_rnc)

    def send_z(blk, slots):
        slots[3] = blk[...]
        return [copy(blk, slots.at[3 - d], 0, d) for d in (3, -3, 2, -2, 1, -1)]

    def window_row(slots, count):
        row = jnp.zeros((count, 128), F32)
        for s in range(7):
            inside = (my + (s - 3) >= 0) & (my + (s - 3) < NTY)
            row = row + jnp.where(inside, roll(slots[s], 8 * (s - 3), 1), 0.0)
        return row

    def folded_window_row(slots):
        part = iota((8, 128), 1) & 63
        out = [jnp.zeros((8, 128), F32)] * 3
        for s in range(7):
            inside = (my + (s - 3) >= 0) & (my + (s - 3) < NTY)
            block = jnp.where(inside, slots[s], 0.0)
            for i in range(3):
                pick = (part >= 24 + 8 * i) & (part < 32 + 8 * i)
                out[i] = out[i] + roll(jnp.where(pick, block, 0.0), 8 * (s - 3 - i), 1)
        return jnp.concatenate(out, axis=0)

    def send_plane(row, ev, count):
        own = pl.ds(8 * count, count)
        ev[own, :] = row
        return [
            copy(ev.at[own], ev.at[pl.ds(((8 - k) % 16) * count, count)], 2 * k, 0)
            for k in (10, 6, 9, 7, 11, 5, 2, 14, 8, 3, 13, 1, 15, 4, 12)
        ]

    def send_sibling(ev, od):
        i = counter[0]
        counter[0] += 1
        made = pltpu.make_async_remote_copy(
            src_ref=ev, dst_ref=od, send_sem=send_sem.at[i], recv_sem=recv_sem.at[i],
            device_id=(mx + 1 - 2 * lax.rem(mx, 2), my), device_id_type=MESH,
        )
        made.start()
        pending.append(made)
        return [made]

    def window_slab(ev, od, index, count, put):
        put(pl.ds(0, 16, stride=2), ev[pl.ds(index, 16, stride=count), :])
        other = od[pl.ds(index, 16, stride=count), :]
        put(pl.ds(1, 16, stride=2), jnp.where(odd, roll(other, -1, 0), other))

    arrive(sent_a)
    for f in range(4):
        def put_rows(z):
            raw0[f, z, 16:18, 0:128] = a_rew[0, f * NZ + z]
            raw0[f, z, 22:24, 0:128] = a_rew[1, f * NZ + z]
            if f == 1:
                pick = slice(z % 2, z % 2 + 1)
                raw0[f, z, 18:19, 0:128] = a_rew[0, 4 * NZ + z // 2, pick]
                raw0[f, z, 21:22, 0:128] = a_rew[1, 4 * NZ + z // 2, pick]

        def put_side(z, x):
            raw0[f, z, :, 128:256] = x

        merge_edges(place[f][0], place[f][1], a_rns, a_rd, put_rows, put_side)

    def send_2(p, rp):
        return [copy(p, rp.at[3 - d], d, 0) for d in (3, -3, 2, -2, 1, -1)]

    arrive(sent_q)
    part = iota((4, 128), 1) & 63
    for f in range(4):
        for k in range(HZ):
            south = roll(q_rp[0, f * 5 + k % 5], -32 if k < 5 else -64, 1)
            north = roll(q_rp[1, f * 5 + k % 5], 32 if k < 5 else 0, 1)
            south = jnp.where(has_s, south, 0.0)
            north = jnp.where(has_n, north, 0.0)
            g_p[f * HZ + k] = jnp.where(part < 16, south, jnp.where(part < 48, g_p[f * HZ + k], north))
    sent_p2 = send_2(g_p, g_rp)

    def sea0(z):
        return (raw0[1, z] > 0.0).astype(F32)

    lev0.faces(lambda z: raw0[0, z], lambda z: raw0[1, z], lambda z: raw0[2, z], sea0, UNROLL)
    lev0.clear_ends()


    def first0(z):
        c = lev0.g[z] * raw0[3, z]
        lev0.c[z] = c
        lev0.u[z + 1] = c

    lev0.each(first0, UNROLL)
    lev0.sweep(lev0.u, lev0.w, UNROLL)

    def remain0(z, u, total):
        r = raw0[3, z] - (lev0.d[z] * u - total)
        t0[z] = r[0:16, 0:128]

    lev0.stencil(lev0.w, UNROLL, remain0)
    b1 = down_0(t0[...])

    arrive(sent_p1)
    for f in range(3):
        def put1(z, start, x):
            raw1[f, z, start:start + 8, :] = x

        merge_1(f, lambda z: raw1[f, z, 8:16, :], p_rpk, p_rns, p_rnc, put1)

    def sea_1(z):
        return (raw1[1, z] > 0.0).astype(F32)

    lev1.faces(lambda z: raw1[0, z], lambda z: raw1[1, z], lambda z: raw1[2, z], sea_1, UNROLL)
    lev1.clear_ends()
    c1 = lev1.g[:, 8:16, :] * b1
    q1[...] = c1
    pack_1(c1, 0, b_pk, b_ns, b_nc)
    sent_b = send_1(b_pk, b_ns, b_nc, b_rpk, b_rns, b_rnc)

    edge_n = jnp.zeros((16, 128), F32)
    edge_s = jnp.zeros((16, 128), F32)
    for z in range(NZ):
        x = lev0.w[z + 1, 0:16, 0:128]
        o_ew[0, z] = x[0:4]
        o_ew[1, z] = x[12:16]
        edge_n = jnp.where(lane16 >= 3 * z, roll(x, 3 * z - 125, 1), edge_n)
        edge_s = jnp.where(lane16 >= 3 * z, roll(x, 3 * z, 1), edge_s)
    o_ns[0, 0] = edge_n
    o_ns[1, 0] = edge_s

    mall = restrict_all()

    def down_all(x):
        pair = jnp.concatenate([x[0:HZ], x[HZ:NZ]], axis=2).reshape(HZ * 16, 256)
        return jnp.sum(mm(pair, mall).reshape(HZ, 16, 128), axis=1)

    sea4 = (down_all(mask[...].astype(F32)) > 0.0).astype(F32)
    h_blk[0:10, :] = down_all(kappa[...])
    h_blk[10:20, :] = sea4 * (down_all(lon_diff[...]) * (1.0 / 256))
    h_blk[20:30, :] = sea4 * (down_all(lat_diff[...]) * (1.0 / 256))
    h_blk[30:32, :] = jnp.zeros((2, 128), F32)

    arrive(sent_p2)
    for f in range(4):
        for s in range(7):
            piece = g_p if s == 3 else g_rp.at[s]
            raw2[f, :, 4 * s:4 * s + 4, :] = piece[f * HZ:(f + 1) * HZ]
        raw2[f, :, 28:32, :] = jnp.zeros((HZ, 4, 128), F32)
    lev2.faces(lambda z: raw2[0, z], lambda z: raw2[1, z], lambda z: raw2[2, z], lambda z: raw2[3, z], UNROLL)

    m2 = restrict_2()

    def down_2(x):
        t3[...] = mm(x.reshape(HZ * 32, 128), m2).reshape(HZ, 32, 128)
        return t3[:, pl.ds(0, 16, stride=2), :] + t3[:, pl.ds(1, 16, stride=2), :]

    raw3[0] = down_2(raw2[0])
    raw3[1] = 0.25 * down_2(raw2[1])
    raw3[2] = 0.25 * down_2(raw2[2])
    raw3[3] = (down_2(raw2[3]) > 0.0).astype(F32)
    lev3.faces(lambda z: raw3[0, z], lambda z: raw3[1, z], lambda z: raw3[2, z], lambda z: raw3[3, z], UNROLL)

    arrive(sent_b)
    sent_hz = send_z(h_blk, h_z)

    def put1c(z, start, x):
        lev1.c[z, start:start + 8, :] = x
        lev1.u[z + 1, start:start + 8, :] = x

    merge_1(0, lambda z: q1[z], b_rpk, b_rns, b_rnc, put1c)
    lev1.sweep(lev1.u, lev1.w, UNROLL)

    def remain1(z, r):
        q1[z] = r[8:16]

    lev1.remain(lev1.w, UNROLL, remain1)
    b2 = down_1(q1[...])

    f_p[...] = lev2.g[:, 12:16, :] * b2
    sent_c = send_2(f_p, f_rp)

    arrive(sent_hz)
    row_h = window_row(h_z, 32)
    arrive(sent_c)
    sent_hp = send_plane(row_h, h_ev, 32)
    sent_o = send_edges(o_ew, o_ns, o_rew, o_rns, o_rd)
    for s in range(7):
        piece = f_p if s == 3 else f_rp.at[s]
        lev2.c[:, 4 * s:4 * s + 4, :] = piece[...]
    lev2.c[:, 28:32, :] = jnp.zeros((HZ, 4, 128), F32)
    lev2.start(UNROLL)
    lev2.sweep(lev2.u, lev2.w, UNROLL)

    def remain2(z, r):
        t4[z] = r

    lev2.remain(lev2.w, UNROLL, remain2)

    lev3.c[...] = lev3.g[...] * down_2(t4[...])
    lev3.start(UNROLL)
    lev3.sweep(lev3.u, lev3.w, UNROLL)

    def remain3(z, r):
        t3[z, 0:16, :] = r

    lev3.remain(lev3.w, UNROLL, remain3)
    m3 = restrict_3()
    t3[:, 0:16, :] = mm(t3[:, 0:16, :].reshape(HZ * 16, 128), m3).reshape(HZ, 16, 128)
    for z in range(8):
        row = t3[z, 6:7, :] + t3[z, 7:8, :] + roll(t3[z, 8:9, :] + t3[z, 9:10, :], 8, 1)
        if z < 4:
            at = 6 if z < 2 else 8
            last = t3[8 + z % 2, at:at + 1, :] + t3[8 + z % 2, at + 1:at + 2, :]
            row = row + roll(last, 16, 1)
        k_blk[z:z + 1, :] = row
    sent_kz = send_z(k_blk, k_z)

    arrive(sent_hp)
    sent_hs = send_sibling(h_ev, h_od)

    arrive(sent_kz)
    sent_kp = send_plane(folded_window_row(k_z), k_ev, 24)

    arrive(sent_hs)
    for f in range(3):
        for z in range(HZ):
            def put4(rows, x):
                raw4[f, z, rows, :] = x

            window_slab(h_ev, h_od, f * HZ + z, 32, put4)

    def sea_4(z):
        return (raw4[1, z] > 0.0).astype(F32)

    lev4.faces(lambda z: raw4[0, z], lambda z: raw4[1, z], lambda z: raw4[2, z], sea_4, UNROLL)

    arrive(sent_kp)
    for z in range(HZ):
        for i in range(2):
            at = 8 * i + z if z < 8 else 16 + 2 * i + z - 8
            lev4.c[z, pl.ds(i, 16, stride=2), :] = k_ev[pl.ds(at, 16, stride=24), :]
    for z in range(HZ):
        lev4.c[z] = lev4.g[z] * lev4.c[z]
    lev4.start(UNROLL)

    def two(step, carry):
        lev4.sweep(lev4.u, lev4.w, UNROLL)
        lev4.sweep(lev4.w, lev4.u, UNROLL)
        return carry

    lax.fori_loop(0, 7, two, 0)
    middle = slice(8, 24)
    for src, dst in ((lev4.u, lev4.w), (lev4.w, lev4.u)) * 2 + ((lev4.u, lev4.w),):
        lev4.sweep(src, dst, UNROLL, middle)

    up = mm(lev4.w[1:HZ + 1, 13:21, :].reshape(HZ * 8, 128), prolong_3()).reshape(HZ, 8, 128)
    for start in range(2):
        t3[:, pl.ds(start, 8, stride=2), :] = up

    def add3(z):
        lev3.w[z + 1] = lev3.w[z + 1] + t3[z, 0:16, :]

    lev3.each(add3, UNROLL)
    lev3.wrap(lev3.w)
    lev3.sweep(lev3.w, lev3.u, UNROLL)
    lev3.sweep(lev3.u, lev3.w, UNROLL)

    up = mm(lev3.w[1:HZ + 1].reshape(HZ * 16, 128), prolong_2()).reshape(HZ, 16, 128)
    for start in range(2):
        t3[:, pl.ds(start, 16, stride=2), :] = up

    def add2(z):
        lev2.w[z + 1] = lev2.w[z + 1] + t3[z]

    lev2.each(add2, UNROLL)
    lev2.wrap(lev2.w)
    lev2.sweep(lev2.w, lev2.u, UNROLL)
    lev2.sweep(lev2.u, lev2.w, UNROLL)

    t3[:, 0:16, :] = lev2.w[1:HZ + 1, 8:24, :]
    up = mm(t3[:, 0:16, :].reshape(HZ * 16, 128), prolong_1()).reshape(HZ, 16, 256)
    for start in range(2):
        t1[0:HZ, :, :] = up[:, :, 0:128]
        t1[HZ:NZ, :, :] = up[:, :, 128:256]
    for z in range(NZ):
        for start in range(2):
            q = pl.ds(start, 12, stride=2)
            raw1[0, z, q, :] = t1[z, 0:12, :]

    def add1(z):
        lev1.w[z + 1] = lev1.w[z + 1] + raw1[0, z]

    lev1.each(add1, UNROLL)
    lev1.sweep(lev1.w, lev1.u, UNROLL)
    lev1.sweep(lev1.u, lev1.w, UNROLL)

    arrive(sent_o)

    def put_rows0(z):
        lev0.w[z + 1, 16:20, 0:128] = o_rew[0, z]
        lev0.w[z + 1, 20:24, 0:128] = o_rew[1, z]

    def put_side0(z, x):
        lev0.w[z + 1, :, 128:256] = x

    merge_edges(0, 0, o_rns, o_rd, put_rows0, put_side0)
    for z in range(NZ):
        t1[z, 0:8, :] = lev1.w[z + 1, 8:16, :]
        t1[z, 8:10, :] = lev1.w[z + 1, 16:18, :]
        t1[z, 10:12, :] = lev1.w[z + 1, 6:8, :]
        t1[z, 12:16, :] = jnp.zeros((4, 128), F32)
    up = mm(t1[...].reshape(NZ * 16, 128), prolong_0()).reshape(NZ, 16, 256)
    for z in range(NZ):
        for half in range(2):
            part = up[z, 0:12, 128 * half:128 * half + 128]
            for start in range(2):
                raw1[half, z, pl.ds(start, 12, stride=2), :] = part

    def add0(z):
        for half in range(2):
            lanes = slice(128 * half, 128 * half + 128)
            lev0.w[z + 1, :, lanes] = lev0.w[z + 1, :, lanes] + raw1[half, z]

    lev0.each(add0, UNROLL)
    lev0.sweep(lev0.w, lev0.u, UNROLL)
    lev0.sweep(lev0.u, lev0.w, UNROLL)

    def last0(z, u, total):
        r = raw0[3, z] - (lev0.d[z] * u - total)
        sol[z] = u[0:16, 0:128]
        resid[z] = r[0:16, 0:128]

    lev0.stencil(lev0.w, UNROLL, last0)

    for made in pending:
        made.wait_send()


def level_scratch(slabs, rows, lanes):
    def vmem(count):
        return pltpu.VMEM((count, rows, lanes), F32)

    return [vmem(slabs), vmem(slabs), vmem(slabs + 1), vmem(slabs), vmem(slabs), vmem(slabs), vmem(slabs + 2), vmem(slabs + 2)]


def shards(source, kappa_sq, lon_diff, lat_diff, sea_mask):
    def vmem(*shape):
        return pltpu.VMEM(shape, F32)

    scratch = [
        vmem(NZ, 16, 128), vmem(NZ, 16, 128), vmem(NZ, 16, 128), vmem(NZ, 16, 128),
        pltpu.VMEM((NZ, 16, 128), jnp.int32), pltpu.SemaphoreType.DMA((5,)),
        vmem(4, NZ, 24, 256), vmem(8, 128), level_scratch(NZ, 24, 256),
        vmem(3, NZ, 24, 128), level_scratch(NZ, 24, 128),
        vmem(4, HZ, 32, 128), level_scratch(HZ, 32, 128),
        vmem(4, HZ, 16, 128), level_scratch(HZ, 16, 128),
        vmem(3, HZ, 32, 128), level_scratch(HZ, 32, 128),
        vmem(NZ, 16, 128), vmem(NZ, 16, 128), vmem(HZ, 8, 128), vmem(HZ, 32, 128), vmem(HZ, 32, 128), vmem(NZ, 8, 128),
        vmem(2, 4 * NZ + HZ, 2, 128), vmem(2, 2, 16, 128), vmem(2, 4 * NZ + HZ, 2, 128), vmem(2, 2, 16, 128), vmem(4, 2, 8, 128),
        vmem(HZ, 8, 128), vmem(2, 5, 8, 128), vmem(2, 2, 5, 4, 128),
        vmem(2, HZ, 8, 128), vmem(2, 5, 8, 128), vmem(2, 2, 5, 4, 128),
        vmem(HZ, 4, 128), vmem(7, HZ, 4, 128),
        vmem(8, 128), vmem(7, 8, 128), vmem(16 * 24, 128),
        vmem(3 * HZ, 8, 128), vmem(2, 15, 8, 128), vmem(2, 2, 15, 4, 128),
        vmem(2, 3 * HZ, 8, 128), vmem(2, 15, 8, 128), vmem(2, 2, 15, 4, 128),
        vmem(20, 4, 128), vmem(2, 20, 4, 128),
        vmem(4 * HZ, 4, 128), vmem(7, 4 * HZ, 4, 128),
        vmem(32, 128), vmem(7, 32, 128), vmem(16 * 32, 128), vmem(16 * 32, 128),
        vmem(2, NZ, 4, 128), vmem(2, 1, 16, 128), vmem(2, NZ, 4, 128), vmem(2, 1, 16, 128), vmem(4, 1, 8, 128),
        pltpu.SemaphoreType.DMA((96,)), pltpu.SemaphoreType.DMA((96,)),
    ]
    shape = jax.ShapeDtypeStruct(source.shape, F32)
    anywhere = pl.BlockSpec(memory_space=pl.ANY)
    return pl.pallas_call(
        body,
        out_shape=(shape, shape),
        in_specs=[anywhere] * 5,
        out_specs=[pl.BlockSpec(memory_space=pltpu.VMEM)] * 2,
        scratch_shapes=scratch,
        compiler_params=pltpu.CompilerParams(
            collective_id=0, has_side_effects=True, vmem_limit_bytes=54848 * 1024
        ),
    )(source, kappa_sq, lon_diff, lat_diff, sea_mask)

def solution(mesh):
    spec = P(None, "tx", "ty")
    return jax.shard_map(
        shards, mesh=mesh, in_specs=(spec,) * 5, out_specs=(spec, spec), check_vma=False
    )
```

```python
import jax
import jax.numpy as jnp
from jax import lax
from jax.experimental import pallas as pl
from jax.experimental.pallas import tpu as pltpu
from jax.sharding import PartitionSpec as P

NZ = 20
HZ = 10
NTX = 32
NTY = 16
OMEGA = 0.8
UNROLL = 20
MESH = pl.DeviceIdType.MESH
F32 = jnp.float32

DIAGONALS = ((1, 1), (-1, 1), (1, -1), (-1, -1))


def iota(shape, dim):
    return lax.broadcasted_iota(jnp.int32, shape, dim)


def mm(x, m):
    high = x.astype(jnp.bfloat16)
    low = (x - high.astype(F32)).astype(jnp.bfloat16)
    m = m.astype(jnp.bfloat16)
    return lax.dot_general(
        jnp.concatenate([high, low], axis=1), jnp.concatenate([m, m], axis=0),
        (((1,), (0,)), ((), ())), preferred_element_type=F32,
    )


def roll(x, shift, axis):
    shift = shift % x.shape[axis]
    return x if shift == 0 else pltpu.roll(x, shift, axis)


def one_hot(shape, hit, value=1.0):
    row, col = iota(shape, 0), iota(shape, 1)
    return jnp.where(hit(row, col), F32(value), F32(0.0))


def restrict_0():
    return one_hot((128, 128), lambda n, m: m == 32 + (n >> 1), 0.25)


def restrict_1():
    return one_hot((256, 128), lambda n, m: m == n >> 1, 0.25)


def restrict_2():
    return one_hot((128, 128), lambda n, m: m == (n & 64) + 8 + ((n & 63) >> 1), 0.25)


def restrict_3():
    def hit(n, m):
        q = n & 63
        return (m == (n & 64) + 16 + (q >> 1)) & (q >= 16) & (q < 32)

    return one_hot((128, 128), hit, 0.25)


def restrict_all():
    return one_hot((256, 128), lambda n, m: m == ((n & 128) >> 1) + 24 + ((n & 127) >> 4), 1.0 / 256)


def prolong_3():
    return one_hot((128, 128), lambda m, n: m == (n & 64) + 16 + ((n & 63) >> 1))


def prolong_2():
    return one_hot((128, 128), lambda m, n: m == (n & 64) + 8 + ((n & 63) >> 1))


def prolong_1():
    return one_hot((128, 256), lambda m, n: m == n >> 1)


def prolong_0():
    def hit(m, n):
        rel = jnp.where(n >= 192, n - 256, n)
        return (m == 32 + (rel >> 1)) & (rel < 132) & (rel >= -4)

    return one_hot((128, 256), hit)


class Level:
    def __init__(self, slabs, folded, refs):
        self.slabs = slabs
        self.folded = folded
        self.e, self.n, self.v, self.g, self.d, self.c, self.u, self.w = refs

    def each(self, body, unroll):
        def step(z, carry):
            body(z)
            return carry

        lax.fori_loop(0, self.slabs, step, 0, unroll=min(unroll, self.slabs))

    def wrap(self, ref, rows=slice(None)):
        if self.folded:
            ref[0, rows] = roll(ref[self.slabs, rows], 64, 1)
            ref[self.slabs + 1, rows] = roll(ref[1, rows], 64, 1)

    def clear_ends(self):
        if not self.folded:
            for ref in (self.c, self.u, self.w):
                ref[0] = jnp.zeros_like(ref[0])
                ref[self.slabs + 1] = jnp.zeros_like(ref[0])

    def faces(self, kap, lond, latd, sea, unroll, right=None):
        top = self.slabs - 1
        first = sea(0)
        if self.folded:
            low = iota(self.v.shape[1:], 1) < 64
            face_top = jnp.where(low, sea(top) * roll(first, 64, 1), 0.0)
            face_first = roll(face_top, 64, 1)
        else:
            face_top = face_first = jnp.zeros_like(first)
        self.v[0] = face_first

        def slab(z, s, face_below, face_above):
            lw = s * lond(z)
            tw = s * latd(z)
            east = 0.5 * (lw * roll(s, -1, 0) + s * roll(lw, -1, 0))
            north = 0.5 * (tw * roll(s, -1, 1) + s * roll(tw, -1, 1))
            west = roll(east, 1, 0)
            south = roll(north, 1, 1)
            diag = s * kap(z) + (west + east + south + north + face_below + face_above) + (1.0 - s)
            scale = OMEGA / diag
            self.v[z + 1] = face_above
            self.e[z] = east
            self.n[z] = north
            self.d[z] = diag
            self.g[z] = scale
            if right is not None:
                self.c[z + 1] = scale * right(z)

        def step(z, carry):
            s, face_below = carry
            s_above = sea(z + 1)
            face_above = s * s_above
            slab(z, s, face_below, face_above)
            return s_above, face_above

        s, face_below = lax.fori_loop(0, top, step, (first, face_first), unroll=min(unroll, top))
        slab(top, s, face_below, face_top)

    def stencil(self, src, unroll, use, rows=slice(None)):
        def step(z, carry):
            below, u, face_below = carry
            above = src[z + 2, rows]
            face_above = self.v[z + 1, rows]
            e = self.e[z, rows]
            n = self.n[z, rows]
            use(z, u, (
                roll(e * u, 1, 0)
                + e * roll(u, -1, 0)
                + roll(n * u, 1, 1)
                + n * roll(u, -1, 1)
                + face_below * below
                + face_above * above
            ))
            return u, above, face_above

        lax.fori_loop(0, self.slabs, step, (src[0, rows], src[1, rows], self.v[0, rows]), unroll=min(unroll, self.slabs))

    def sweep(self, src, dst, unroll, rows=slice(None)):
        def use(z, u, total):
            dst[z + 1, rows] = (1.0 - OMEGA) * u + self.c[z + 1, rows] + self.g[z, rows] * total

        self.stencil(src, unroll, use, rows)
        self.wrap(dst, rows)

    def remain(self, src, unroll, put):
        self.stencil(src, unroll, lambda z, u, total: put(z, self.d[z] * (1.25 * self.c[z + 1] - u) + total))


def pack_edge(slabs, width, base, count):
    lane = iota(slabs[0].shape, 1)
    out = roll(slabs[0], -base, 1)
    for i in range(1, count):
        out = jnp.where(lane >= width * i, roll(slabs[i], width * i - base, 1), out)
    return out


def body(
    source_in, kappa_in, lon_in, lat_in, mask_in,
    sol, resid,
    source, kappa, lon_diff, lat_diff, mask, in_sem,
    raw0, src0, l0, raw1, l1, raw2, l2, raw3, l3, raw4, l4, t0, t1, t2, t3, t4, q1,
    a_ew, a_ns, a_rew, a_rns, a_rd,
    b_pk, b_ns, b_nc, b_rpk, b_rns, b_rnc,
    f_p, f_rp,
    k_blk, k_z, k_ev,
    p_pk, p_ns, p_nc, p_rpk, p_rns, p_rnc, q_p, q_rp, g_p, g_rp, h_blk, h_z, h_ev, h_od,
    o_ew, o_ns, o_rew, o_rns, o_rd,
    send_sem, recv_sem,
):
    mx, my = lax.axis_index("tx"), lax.axis_index("ty")
    odd = lax.rem(mx, 2) == 1
    counter = [0]
    pending = []
    places = {}

    def shifted(axis, here, shift, count):
        shift = shift % count
        if (axis, shift) not in places:
            there = here + shift
            places[axis, shift] = jnp.where(there >= count, there - count, there) if shift else here
        return places[axis, shift]

    def device(dx, dy):
        return (shifted(0, mx, dx, NTX), shifted(1, my, dy, NTY))

    def copy(src, dst, dx, dy):
        i = counter[0]
        counter[0] += 1
        made = pltpu.make_async_remote_copy(
            src_ref=src, dst_ref=dst, send_sem=send_sem.at[i], recv_sem=recv_sem.at[i],
            device_id=device(dx, dy),
            device_id_type=MESH,
        )
        made.start()
        pending.append(made)
        return made

    def arrive(copies):
        for made in copies:
            made.wait_recv()

    lev0 = Level(NZ, False, l0)
    lev1 = Level(NZ, False, l1)
    lev2 = Level(HZ, True, l2)
    lev3 = Level(HZ, True, l3)
    lev4 = Level(HZ, True, l4)

    fetched = [
        pltpu.make_async_copy(src, dst, in_sem.at[i])
        for i, (src, dst) in enumerate((
            (mask_in, mask), (lon_in, lon_diff), (lat_in, lat_diff), (kappa_in, kappa), (source_in, source)
        ))
    ]
    for made in fetched:
        made.start()

    peers = [(2 * k, 0) for k in range(1, 16)] + [(1, 0), (-1, 0), (3, 0), (-3, 0)]
    peers += [(0, d) for d in (1, 2, 3, -1, -2, -3)] + list(DIAGONALS)
    barrier = pltpu.get_barrier_semaphore()
    for dx, dy in peers:
        pl.semaphore_signal(
            barrier, inc=1,
            device_id=device(dx, dy),
            device_id_type=MESH,
        )

    lane16 = iota((16, 128), 1)
    place = ((1, 0), (0, 0), (0, 60), (1, 60))
    edge_n = [jnp.zeros((16, 128), F32)] * 4
    edge_s = [jnp.zeros((16, 128), F32)] * 4
    own0 = (
        lambda z: kappa[z],
        lambda z: mask[z].astype(F32) * lon_diff[z],
        lambda z: mask[z].astype(F32) * lat_diff[z],
        lambda z: source[z],
    )
    for f, needed in ((1, (0, 1)), (2, (2,)), (0, (3,)), (3, (4,))):
        for i in needed:
            fetched[i].wait()
        for z in range(NZ):
            x = own0[f](z)
            raw0[f, z, 0:16, 0:128] = x
            a_ew[0, f * NZ + z] = x[0:2]
            a_ew[1, f * NZ + z] = x[14:16]
            if f == 1:
                a_ew[0, 4 * NZ + z // 2, z % 2:z % 2 + 1] = x[2:3]
                a_ew[1, 4 * NZ + z // 2, z % 2:z % 2 + 1] = x[13:14]
            start = place[f][1] + 3 * z
            edge_n[f] = jnp.where(lane16 >= start, roll(x, start - 125, 1), edge_n[f])
            edge_s[f] = jnp.where(lane16 >= start, roll(x, start, 1), edge_s[f])
    for pair, (f, g) in enumerate(((1, 2), (0, 3))):
        a_ns[0, pair] = jnp.where(lane16 < 60, edge_n[f], edge_n[g])
        a_ns[1, pair] = jnp.where(lane16 < 60, edge_s[f], edge_s[g])

    pl.semaphore_wait(barrier, len(peers))

    def send_edges(ew, ns, rew, rns, rd):
        made = [copy(ns.at[0, :, 8:16, :], rd.at[0], 1, 1)]
        made.append(copy(ns.at[0, :, 0:8, :], rd.at[1], -1, 1))
        made.append(copy(ns.at[1, :, 8:16, :], rd.at[2], 1, -1))
        made.append(copy(ns.at[1, :, 0:8, :], rd.at[3], -1, -1))
        made += [copy(ew.at[0], rew.at[0], -1, 0), copy(ew.at[1], rew.at[1], 1, 0)]
        made += [copy(ns.at[0], rns.at[0], 0, 1), copy(ns.at[1], rns.at[1], 0, -1)]
        return made

    has_s, has_n = my > 0, my < NTY - 1

    def merge_edges(f, base, rns, rd, put_rows, put_side):
        sub = iota((8, 128), 0)
        south = jnp.concatenate([rns[0, f], jnp.where(sub < 4, rd[1, f], rd[0, f])], axis=0)
        north = jnp.concatenate([rns[1, f], jnp.where(sub < 4, rd[3, f], rd[2, f])], axis=0)
        lane = iota((24, 128), 1)
        south = jnp.where(has_s, south, 0.0)
        north = jnp.where(has_n, north, 0.0)
        for z in range(NZ):
            put_rows(z)
            start = base + 3 * z
            side = jnp.where(lane < 3, roll(north, -start, 1), roll(south, 125 - start, 1))
            put_side(z, jnp.where((lane < 3) | (lane >= 125), side, 0.0))

    sent_a = send_edges(a_ew, a_ns, a_rew, a_rns, a_rd)
    for f in range(4):
        for z in range(NZ):
            raw0[f, z, 16:24, 0:128] = jnp.zeros((8, 128), F32)

    m0 = restrict_0()

    def down_0(x):
        t1[...] = mm(x.reshape(NZ * 16, 128), m0).reshape(NZ, 16, 128)
        return t1[:, pl.ds(0, 8, stride=2), :] + t1[:, pl.ds(1, 8, stride=2), :]

    def pack_1(x, f, pk, ns, nc):
        lane = iota((8, 128), 1)
        for k in range(HZ):
            pk[f * HZ + k] = jnp.where(lane < 64, roll(x[k], -32, 1), roll(x[k + HZ], 32, 1))
        for k in range(5):
            group = [x[k + 5 * j] for j in range(4)]
            for side, base in ((0, 64), (1, 32)):
                edge = pack_edge(group, 32, base, 4)
                ns[side, f * 5 + k] = edge
                nc[side, 0, f * 5 + k] = edge[0:4]
                nc[side, 1, f * 5 + k] = edge[4:8]

    def send_1(pk, ns, nc, rpk, rns, rnc):
        made = [copy(nc.at[0, 1], rnc.at[0, 1], 1, 1)]
        made.append(copy(nc.at[0, 0], rnc.at[0, 0], -1, 1))
        made.append(copy(nc.at[1, 1], rnc.at[1, 1], 1, -1))
        made.append(copy(nc.at[1, 0], rnc.at[1, 0], -1, -1))
        made += [copy(pk, rpk.at[0], -1, 0), copy(pk, rpk.at[1], 1, 0)]
        made += [copy(ns.at[0], rns.at[0], 0, 1), copy(ns.at[1], rns.at[1], 0, -1)]
        return made

    def merge_1(f, own, rpk, rns, rnc, put, first):
        lane = iota((8, 128), 1)
        blank = jnp.zeros((4, 128), F32)

        def edges(z, pieces):
            south = jnp.where(has_s, roll(pieces[0], -32 * (z // 5), 1), 0.0)
            north = jnp.where(has_n, roll(pieces[1], 96 - 32 * (z // 5), 1), 0.0)
            return south, north

        for z in range(NZ):
            at = f * 5 + z % 5
            if first:
                k, shift = (z, 32) if z < HZ else (z - HZ, -32)
                south, north = edges(z, (rns[0, at], rns[1, at]))
                put(z, 8, jnp.where(lane < 32, south, jnp.where(lane < 96, own(z), north)))
                put(z, 16, roll(rpk[0, f * HZ + k], shift, 1))
                put(z, 0, roll(rpk[1, f * HZ + k], shift, 1))
            else:
                for i, start in ((0, 16), (1, 0)):
                    pieces = [rnc[side, i, at] for side in range(2)]
                    pieces = [jnp.concatenate([p, blank] if i == 0 else [blank, p], axis=0) for p in pieces]
                    south, north = edges(z, pieces)
                    put(z, start, jnp.where(lane < 32, south, jnp.where(lane < 96, own(z)[start:start + 8], north)))

    own1 = [
        down_0(kappa[...]),
        0.25 * down_0(lon_diff[...]),
        0.25 * down_0(lat_diff[...]),
        (down_0(mask[...].astype(F32)) > 0.0).astype(F32),
    ]

    m1 = restrict_1()

    def down_1(x):
        pair = jnp.concatenate([x[0:HZ], x[HZ:NZ]], axis=2).reshape(HZ * 8, 256)
        t2[...] = mm(pair, m1).reshape(HZ, 8, 128)
        return t2[:, pl.ds(0, 4, stride=2), :] + t2[:, pl.ds(1, 4, stride=2), :]

    own2 = [
        down_1(own1[0]),
        0.25 * down_1(own1[1]),
        0.25 * down_1(own1[2]),
        (down_1(own1[3]) > 0.0).astype(F32),
    ]
    for f in range(4):
        g_p[f * HZ:(f + 1) * HZ] = own2[f]
        for k in range(5):
            q_p[f * 5 + k] = own2[f][k] + roll(own2[f][k + 5], 32, 1)
    sent_q = [copy(q_p, q_rp.at[0], 0, 1), copy(q_p, q_rp.at[1], 0, -1)]

    for f, x in enumerate((own1[0], own1[3] * own1[1], own1[3] * own1[2])):
        pack_1(x, f, p_pk, p_ns, p_nc)
        raw1[f, :, 8:16, :] = x
    sent_p1 = send_1(p_pk, p_ns, p_nc, p_rpk, p_rns, p_rnc)

    def send_z(blk, slots):
        slots[3] = blk[...]
        return [copy(blk, slots.at[3 - d], 0, d) for d in (3, -3, 2, -2, 1, -1)]

    def window_row(slots, count):
        row = jnp.zeros((count, 128), F32)
        for s in range(7):
            inside = (my + (s - 3) >= 0) & (my + (s - 3) < NTY)
            row = row + jnp.where(inside, roll(slots[s], 8 * (s - 3), 1), 0.0)
        return row

    def folded_window_row(slots):
        part = iota((8, 128), 1) & 63
        out = [jnp.zeros((8, 128), F32)] * 3
        for s in range(7):
            inside = (my + (s - 3) >= 0) & (my + (s - 3) < NTY)
            block = jnp.where(inside, slots[s], 0.0)
            for i in range(3):
                pick = (part >= 24 + 8 * i) & (part < 32 + 8 * i)
                out[i] = out[i] + roll(jnp.where(pick, block, 0.0), 8 * (s - 3 - i), 1)
        return jnp.concatenate(out, axis=0)

    def send_plane(row, ev, count):
        own = pl.ds(8 * count, count)
        ev[own, :] = row
        return [
            copy(ev.at[own], ev.at[pl.ds(((8 - k) % 16) * count, count)], 2 * k, 0)
            for k in (10, 6, 9, 7, 11, 5, 2, 14, 8, 3, 13, 1, 15, 4, 12)
        ]

    def send_sibling(ev, od):
        i = counter[0]
        counter[0] += 1
        made = pltpu.make_async_remote_copy(
            src_ref=ev, dst_ref=od, send_sem=send_sem.at[i], recv_sem=recv_sem.at[i],
            device_id=(mx + 1 - 2 * lax.rem(mx, 2), my), device_id_type=MESH,
        )
        made.start()
        pending.append(made)
        return [made]

    def window_slab(ev, od, index, count, put):
        put(pl.ds(0, 16, stride=2), ev[pl.ds(index, 16, stride=count), :])
        other = od[pl.ds(index, 16, stride=count), :]
        put(pl.ds(1, 16, stride=2), jnp.where(odd, roll(other, -1, 0), other))

    arrive(sent_a)
    for f in range(4):
        def put_rows(z):
            raw0[f, z, 16:18, 0:128] = a_rew[0, f * NZ + z]
            raw0[f, z, 22:24, 0:128] = a_rew[1, f * NZ + z]
            if f == 1:
                pick = slice(z % 2, z % 2 + 1)
                raw0[f, z, 18:19, 0:128] = a_rew[0, 4 * NZ + z // 2, pick]
                raw0[f, z, 21:22, 0:128] = a_rew[1, 4 * NZ + z // 2, pick]

        def put_side(z, x):
            raw0[f, z, :, 128:256] = x

        merge_edges(place[f][0], place[f][1], a_rns, a_rd, put_rows, put_side)

    def send_2(p, rp):
        return [copy(p, rp.at[3 - d], d, 0) for d in (3, -3, 2, -2, 1, -1)]

    arrive(sent_q)
    part = iota((4, 128), 1) & 63
    for f in range(4):
        for k in range(HZ):
            south = roll(q_rp[0, f * 5 + k % 5], -32 if k < 5 else -64, 1)
            north = roll(q_rp[1, f * 5 + k % 5], 32 if k < 5 else 0, 1)
            south = jnp.where(has_s, south, 0.0)
            north = jnp.where(has_n, north, 0.0)
            g_p[f * HZ + k] = jnp.where(part < 16, south, jnp.where(part < 48, g_p[f * HZ + k], north))
    sent_p2 = send_2(g_p, g_rp)

    def sea0(z):
        return (raw0[1, z] > 0.0).astype(F32)

    lev0.faces(lambda z: raw0[0, z], lambda z: raw0[1, z], lambda z: raw0[2, z], sea0, UNROLL, lambda z: raw0[3, z])
    lev0.clear_ends()


    lev0.sweep(lev0.c, lev0.w, UNROLL)

    def remain0(z, u, total):
        r = raw0[3, z] - (lev0.d[z] * u - total)
        t0[z] = r[0:16, 0:128]

    lev0.stencil(lev0.w, UNROLL, remain0)
    b1 = down_0(t0[...])

    arrive(sent_p1)

    def put1(f):
        def put(z, start, x):
            raw1[f, z, start:start + 8, :] = x

        return put

    def sea_1(z):
        return (raw1[1, z] > 0.0).astype(F32)

    for f in range(3):
        merge_1(f, lambda z: raw1[f, z, 8:16, :], p_rpk, p_rns, p_rnc, put1(f), True)
    middle = slice(8, 16)
    c1 = []
    for z in range(NZ):
        s, lw, tw = sea_1(z), raw1[1, z], raw1[2, z, middle, :]
        here = s[middle]
        east = 0.5 * (lw * roll(s, -1, 0) + s * roll(lw, -1, 0))
        north = 0.5 * (tw * roll(here, -1, 1) + here * roll(tw, -1, 1))
        faces = roll(east, 1, 0)[middle] + east[middle] + roll(north, 1, 1) + north
        for other in (z - 1, z + 1):
            if 0 <= other < NZ:
                faces = faces + here * sea_1(other)[middle]
        c1.append(OMEGA / (here * raw1[0, z, middle, :] + faces + (1.0 - here)) * b1[z])
    c1 = jnp.stack(c1)
    q1[...] = c1
    pack_1(c1, 0, b_pk, b_ns, b_nc)
    sent_b = send_1(b_pk, b_ns, b_nc, b_rpk, b_rns, b_rnc)

    for f in range(3):
        merge_1(f, lambda z: raw1[f, z], None, p_rns, p_rnc, put1(f), False)
    lev1.faces(lambda z: raw1[0, z], lambda z: raw1[1, z], lambda z: raw1[2, z], sea_1, UNROLL)
    lev1.clear_ends()

    edge_n = jnp.zeros((16, 128), F32)
    edge_s = jnp.zeros((16, 128), F32)
    for z in range(NZ):
        x = lev0.w[z + 1, 0:16, 0:128]
        o_ew[0, z] = x[0:4]
        o_ew[1, z] = x[12:16]
        edge_n = jnp.where(lane16 >= 3 * z, roll(x, 3 * z - 125, 1), edge_n)
        edge_s = jnp.where(lane16 >= 3 * z, roll(x, 3 * z, 1), edge_s)
    o_ns[0, 0] = edge_n
    o_ns[1, 0] = edge_s

    mall = restrict_all()

    def down_all(x):
        pair = jnp.concatenate([x[0:HZ], x[HZ:NZ]], axis=2).reshape(HZ * 16, 256)
        return jnp.sum(mm(pair, mall).reshape(HZ, 16, 128), axis=1)

    sea4 = (down_all(mask[...].astype(F32)) > 0.0).astype(F32)
    h_blk[0:10, :] = down_all(kappa[...])
    h_blk[10:20, :] = sea4 * (down_all(lon_diff[...]) * (1.0 / 256))
    h_blk[20:30, :] = sea4 * (down_all(lat_diff[...]) * (1.0 / 256))
    h_blk[30:32, :] = jnp.zeros((2, 128), F32)

    arrive(sent_p2)
    for f in range(4):
        for s in range(7):
            piece = g_p if s == 3 else g_rp.at[s]
            raw2[f, :, 4 * s:4 * s + 4, :] = piece[f * HZ:(f + 1) * HZ]
        raw2[f, :, 28:32, :] = jnp.zeros((HZ, 4, 128), F32)
    lev2.faces(lambda z: raw2[0, z], lambda z: raw2[1, z], lambda z: raw2[2, z], lambda z: raw2[3, z], UNROLL)

    m2 = restrict_2()

    def down_2(x):
        t3[...] = mm(x.reshape(HZ * 32, 128), m2).reshape(HZ, 32, 128)
        return t3[:, pl.ds(0, 16, stride=2), :] + t3[:, pl.ds(1, 16, stride=2), :]

    raw3[0] = down_2(raw2[0])
    raw3[1] = 0.25 * down_2(raw2[1])
    raw3[2] = 0.25 * down_2(raw2[2])
    raw3[3] = (down_2(raw2[3]) > 0.0).astype(F32)
    lev3.faces(lambda z: raw3[0, z], lambda z: raw3[1, z], lambda z: raw3[2, z], lambda z: raw3[3, z], UNROLL)

    arrive(sent_b)
    sent_hz = send_z(h_blk, h_z)

    def put1c(z, start, x):
        lev1.c[z + 1, start:start + 8, :] = x

    merge_1(0, lambda z: q1[z], b_rpk, b_rns, b_rnc, put1c, True)
    merge_1(0, lambda z: lev1.c[z + 1], None, b_rns, b_rnc, put1c, False)
    lev1.sweep(lev1.c, lev1.w, UNROLL)

    def remain1(z, r):
        q1[z] = r[8:16]

    lev1.remain(lev1.w, UNROLL, remain1)
    b2 = down_1(q1[...])

    f_p[...] = lev2.g[:, 12:16, :] * b2
    sent_c = send_2(f_p, f_rp)

    arrive(sent_hz)
    row_h = window_row(h_z, 32)
    arrive(sent_c)
    sent_hp = send_plane(row_h, h_ev, 32)
    sent_o = send_edges(o_ew, o_ns, o_rew, o_rns, o_rd)
    for s in range(7):
        piece = f_p if s == 3 else f_rp.at[s]
        lev2.c[1:HZ + 1, 4 * s:4 * s + 4, :] = piece[...]
    lev2.c[1:HZ + 1, 28:32, :] = jnp.zeros((HZ, 4, 128), F32)
    lev2.wrap(lev2.c)
    lev2.sweep(lev2.c, lev2.w, UNROLL)

    def remain2(z, r):
        t4[z] = r

    lev2.remain(lev2.w, UNROLL, remain2)

    lev3.c[1:HZ + 1] = lev3.g[...] * down_2(t4[...])
    lev3.wrap(lev3.c)
    lev3.sweep(lev3.c, lev3.w, UNROLL)

    def remain3(z, r):
        t3[z, 0:16, :] = r

    lev3.remain(lev3.w, UNROLL, remain3)
    m3 = restrict_3()
    t3[:, 0:16, :] = mm(t3[:, 0:16, :].reshape(HZ * 16, 128), m3).reshape(HZ, 16, 128)
    for z in range(8):
        row = t3[z, 6:7, :] + t3[z, 7:8, :] + roll(t3[z, 8:9, :] + t3[z, 9:10, :], 8, 1)
        if z < 4:
            at = 6 if z < 2 else 8
            last = t3[8 + z % 2, at:at + 1, :] + t3[8 + z % 2, at + 1:at + 2, :]
            row = row + roll(last, 16, 1)
        k_blk[z:z + 1, :] = row
    sent_kz = send_z(k_blk, k_z)

    arrive(sent_hp)
    sent_hs = send_sibling(h_ev, h_od)

    arrive(sent_kz)
    sent_kp = send_plane(folded_window_row(k_z), k_ev, 24)

    arrive(sent_hs)
    for f in range(3):
        for z in range(HZ):
            def put4(rows, x):
                raw4[f, z, rows, :] = x

            window_slab(h_ev, h_od, f * HZ + z, 32, put4)

    def sea_4(z):
        return (raw4[1, z] > 0.0).astype(F32)

    lev4.faces(lambda z: raw4[0, z], lambda z: raw4[1, z], lambda z: raw4[2, z], sea_4, UNROLL)

    arrive(sent_o)

    def put_rows0(z):
        lev0.w[z + 1, 16:20, 0:128] = o_rew[0, z]
        lev0.w[z + 1, 20:24, 0:128] = o_rew[1, z]

    def put_side0(z, x):
        lev0.w[z + 1, :, 128:256] = x

    merge_edges(0, 0, o_rns, o_rd, put_rows0, put_side0)
    arrive(sent_kp)
    for z in range(HZ):
        for i in range(2):
            at = 8 * i + z if z < 8 else 16 + 2 * i + z - 8
            lev4.c[z + 1, pl.ds(i, 16, stride=2), :] = k_ev[pl.ds(at, 16, stride=24), :]
    for z in range(HZ):
        lev4.c[z + 1] = lev4.g[z] * lev4.c[z + 1]
    lev4.wrap(lev4.c)
    lev4.sweep(lev4.c, lev4.u, UNROLL)

    def two(step, carry):
        lev4.sweep(lev4.u, lev4.w, UNROLL)
        lev4.sweep(lev4.w, lev4.u, UNROLL)
        return carry

    lax.fori_loop(0, 6, two, 0)
    lev4.sweep(lev4.u, lev4.w, UNROLL)
    centre = slice(8, 24)
    for src, dst in ((lev4.w, lev4.u), (lev4.u, lev4.w)) * 2 + ((lev4.w, lev4.u),):
        lev4.sweep(src, dst, UNROLL, centre)

    up = mm(lev4.u[1:HZ + 1, 13:21, :].reshape(HZ * 8, 128), prolong_3()).reshape(HZ, 8, 128)
    for start in range(2):
        t3[:, pl.ds(start, 8, stride=2), :] = up

    def add3(z):
        lev3.w[z + 1] = lev3.w[z + 1] + t3[z, 0:16, :]

    lev3.each(add3, UNROLL)
    lev3.wrap(lev3.w)
    lev3.sweep(lev3.w, lev3.u, UNROLL)
    lev3.sweep(lev3.u, lev3.w, UNROLL)

    up = mm(lev3.w[1:HZ + 1].reshape(HZ * 16, 128), prolong_2()).reshape(HZ, 16, 128)
    for start in range(2):
        t3[:, pl.ds(start, 16, stride=2), :] = up

    def add2(z):
        lev2.w[z + 1] = lev2.w[z + 1] + t3[z]

    lev2.each(add2, UNROLL)
    lev2.wrap(lev2.w)
    lev2.sweep(lev2.w, lev2.u, UNROLL)
    lev2.sweep(lev2.u, lev2.w, UNROLL)

    t3[:, 0:16, :] = lev2.w[1:HZ + 1, 8:24, :]
    up = mm(t3[:, 0:16, :].reshape(HZ * 16, 128), prolong_1()).reshape(HZ, 16, 256)
    for start in range(2):
        t1[0:HZ, :, :] = up[:, :, 0:128]
        t1[HZ:NZ, :, :] = up[:, :, 128:256]
    for z in range(NZ):
        for start in range(2):
            q = pl.ds(start, 12, stride=2)
            raw1[0, z, q, :] = t1[z, 0:12, :]

    def add1(z):
        lev1.w[z + 1] = lev1.w[z + 1] + raw1[0, z]

    lev1.each(add1, UNROLL)
    lev1.sweep(lev1.w, lev1.u, UNROLL)
    lev1.sweep(lev1.u, lev1.w, UNROLL)

    for z in range(NZ):
        t1[z, 0:8, :] = lev1.w[z + 1, 8:16, :]
        t1[z, 8:10, :] = lev1.w[z + 1, 16:18, :]
        t1[z, 10:12, :] = lev1.w[z + 1, 6:8, :]
        t1[z, 12:16, :] = jnp.zeros((4, 128), F32)
    up = mm(t1[...].reshape(NZ * 16, 128), prolong_0()).reshape(NZ, 16, 256)
    for z in range(NZ):
        for half in range(2):
            part = up[z, 0:12, 128 * half:128 * half + 128]
            for start in range(2):
                raw1[half, z, pl.ds(start, 12, stride=2), :] = part

    def add0(z):
        for half in range(2):
            lanes = slice(128 * half, 128 * half + 128)
            lev0.w[z + 1, :, lanes] = lev0.w[z + 1, :, lanes] + raw1[half, z]

    lev0.each(add0, UNROLL)
    lev0.sweep(lev0.w, lev0.u, UNROLL)
    lev0.sweep(lev0.u, lev0.w, UNROLL)

    def last0(z, u, total):
        r = raw0[3, z] - (lev0.d[z] * u - total)
        sol[z] = u[0:16, 0:128]
        resid[z] = r[0:16, 0:128]

    lev0.stencil(lev0.w, UNROLL, last0)

    for made in pending:
        made.wait_send()


def level_scratch(slabs, rows, lanes):
    def vmem(count):
        return pltpu.VMEM((count, rows, lanes), F32)

    return [vmem(slabs), vmem(slabs), vmem(slabs + 1), vmem(slabs), vmem(slabs), vmem(slabs + 2), vmem(slabs + 2), vmem(slabs + 2)]


def shards(source, kappa_sq, lon_diff, lat_diff, sea_mask):
    def vmem(*shape):
        return pltpu.VMEM(shape, F32)

    scratch = [
        vmem(NZ, 16, 128), vmem(NZ, 16, 128), vmem(NZ, 16, 128), vmem(NZ, 16, 128),
        pltpu.VMEM((NZ, 16, 128), jnp.int32), pltpu.SemaphoreType.DMA((5,)),
        vmem(4, NZ, 24, 256), vmem(8, 128), level_scratch(NZ, 24, 256),
        vmem(3, NZ, 24, 128), level_scratch(NZ, 24, 128),
        vmem(4, HZ, 32, 128), level_scratch(HZ, 32, 128),
        vmem(4, HZ, 16, 128), level_scratch(HZ, 16, 128),
        vmem(3, HZ, 32, 128), level_scratch(HZ, 32, 128),
        vmem(NZ, 16, 128), vmem(NZ, 16, 128), vmem(HZ, 8, 128), vmem(HZ, 32, 128), vmem(HZ, 32, 128), vmem(NZ, 8, 128),
        vmem(2, 4 * NZ + HZ, 2, 128), vmem(2, 2, 16, 128), vmem(2, 4 * NZ + HZ, 2, 128), vmem(2, 2, 16, 128), vmem(4, 2, 8, 128),
        vmem(HZ, 8, 128), vmem(2, 5, 8, 128), vmem(2, 2, 5, 4, 128),
        vmem(2, HZ, 8, 128), vmem(2, 5, 8, 128), vmem(2, 2, 5, 4, 128),
        vmem(HZ, 4, 128), vmem(7, HZ, 4, 128),
        vmem(8, 128), vmem(7, 8, 128), vmem(16 * 24, 128),
        vmem(3 * HZ, 8, 128), vmem(2, 15, 8, 128), vmem(2, 2, 15, 4, 128),
        vmem(2, 3 * HZ, 8, 128), vmem(2, 15, 8, 128), vmem(2, 2, 15, 4, 128),
        vmem(20, 4, 128), vmem(2, 20, 4, 128),
        vmem(4 * HZ, 4, 128), vmem(7, 4 * HZ, 4, 128),
        vmem(32, 128), vmem(7, 32, 128), vmem(16 * 32, 128), vmem(16 * 32, 128),
        vmem(2, NZ, 4, 128), vmem(2, 1, 16, 128), vmem(2, NZ, 4, 128), vmem(2, 1, 16, 128), vmem(4, 1, 8, 128),
        pltpu.SemaphoreType.DMA((96,)), pltpu.SemaphoreType.DMA((96,)),
    ]
    shape = jax.ShapeDtypeStruct(source.shape, F32)
    anywhere = pl.BlockSpec(memory_space=pl.ANY)
    return pl.pallas_call(
        body,
        out_shape=(shape, shape),
        in_specs=[anywhere] * 5,
        out_specs=[pl.BlockSpec(memory_space=pltpu.VMEM)] * 2,
        scratch_shapes=scratch,
        compiler_params=pltpu.CompilerParams(
            collective_id=0, has_side_effects=True, vmem_limit_bytes=54848 * 1024
        ),
    )(source, kappa_sq, lon_diff, lat_diff, sea_mask)

def solution(mesh):
    spec = P(None, "tx", "ty")
    return jax.shard_map(
        shards, mesh=mesh, in_specs=(spec,) * 5, out_specs=(spec, spec), check_vma=False
    )
```

```python
import jax
import jax.numpy as jnp
from jax import lax
from jax.experimental import pallas as pl
from jax.experimental.pallas import tpu as pltpu
from jax.sharding import PartitionSpec as P

NZ = 20
HZ = 10
NTX = 32
NTY = 16
OMEGA = 0.8
UNROLL = 5
MESH = pl.DeviceIdType.MESH
F32 = jnp.float32

DIAGONALS = ((1, 1), (-1, 1), (1, -1), (-1, -1))


def iota(shape, dim):
    return lax.broadcasted_iota(jnp.int32, shape, dim)


def mm(x, m):
    high = x.astype(jnp.bfloat16)
    low = (x - high.astype(F32)).astype(jnp.bfloat16)
    m = m.astype(jnp.bfloat16)
    return lax.dot_general(
        jnp.concatenate([high, low], axis=1), jnp.concatenate([m, m], axis=0),
        (((1,), (0,)), ((), ())), preferred_element_type=F32,
    )


def roll(x, shift, axis):
    shift = shift % x.shape[axis]
    return x if shift == 0 else pltpu.roll(x, shift, axis)


def one_hot(shape, hit, value=1.0):
    row, col = iota(shape, 0), iota(shape, 1)
    return jnp.where(hit(row, col), F32(value), F32(0.0))


def restrict_0():
    return one_hot((128, 128), lambda n, m: m == 32 + (n >> 1), 0.25)


def restrict_1():
    return one_hot((256, 128), lambda n, m: m == n >> 1, 0.25)


def restrict_2():
    return one_hot((128, 128), lambda n, m: m == (n & 64) + 8 + ((n & 63) >> 1), 0.25)


def restrict_3():
    def hit(n, m):
        q = n & 63
        return (m == (n & 64) + 16 + (q >> 1)) & (q >= 16) & (q < 32)

    return one_hot((128, 128), hit, 0.25)


def restrict_all():
    return one_hot((256, 128), lambda n, m: m == ((n & 128) >> 1) + 24 + ((n & 127) >> 4), 1.0 / 256)


def prolong_3():
    return one_hot((128, 128), lambda m, n: m == (n & 64) + 16 + ((n & 63) >> 1))


def prolong_2():
    return one_hot((128, 128), lambda m, n: m == (n & 64) + 8 + ((n & 63) >> 1))


def prolong_1():
    return one_hot((128, 256), lambda m, n: m == n >> 1)


def prolong_0():
    def hit(m, n):
        rel = jnp.where(n >= 192, n - 256, n)
        return (m == 32 + (rel >> 1)) & (rel < 132) & (rel >= -4)

    return one_hot((128, 256), hit)


def spin(x, shift):
    return pltpu.roll(x, shift, 1)


def repeat(count, body, unroll=1):
    def step(i, carry):
        body(i)
        return carry

    lax.fori_loop(0, count, step, 0, unroll=unroll)


class Level:
    def __init__(self, slabs, folded, refs):
        self.slabs = slabs
        self.folded = folded
        self.e, self.n, self.v, self.g, self.d, self.c, self.u, self.w = refs

    def each(self, body, unroll):
        def step(z, carry):
            body(z)
            return carry

        lax.fori_loop(0, self.slabs, step, 0, unroll=min(unroll, self.slabs))

    def wrap(self, ref, rows=slice(None)):
        if self.folded:
            ref[0, rows] = roll(ref[self.slabs, rows], 64, 1)
            ref[self.slabs + 1, rows] = roll(ref[1, rows], 64, 1)

    def clear_ends(self):
        if not self.folded:
            for ref in (self.c, self.u, self.w):
                ref[0] = jnp.zeros_like(ref[0])
                ref[self.slabs + 1] = jnp.zeros_like(ref[0])

    def faces(self, kap, lond, latd, sea, unroll, right=None):
        top = self.slabs - 1
        first = sea(0)
        if self.folded:
            low = iota(self.v.shape[1:], 1) < 64
            face_top = jnp.where(low, sea(top) * roll(first, 64, 1), 0.0)
            face_first = roll(face_top, 64, 1)
        else:
            face_top = face_first = jnp.zeros_like(first)
        self.v[0] = face_first

        def slab(z, s, face_below, face_above):
            lw = s * lond(z)
            tw = s * latd(z)
            east = 0.5 * (lw * roll(s, -1, 0) + s * roll(lw, -1, 0))
            north = 0.5 * (tw * roll(s, -1, 1) + s * roll(tw, -1, 1))
            west = roll(east, 1, 0)
            south = roll(north, 1, 1)
            diag = s * kap(z) + (west + east + south + north + face_below + face_above) + (1.0 - s)
            scale = OMEGA / diag
            self.v[z + 1] = face_above
            self.e[z] = east
            self.n[z] = north
            self.d[z] = diag
            self.g[z] = scale
            if right is not None:
                self.c[z + 1] = scale * right(z)

        def step(z, carry):
            s, face_below = carry
            s_above = sea(z + 1)
            face_above = s * s_above
            slab(z, s, face_below, face_above)
            return s_above, face_above

        s, face_below = lax.fori_loop(0, top, step, (first, face_first), unroll=min(unroll, top))
        slab(top, s, face_below, face_top)

    def stencil(self, src, unroll, use, rows=slice(None)):
        def step(z, carry):
            below, u, face_below = carry
            above = src[z + 2, rows]
            face_above = self.v[z + 1, rows]
            e = self.e[z, rows]
            n = self.n[z, rows]
            use(z, u, (
                roll(e * u, 1, 0)
                + e * roll(u, -1, 0)
                + roll(n * u, 1, 1)
                + n * roll(u, -1, 1)
                + face_below * below
                + face_above * above
            ))
            return u, above, face_above

        lax.fori_loop(0, self.slabs, step, (src[0, rows], src[1, rows], self.v[0, rows]), unroll=min(unroll, self.slabs))

    def sweep(self, src, dst, unroll, rows=slice(None)):
        def use(z, u, total):
            dst[z + 1, rows] = (1.0 - OMEGA) * u + self.c[z + 1, rows] + self.g[z, rows] * total

        self.stencil(src, unroll, use, rows)
        self.wrap(dst, rows)

    def remain(self, src, unroll, put):
        self.stencil(src, unroll, lambda z, u, total: put(z, self.d[z] * (1.25 * self.c[z + 1] - u) + total))


def pack_edge(slabs, width, base, count):
    lane = iota(slabs[0].shape, 1)
    out = roll(slabs[0], -base, 1)
    for i in range(1, count):
        out = jnp.where(lane >= width * i, roll(slabs[i], width * i - base, 1), out)
    return out


def body(
    source_in, kappa_in, lon_in, lat_in, mask_in,
    sol, resid,
    source, mask, raw_in, own1, h_tmp, up0, in_sem,
    raw0, src0, l0, raw1, l1, raw2, l2, raw3, l3, raw4, l4, t0, t1, t2, t3, t4, q1,
    a_ew, a_ns, a_rew, a_rns, a_rd,
    b_pk, b_ns, b_nc, b_rpk, b_rns, b_rnc,
    f_p, f_rp,
    k_blk, k_z, k_ev,
    p_pk, p_ns, p_nc, p_rpk, p_rns, p_rnc, q_p, q_rp, g_p, g_rp, h_blk, h_z, h_ev, h_od,
    o_ew, o_ns, o_rew, o_rns, o_rd,
    send_sem, recv_sem,
):
    mx, my = lax.axis_index("tx"), lax.axis_index("ty")
    odd = lax.rem(mx, 2) == 1
    counter = [0]
    pending = []
    places = {}

    def shifted(axis, here, shift, count):
        shift = shift % count
        if (axis, shift) not in places:
            there = here + shift
            places[axis, shift] = jnp.where(there >= count, there - count, there) if shift else here
        return places[axis, shift]

    def device(dx, dy):
        return (shifted(0, mx, dx, NTX), shifted(1, my, dy, NTY))

    def copy(src, dst, dx, dy):
        i = counter[0]
        counter[0] += 1
        made = pltpu.make_async_remote_copy(
            src_ref=src, dst_ref=dst, send_sem=send_sem.at[i], recv_sem=recv_sem.at[i],
            device_id=device(dx, dy),
            device_id_type=MESH,
        )
        made.start()
        pending.append(made)
        return made

    def arrive(copies):
        for made in copies:
            made.wait_recv()

    lev0 = Level(NZ, False, l0)
    lev1 = Level(NZ, False, l1)
    lev2 = Level(HZ, True, l2)
    lev3 = Level(HZ, True, l3)
    lev4 = Level(HZ, True, l4)

    fetched = [
        pltpu.make_async_copy(src, dst, in_sem.at[i])
        for i, (src, dst) in enumerate((
            (mask_in, mask), (lon_in, raw_in.at[1]), (lat_in, raw_in.at[2]), (kappa_in, raw_in.at[0]), (source_in, source)
        ))
    ]
    for made in fetched:
        made.start()

    peers = [(2 * k, 0) for k in range(1, 16)] + [(1, 0), (-1, 0), (3, 0), (-3, 0)]
    peers += [(0, d) for d in (1, 2, 3, -1, -2, -3)] + list(DIAGONALS)
    barrier = pltpu.get_barrier_semaphore()
    for dx, dy in peers:
        pl.semaphore_signal(
            barrier, inc=1,
            device_id=device(dx, dy),
            device_id_type=MESH,
        )

    lane16 = iota((16, 128), 1)
    place = ((1, 0), (0, 0), (0, 60), (1, 60))
    edge_n = [None] * 4
    edge_s = [None] * 4

    def own0(f, z):
        if f == 3:
            return source[z]
        if f == 0:
            return raw_in[0, z]
        if f == 1:
            raw_in[3, z] = mask[z].astype(F32)
        return raw_in[3, z] * raw_in[f, z]

    for f, needed in ((1, (0, 1)), (2, (2,)), (0, (3,)), (3, (4,))):
        for i in needed:
            fetched[i].wait()

        def prepare(pair, carry):
            north, south = carry
            for i in range(2):
                z = 2 * pair + i
                x = own0(f, z)
                raw0[f, z, 0:16, 0:128] = x
                a_ew[0, f * NZ + z] = x[0:2]
                a_ew[1, f * NZ + z] = x[14:16]
                if f == 1:
                    a_ew[0, 4 * NZ + pair, i:i + 1] = x[2:3]
                    a_ew[1, 4 * NZ + pair, i:i + 1] = x[13:14]
                start = place[f][1] + 3 * z
                north = jnp.where(lane16 >= start, spin(x, start + 3), north)
                south = jnp.where(lane16 >= start, spin(x, start), south)
            return north, south

        blank16 = jnp.zeros((16, 128), F32)
        edge_n[f], edge_s[f] = lax.fori_loop(0, HZ, prepare, (blank16, blank16), unroll=2)
    for pair, (f, g) in enumerate(((1, 2), (0, 3))):
        a_ns[0, pair] = jnp.where(lane16 < 60, edge_n[f], edge_n[g])
        a_ns[1, pair] = jnp.where(lane16 < 60, edge_s[f], edge_s[g])

    pl.semaphore_wait(barrier, len(peers))

    def send_edges(ew, ns, rew, rns, rd):
        made = [copy(ns.at[0, :, 8:16, :], rd.at[0], 1, 1)]
        made.append(copy(ns.at[0, :, 0:8, :], rd.at[1], -1, 1))
        made.append(copy(ns.at[1, :, 8:16, :], rd.at[2], 1, -1))
        made.append(copy(ns.at[1, :, 0:8, :], rd.at[3], -1, -1))
        made += [copy(ew.at[0], rew.at[0], -1, 0), copy(ew.at[1], rew.at[1], 1, 0)]
        made += [copy(ns.at[0], rns.at[0], 0, 1), copy(ns.at[1], rns.at[1], 0, -1)]
        return made

    has_s, has_n = my > 0, my < NTY - 1

    def merge_edges(fields, rns, rd, put_rows, put_side):
        sub = iota((8, 128), 0)
        lane = iota((24, 128), 1)
        sides = []
        for f, pair, base in fields:
            south = jnp.concatenate([rns[0, pair], jnp.where(sub < 4, rd[1, pair], rd[0, pair])], axis=0)
            north = jnp.concatenate([rns[1, pair], jnp.where(sub < 4, rd[3, pair], rd[2, pair])], axis=0)
            sides.append((jnp.where(has_s, south, 0.0), jnp.where(has_n, north, 0.0)))

        def two(half):
            for i in range(2):
                z = 2 * half + i
                for (f, pair, base), (south, north) in zip(fields, sides):
                    put_rows(f, z, half, i)
                    start = base + 3 * z
                    back = lax.rem(128 - start, 128)
                    side = jnp.where(lane < 3, spin(north, back), spin(south, 125 - start))
                    put_side(f, z, jnp.where((lane < 3) | (lane >= 125), side, 0.0))

        repeat(HZ, two)

    sent_a = send_edges(a_ew, a_ns, a_rew, a_rns, a_rd)

    def clear(z):
        for f in range(4):
            raw0[f, z, 16:24, 0:128] = jnp.zeros((8, 128), F32)

    repeat(NZ, clear, 4)

    m0 = restrict_0()

    def down_0(x):
        t1[...] = mm(x.reshape(NZ * 16, 128), m0).reshape(NZ, 16, 128)
        return t1[:, pl.ds(0, 8, stride=2), :] + t1[:, pl.ds(1, 8, stride=2), :]

    def pack_1(x, f, pk, ns, nc):
        lane = iota((8, 128), 1)

        def step(k):
            group = [x(k + 5 * j) for j in range(4)]
            for j in range(2):
                pk[f * HZ + 5 * j + k] = jnp.where(lane < 64, roll(group[j], -32, 1), roll(group[j + 2], 32, 1))
            for side, base in ((0, 64), (1, 32)):
                edge = pack_edge(group, 32, base, 4)
                ns[side, f * 5 + k] = edge
                nc[side, 0, f * 5 + k] = edge[0:4]
                nc[side, 1, f * 5 + k] = edge[4:8]

        repeat(5, step)

    def send_1(pk, ns, nc, rpk, rns, rnc):
        made = [copy(nc.at[0, 1], rnc.at[0, 1], 1, 1)]
        made.append(copy(nc.at[0, 0], rnc.at[0, 0], -1, 1))
        made.append(copy(nc.at[1, 1], rnc.at[1, 1], 1, -1))
        made.append(copy(nc.at[1, 0], rnc.at[1, 0], -1, -1))
        made += [copy(pk, rpk.at[0], -1, 0), copy(pk, rpk.at[1], 1, 0)]
        made += [copy(ns.at[0], rns.at[0], 0, 1), copy(ns.at[1], rns.at[1], 0, -1)]
        return made

    def merge_1(f, own, rpk, rns, rnc, put, first):
        lane = iota((8, 128), 1)
        blank = jnp.zeros((4, 128), F32)

        def edges(j, pieces):
            south = jnp.where(has_s, roll(pieces[0], -32 * j, 1), 0.0)
            north = jnp.where(has_n, roll(pieces[1], 96 - 32 * j, 1), 0.0)
            return south, north

        def step(k):
            at = f * 5 + k
            for j in range(4):
                z = k + 5 * j
                if first:
                    folded, shift = f * HZ + k + 5 * (j % 2), 32 if j < 2 else -32
                    south, north = edges(j, (rns[0, at], rns[1, at]))
                    put(z, 8, jnp.where(lane < 32, south, jnp.where(lane < 96, own(z), north)))
                    put(z, 16, roll(rpk[0, folded], shift, 1))
                    put(z, 0, roll(rpk[1, folded], shift, 1))
                else:
                    for i, start in ((0, 16), (1, 0)):
                        pieces = [rnc[side, i, at] for side in range(2)]
                        pieces = [jnp.concatenate([p, blank] if i == 0 else [blank, p], axis=0) for p in pieces]
                        south, north = edges(j, pieces)
                        put(z, start, jnp.where(lane < 32, south, jnp.where(lane < 96, own(z)[start:start + 8], north)))

        repeat(5, step)

    def coarsen_1(f):
        own1[f] = down_0(raw_in[f])

    repeat(4, coarsen_1)

    def weigh_1(z):
        sea = (own1[3, z] > 0.0).astype(F32)
        own1[3, z] = sea
        raw1[0, z, 8:16, :] = own1[0, z]
        for f in (1, 2):
            x = 0.25 * own1[f, z]
            own1[f, z] = x
            raw1[f, z, 8:16, :] = sea * x

    repeat(NZ, weigh_1, 4)

    m1 = restrict_1()

    def down_1(x):
        pair = jnp.concatenate([x[0:HZ], x[HZ:NZ]], axis=2).reshape(HZ * 8, 256)
        t2[...] = mm(pair, m1).reshape(HZ, 8, 128)
        return t2[:, pl.ds(0, 4, stride=2), :] + t2[:, pl.ds(1, 4, stride=2), :]

    def coarsen_2(f):
        g_p[pl.ds(f * HZ, HZ)] = down_1(own1[f])

    repeat(4, coarsen_2)

    def finish_2(k):
        for f in range(4):
            pair = []
            for z in (k, k + 5):
                x = g_p[f * HZ + z]
                x = x if f == 0 else (x > 0.0).astype(F32) if f == 3 else 0.25 * x
                g_p[f * HZ + z] = x
                pair.append(x)
            q_p[f * 5 + k] = pair[0] + roll(pair[1], 32, 1)

    repeat(5, finish_2)
    sent_q = [copy(q_p, q_rp.at[0], 0, 1), copy(q_p, q_rp.at[1], 0, -1)]

    for f in range(3):
        pack_1(lambda z: raw1[f, z, 8:16, :], f, p_pk, p_ns, p_nc)
    sent_p1 = send_1(p_pk, p_ns, p_nc, p_rpk, p_rns, p_rnc)

    def send_z(blk, slots):
        slots[3] = blk[...]
        return [copy(blk, slots.at[3 - d], 0, d) for d in (3, -3, 2, -2, 1, -1)]

    def window_row(slots, count):
        row = jnp.zeros((count, 128), F32)
        for s in range(7):
            inside = (my + (s - 3) >= 0) & (my + (s - 3) < NTY)
            row = row + jnp.where(inside, roll(slots[s], 8 * (s - 3), 1), 0.0)
        return row

    def folded_window_row(slots):
        part = iota((8, 128), 1) & 63
        out = [jnp.zeros((8, 128), F32)] * 3
        for s in range(7):
            inside = (my + (s - 3) >= 0) & (my + (s - 3) < NTY)
            block = jnp.where(inside, slots[s], 0.0)
            for i in range(3):
                pick = (part >= 24 + 8 * i) & (part < 32 + 8 * i)
                out[i] = out[i] + roll(jnp.where(pick, block, 0.0), 8 * (s - 3 - i), 1)
        return jnp.concatenate(out, axis=0)

    def send_plane(row, ev, count):
        own = pl.ds(8 * count, count)
        ev[own, :] = row
        return [
            copy(ev.at[own], ev.at[pl.ds(((8 - k) % 16) * count, count)], 2 * k, 0)
            for k in (10, 6, 9, 7, 11, 5, 2, 14, 8, 3, 13, 1, 15, 4, 12)
        ]

    def send_sibling(ev, od):
        i = counter[0]
        counter[0] += 1
        made = pltpu.make_async_remote_copy(
            src_ref=ev, dst_ref=od, send_sem=send_sem.at[i], recv_sem=recv_sem.at[i],
            device_id=(mx + 1 - 2 * lax.rem(mx, 2), my), device_id_type=MESH,
        )
        made.start()
        pending.append(made)
        return [made]

    def window_slab(ev, od, index, count, put):
        put(pl.ds(0, 16, stride=2), ev[pl.ds(index, 16, stride=count), :])
        other = od[pl.ds(index, 16, stride=count), :]
        put(pl.ds(1, 16, stride=2), jnp.where(odd, roll(other, -1, 0), other))

    arrive(sent_a)

    def put_rows(f, z, half, i):
        raw0[f, z, 16:18, 0:128] = a_rew[0, f * NZ + z]
        raw0[f, z, 22:24, 0:128] = a_rew[1, f * NZ + z]
        if f == 1:
            raw0[f, z, 18:19, 0:128] = a_rew[0, 4 * NZ + half, i:i + 1]
            raw0[f, z, 21:22, 0:128] = a_rew[1, 4 * NZ + half, i:i + 1]

    def put_side(f, z, x):
        raw0[f, z, :, 128:256] = x

    merge_edges([(f,) + place[f] for f in range(4)], a_rns, a_rd, put_rows, put_side)

    def send_2(p, rp):
        return [copy(p, rp.at[3 - d], d, 0) for d in (3, -3, 2, -2, 1, -1)]

    arrive(sent_q)
    part = iota((4, 128), 1) & 63

    def extend_2(k):
        for f in range(4):
            for j in range(2):
                south = jnp.where(has_s, roll(q_rp[0, f * 5 + k], -32 - 32 * j, 1), 0.0)
                north = jnp.where(has_n, roll(q_rp[1, f * 5 + k], 32 - 32 * j, 1), 0.0)
                at = f * HZ + 5 * j + k
                g_p[at] = jnp.where(part < 16, south, jnp.where(part < 48, g_p[at], north))

    repeat(5, extend_2)
    sent_p2 = send_2(g_p, g_rp)

    def sea0(z):
        return (raw0[1, z] > 0.0).astype(F32)

    lev0.faces(lambda z: raw0[0, z], lambda z: raw0[1, z], lambda z: raw0[2, z], sea0, UNROLL, lambda z: raw0[3, z])
    lev0.clear_ends()


    lev0.sweep(lev0.c, lev0.w, UNROLL)

    def remain0(z, u, total):
        r = raw0[3, z] - (lev0.d[z] * u - total)
        t0[z] = r[0:16, 0:128]

    lev0.stencil(lev0.w, UNROLL, remain0)
    q1[...] = down_0(t0[...])

    arrive(sent_p1)

    def put1(f):
        def put(z, start, x):
            raw1[f, z, start:start + 8, :] = x

        return put

    def sea_1(z):
        return (raw1[1, z] > 0.0).astype(F32)

    for f in range(3):
        merge_1(f, lambda z: raw1[f, z, 8:16, :], p_rpk, p_rns, p_rnc, put1(f), True)
    middle = slice(8, 16)

    def own_right(z, carry):
        here, below = carry
        s, lw, tw = sea_1(z), raw1[1, z], raw1[2, z, middle, :]
        east = 0.5 * (lw * roll(s, -1, 0) + s * roll(lw, -1, 0))
        north = 0.5 * (tw * roll(here, -1, 1) + here * roll(tw, -1, 1))
        above = jnp.where(z < NZ - 1, sea_1(jnp.minimum(z + 1, NZ - 1))[middle], 0.0)
        face_above = here * above
        faces = roll(east, 1, 0)[middle] + east[middle] + roll(north, 1, 1) + north + below + face_above
        q1[z] = OMEGA / (here * raw1[0, z, middle, :] + faces + (1.0 - here)) * q1[z]
        return above, face_above

    first = sea_1(0)[middle]
    lax.fori_loop(0, NZ, own_right, (first, jnp.zeros_like(first)), unroll=UNROLL)
    pack_1(lambda z: q1[z], 0, b_pk, b_ns, b_nc)
    sent_b = send_1(b_pk, b_ns, b_nc, b_rpk, b_rns, b_rnc)

    for f in range(3):
        merge_1(f, lambda z: raw1[f, z], None, p_rns, p_rnc, put1(f), False)
    lev1.faces(lambda z: raw1[0, z], lambda z: raw1[1, z], lambda z: raw1[2, z], sea_1, UNROLL)
    lev1.clear_ends()

    def smooth_edges(z, carry):
        north, south = carry
        x = lev0.w[z + 1, 0:16, 0:128]
        o_ew[0, z] = x[0:4]
        o_ew[1, z] = x[12:16]
        north = jnp.where(lane16 >= 3 * z, spin(x, 3 * z + 3), north)
        south = jnp.where(lane16 >= 3 * z, spin(x, 3 * z), south)
        return north, south

    edge_n, edge_s = lax.fori_loop(0, NZ, smooth_edges, (blank16, blank16), unroll=4)
    o_ns[0, 0] = edge_n
    o_ns[1, 0] = edge_s

    mall = restrict_all()

    def down_all(x):
        pair = jnp.concatenate([x[0:HZ], x[HZ:NZ]], axis=2).reshape(HZ * 16, 256)
        return jnp.sum(mm(pair, mall).reshape(HZ, 16, 128), axis=1)

    def coarsen_all(f):
        h_tmp[f] = down_all(raw_in[f])

    repeat(4, coarsen_all)
    sea4 = (h_tmp[3] > 0.0).astype(F32)
    h_blk[0:10, :] = h_tmp[0]
    h_blk[10:20, :] = sea4 * h_tmp[1] * (1.0 / 256)
    h_blk[20:30, :] = sea4 * h_tmp[2] * (1.0 / 256)
    h_blk[30:32, :] = jnp.zeros((2, 128), F32)

    arrive(sent_p2)

    def window_2(k):
        for f in range(4):
            for s in range(7):
                piece = g_p if s == 3 else g_rp.at[s]
                raw2[f, k, 4 * s:4 * s + 4, :] = piece[f * HZ + k]
            raw2[f, k, 28:32, :] = jnp.zeros((4, 128), F32)

    repeat(HZ, window_2)
    lev2.faces(lambda z: raw2[0, z], lambda z: raw2[1, z], lambda z: raw2[2, z], lambda z: raw2[3, z], UNROLL)

    m2 = restrict_2()

    def down_2(x):
        t3[...] = mm(x.reshape(HZ * 32, 128), m2).reshape(HZ, 32, 128)
        return t3[:, pl.ds(0, 16, stride=2), :] + t3[:, pl.ds(1, 16, stride=2), :]

    def coarsen_3(f):
        raw3[f] = down_2(raw2[f])

    repeat(4, coarsen_3)

    def finish_3(k):
        for f in (1, 2):
            raw3[f, k] = 0.25 * raw3[f, k]
        raw3[3, k] = (raw3[3, k] > 0.0).astype(F32)

    repeat(HZ, finish_3, 5)
    lev3.faces(lambda z: raw3[0, z], lambda z: raw3[1, z], lambda z: raw3[2, z], lambda z: raw3[3, z], UNROLL)

    arrive(sent_b)
    sent_hz = send_z(h_blk, h_z)

    def put1c(z, start, x):
        lev1.c[z + 1, start:start + 8, :] = x

    merge_1(0, lambda z: q1[z], b_rpk, b_rns, b_rnc, put1c, True)
    merge_1(0, lambda z: lev1.c[z + 1], None, b_rns, b_rnc, put1c, False)
    lev1.sweep(lev1.c, lev1.w, UNROLL)

    def remain1(z, r):
        q1[z] = r[8:16]

    lev1.remain(lev1.w, UNROLL, remain1)
    b2 = down_1(q1[...])

    f_p[...] = lev2.g[:, 12:16, :] * b2
    sent_c = send_2(f_p, f_rp)

    arrive(sent_hz)
    row_h = window_row(h_z, 32)
    arrive(sent_c)
    sent_hp = send_plane(row_h, h_ev, 32)
    sent_o = send_edges(o_ew, o_ns, o_rew, o_rns, o_rd)
    for s in range(7):
        piece = f_p if s == 3 else f_rp.at[s]
        lev2.c[1:HZ + 1, 4 * s:4 * s + 4, :] = piece[...]
    lev2.c[1:HZ + 1, 28:32, :] = jnp.zeros((HZ, 4, 128), F32)
    lev2.wrap(lev2.c)
    lev2.sweep(lev2.c, lev2.w, UNROLL)

    def remain2(z, r):
        t4[z] = r

    lev2.remain(lev2.w, UNROLL, remain2)

    lev3.c[1:HZ + 1] = lev3.g[...] * down_2(t4[...])
    lev3.wrap(lev3.c)
    lev3.sweep(lev3.c, lev3.w, UNROLL)

    def remain3(z, r):
        t3[z, 0:16, :] = r

    lev3.remain(lev3.w, UNROLL, remain3)
    m3 = restrict_3()
    t3[:, 0:16, :] = mm(t3[:, 0:16, :].reshape(HZ * 16, 128), m3).reshape(HZ, 16, 128)
    for z in range(8):
        row = t3[z, 6:7, :] + t3[z, 7:8, :] + roll(t3[z, 8:9, :] + t3[z, 9:10, :], 8, 1)
        if z < 4:
            at = 6 if z < 2 else 8
            last = t3[8 + z % 2, at:at + 1, :] + t3[8 + z % 2, at + 1:at + 2, :]
            row = row + roll(last, 16, 1)
        k_blk[z:z + 1, :] = row
    sent_kz = send_z(k_blk, k_z)

    arrive(sent_hp)
    sent_hs = send_sibling(h_ev, h_od)

    arrive(sent_kz)
    sent_kp = send_plane(folded_window_row(k_z), k_ev, 24)

    arrive(sent_hs)
    for f in range(3):
        for z in range(HZ):
            def put4(rows, x):
                raw4[f, z, rows, :] = x

            window_slab(h_ev, h_od, f * HZ + z, 32, put4)

    def sea_4(z):
        return (raw4[1, z] > 0.0).astype(F32)

    lev4.faces(lambda z: raw4[0, z], lambda z: raw4[1, z], lambda z: raw4[2, z], sea_4, UNROLL)

    arrive(sent_o)

    def put_rows0(f, z, half, i):
        lev0.w[z + 1, 16:20, 0:128] = o_rew[0, z]
        lev0.w[z + 1, 20:24, 0:128] = o_rew[1, z]

    def put_side0(f, z, x):
        lev0.w[z + 1, :, 128:256] = x

    merge_edges([(0, 0, 0)], o_rns, o_rd, put_rows0, put_side0)
    arrive(sent_kp)
    for z in range(HZ):
        for i in range(2):
            at = 8 * i + z if z < 8 else 16 + 2 * i + z - 8
            lev4.c[z + 1, pl.ds(i, 16, stride=2), :] = k_ev[pl.ds(at, 16, stride=24), :]
    for z in range(HZ):
        lev4.c[z + 1] = lev4.g[z] * lev4.c[z + 1]
    lev4.wrap(lev4.c)
    lev4.sweep(lev4.c, lev4.u, UNROLL)

    def two(step, carry):
        lev4.sweep(lev4.u, lev4.w, HZ)
        lev4.sweep(lev4.w, lev4.u, HZ)
        return carry

    lax.fori_loop(0, 6, two, 0)
    lev4.sweep(lev4.u, lev4.w, UNROLL)
    centre = slice(8, 24)
    lev4.sweep(lev4.w, lev4.u, HZ, centre)

    def two_centre(step, carry):
        lev4.sweep(lev4.u, lev4.w, HZ, centre)
        lev4.sweep(lev4.w, lev4.u, HZ, centre)
        return carry

    lax.fori_loop(0, 2, two_centre, 0)

    up = mm(lev4.u[1:HZ + 1, 13:21, :].reshape(HZ * 8, 128), prolong_3()).reshape(HZ, 8, 128)
    for start in range(2):
        t3[:, pl.ds(start, 8, stride=2), :] = up

    def add3(z):
        lev3.w[z + 1] = lev3.w[z + 1] + t3[z, 0:16, :]

    lev3.each(add3, UNROLL)
    lev3.wrap(lev3.w)
    lev3.sweep(lev3.w, lev3.u, UNROLL)
    lev3.sweep(lev3.u, lev3.w, UNROLL)

    up = mm(lev3.w[1:HZ + 1].reshape(HZ * 16, 128), prolong_2()).reshape(HZ, 16, 128)
    for start in range(2):
        t3[:, pl.ds(start, 16, stride=2), :] = up

    def add2(z):
        lev2.w[z + 1] = lev2.w[z + 1] + t3[z]

    lev2.each(add2, UNROLL)
    lev2.wrap(lev2.w)
    lev2.sweep(lev2.w, lev2.u, UNROLL)
    lev2.sweep(lev2.u, lev2.w, UNROLL)

    t3[:, 0:16, :] = lev2.w[1:HZ + 1, 8:24, :]
    up = mm(t3[:, 0:16, :].reshape(HZ * 16, 128), prolong_1()).reshape(HZ, 16, 256)
    t1[0:HZ, :, :] = up[:, :, 0:128]
    t1[HZ:NZ, :, :] = up[:, :, 128:256]

    def spread1(z):
        for start in range(2):
            raw1[0, z, pl.ds(start, 12, stride=2), :] = t1[z, 0:12, :]

    repeat(NZ, spread1, 4)

    def add1(z):
        lev1.w[z + 1] = lev1.w[z + 1] + raw1[0, z]

    lev1.each(add1, UNROLL)
    lev1.sweep(lev1.w, lev1.u, UNROLL)
    lev1.sweep(lev1.u, lev1.w, UNROLL)

    def gather0(z):
        t1[z, 0:8, :] = lev1.w[z + 1, 8:16, :]
        t1[z, 8:10, :] = lev1.w[z + 1, 16:18, :]
        t1[z, 10:12, :] = lev1.w[z + 1, 6:8, :]
        t1[z, 12:16, :] = jnp.zeros((4, 128), F32)

    repeat(NZ, gather0, 4)
    up0[...] = mm(t1[...].reshape(NZ * 16, 128), prolong_0()).reshape(NZ, 16, 256)

    def spread0(z):
        for half in range(2):
            part = up0[z, 0:12, 128 * half:128 * half + 128]
            for start in range(2):
                raw1[half, z, pl.ds(start, 12, stride=2), :] = part

    repeat(NZ, spread0, 4)

    def add0(z):
        for half in range(2):
            lanes = slice(128 * half, 128 * half + 128)
            lev0.w[z + 1, :, lanes] = lev0.w[z + 1, :, lanes] + raw1[half, z]

    lev0.each(add0, UNROLL)
    lev0.sweep(lev0.w, lev0.u, UNROLL)
    lev0.sweep(lev0.u, lev0.w, UNROLL)

    def last0(z, u, total):
        r = raw0[3, z] - (lev0.d[z] * u - total)
        sol[z] = u[0:16, 0:128]
        resid[z] = r[0:16, 0:128]

    lev0.stencil(lev0.w, UNROLL, last0)

    for made in pending:
        made.wait_send()


def level_scratch(slabs, rows, lanes):
    def vmem(count):
        return pltpu.VMEM((count, rows, lanes), F32)

    return [vmem(slabs), vmem(slabs), vmem(slabs + 1), vmem(slabs), vmem(slabs), vmem(slabs + 2), vmem(slabs + 2), vmem(slabs + 2)]


def shards(source, kappa_sq, lon_diff, lat_diff, sea_mask):
    def vmem(*shape):
        return pltpu.VMEM(shape, F32)

    scratch = [
        vmem(NZ, 16, 128), pltpu.VMEM((NZ, 16, 128), jnp.int32),
        vmem(4, NZ, 16, 128), vmem(4, NZ, 8, 128), vmem(4, HZ, 128), vmem(NZ, 16, 256), pltpu.SemaphoreType.DMA((5,)),
        vmem(4, NZ, 24, 256), vmem(8, 128), level_scratch(NZ, 24, 256),
        vmem(3, NZ, 24, 128), level_scratch(NZ, 24, 128),
        vmem(4, HZ, 32, 128), level_scratch(HZ, 32, 128),
        vmem(4, HZ, 16, 128), level_scratch(HZ, 16, 128),
        vmem(3, HZ, 32, 128), level_scratch(HZ, 32, 128),
        vmem(NZ, 16, 128), vmem(NZ, 16, 128), vmem(HZ, 8, 128), vmem(HZ, 32, 128), vmem(HZ, 32, 128), vmem(NZ, 8, 128),
        vmem(2, 4 * NZ + HZ, 2, 128), vmem(2, 2, 16, 128), vmem(2, 4 * NZ + HZ, 2, 128), vmem(2, 2, 16, 128), vmem(4, 2, 8, 128),
        vmem(HZ, 8, 128), vmem(2, 5, 8, 128), vmem(2, 2, 5, 4, 128),
        vmem(2, HZ, 8, 128), vmem(2, 5, 8, 128), vmem(2, 2, 5, 4, 128),
        vmem(HZ, 4, 128), vmem(7, HZ, 4, 128),
        vmem(8, 128), vmem(7, 8, 128), vmem(16 * 24, 128),
        vmem(3 * HZ, 8, 128), vmem(2, 15, 8, 128), vmem(2, 2, 15, 4, 128),
        vmem(2, 3 * HZ, 8, 128), vmem(2, 15, 8, 128), vmem(2, 2, 15, 4, 128),
        vmem(20, 4, 128), vmem(2, 20, 4, 128),
        vmem(4 * HZ, 4, 128), vmem(7, 4 * HZ, 4, 128),
        vmem(32, 128), vmem(7, 32, 128), vmem(16 * 32, 128), vmem(16 * 32, 128),
        vmem(2, NZ, 4, 128), vmem(2, 1, 16, 128), vmem(2, NZ, 4, 128), vmem(2, 1, 16, 128), vmem(4, 1, 8, 128),
        pltpu.SemaphoreType.DMA((96,)), pltpu.SemaphoreType.DMA((96,)),
    ]
    shape = jax.ShapeDtypeStruct(source.shape, F32)
    anywhere = pl.BlockSpec(memory_space=pl.ANY)
    return pl.pallas_call(
        body,
        out_shape=(shape, shape),
        in_specs=[anywhere] * 5,
        out_specs=[pl.BlockSpec(memory_space=pltpu.VMEM)] * 2,
        scratch_shapes=scratch,
        compiler_params=pltpu.CompilerParams(
            collective_id=0, has_side_effects=True, vmem_limit_bytes=54848 * 1024
        ),
    )(source, kappa_sq, lon_diff, lat_diff, sea_mask)

def solution(mesh):
    spec = P(None, "tx", "ty")
    return jax.shard_map(
        shards, mesh=mesh, in_specs=(spec,) * 5, out_specs=(spec, spec), check_vma=False
    )
```

```python
import jax
import jax.numpy as jnp
from jax import lax
from jax.experimental import pallas as pl
from jax.experimental.pallas import tpu as pltpu
from jax.sharding import PartitionSpec as P

NZ = 20
HZ = 10
QZ = 5
NTX = 32
NTY = 16
OMEGA = 0.8
UNROLL = 20
MESH = pl.DeviceIdType.MESH
F32 = jnp.float32

DIAGONALS = ((1, 1), (-1, 1), (1, -1), (-1, -1))


def iota(shape, dim):
    return lax.broadcasted_iota(jnp.int32, shape, dim)


def mm(x, m):
    high = x.astype(jnp.bfloat16)
    low = (x - high.astype(F32)).astype(jnp.bfloat16)
    m = m.astype(jnp.bfloat16)
    return lax.dot_general(
        jnp.concatenate([high, low], axis=1), jnp.concatenate([m, m], axis=0),
        (((1,), (0,)), ((), ())), preferred_element_type=F32,
    )


def roll(x, shift, axis):
    shift = shift % x.shape[axis]
    return x if shift == 0 else pltpu.roll(x, shift, axis)


def one_hot(shape, hit, value=1.0):
    row, col = iota(shape, 0), iota(shape, 1)
    return jnp.where(hit(row, col), F32(value), F32(0.0))


def restrict_0():
    return one_hot((128, 128), lambda n, m: m == 32 + (n >> 1), 0.25)


def restrict_1():
    return one_hot((256, 128), lambda n, m: m == n >> 1, 0.25)


def restrict_2():
    return one_hot((128, 128), lambda n, m: m == (n & 64) + 8 + ((n & 63) >> 1), 0.25)


def restrict_3():
    def hit(n, m):
        q = n & 63
        return (m == (n & 64) + 16 + (q >> 1)) & (q >= 16) & (q < 32)

    return one_hot((128, 128), hit, 0.25)


def restrict_all():
    return one_hot((256, 128), lambda n, m: m == ((n & 128) >> 1) + 24 + ((n & 127) >> 4), 1.0 / 256)


def prolong_3():
    def hit(m, n):
        q = n & 63
        return (m == (n & 64) + ((n & 128) >> 2) + 4 + (q >> 1)) & (q < 56)

    return one_hot((128, 256), hit)


def prolong_2():
    return one_hot((128, 128), lambda m, n: m == (n & 64) + 8 + ((n & 63) >> 1))


def prolong_1():
    return one_hot((128, 256), lambda m, n: m == n >> 1)


def prolong_0():
    def hit(m, n):
        rel = jnp.where(n >= 192, n - 256, n)
        return (m == 32 + (rel >> 1)) & (rel < 132) & (rel >= -4)

    return one_hot((128, 256), hit)


class Level:
    def __init__(self, slabs, seam, refs):
        self.slabs = slabs
        self.seam = seam
        self.e, self.n, self.v, self.g, self.d, self.c, self.u, self.w = refs

    def each(self, body, unroll):
        def step(z, carry):
            body(z)
            return carry

        lax.fori_loop(0, self.slabs, step, 0, unroll=min(unroll, self.slabs))

    def wrap(self, ref, rows=slice(None)):
        if self.seam:
            ref[0, rows] = roll(ref[self.slabs, rows], self.seam, 1)
            ref[self.slabs + 1, rows] = roll(ref[1, rows], -self.seam, 1)

    def clear_ends(self):
        if not self.seam:
            for ref in (self.c, self.u, self.w):
                ref[0] = jnp.zeros_like(ref[0])
                ref[self.slabs + 1] = jnp.zeros_like(ref[0])

    def faces(self, kap, lond, latd, sea, unroll, right=None):
        top = self.slabs - 1
        first = sea(0)
        if self.seam:
            low = iota(self.v.shape[1:], 1) < 64
            face_top = jnp.where(low, sea(top) * roll(first, 64, 1), 0.0)
            face_first = roll(face_top, 64, 1)
        else:
            face_top = face_first = jnp.zeros_like(first)
        self.v[0] = face_first

        def slab(z, s, face_below, face_above):
            lw = s * lond(z)
            tw = s * latd(z)
            east = 0.5 * (lw * roll(s, -1, 0) + s * roll(lw, -1, 0))
            north = 0.5 * (tw * roll(s, -1, 1) + s * roll(tw, -1, 1))
            west = roll(east, 1, 0)
            south = roll(north, 1, 1)
            diag = s * kap(z) + (west + east + south + north + face_below + face_above) + (1.0 - s)
            scale = OMEGA / diag
            self.v[z + 1] = face_above
            self.e[z] = east
            self.n[z] = north
            self.d[z] = diag
            self.g[z] = scale
            if right is not None:
                self.c[z + 1] = scale * right(z)

        def step(z, carry):
            s, face_below = carry
            s_above = sea(z + 1)
            face_above = s * s_above
            slab(z, s, face_below, face_above)
            return s_above, face_above

        s, face_below = lax.fori_loop(0, top, step, (first, face_first), unroll=min(unroll, top))
        slab(top, s, face_below, face_top)

    def stencil(self, src, unroll, use, rows=slice(None), first=0):
        def step(z, carry):
            below, u, face_below = carry
            above = src[z + 2, rows]
            face_above = self.v[z + 1, rows]
            e = self.e[z, rows]
            n = self.n[z, rows]
            use(z, u, (
                roll(e * u, 1, 0)
                + e * roll(u, -1, 0)
                + roll(n * u, 1, 1)
                + n * roll(u, -1, 1)
                + face_below * below
                + face_above * above
            ))
            return u, above, face_above

        def start(z):
            return src[z, rows], src[z + 1, rows], self.v[z, rows]

        if self.seam:
            for i in range(self.slabs):
                z = (first + i) % self.slabs
                carry = step(z, start(z) if i == 0 or z == 0 else carry)
        else:
            lax.fori_loop(0, self.slabs, step, start(0), unroll=min(unroll, self.slabs))

    def sweep(self, src, dst, unroll, rows=slice(None), first=0):
        def use(z, u, total):
            new = (1.0 - OMEGA) * u + self.c[z + 1, rows] + self.g[z, rows] * total
            dst[z + 1, rows] = new
            if self.seam and z == 0:
                dst[self.slabs + 1, rows] = roll(new, -self.seam, 1)
            if self.seam and z == self.slabs - 1:
                dst[0, rows] = roll(new, self.seam, 1)

        self.stencil(src, unroll, use, rows, first)

    def remain(self, src, unroll, put, first=0):
        def use(z, u, total):
            put(z, self.d[z] * (1.25 * self.c[z + 1] - u) + total)

        self.stencil(src, unroll, use, first=first)


def pack_edge(slabs, width, base, count):
    lane = iota(slabs[0].shape, 1)
    out = roll(slabs[0], -base, 1)
    for i in range(1, count):
        out = jnp.where(lane >= width * i, roll(slabs[i], width * i - base, 1), out)
    return out


def body(
    source_in, kappa_in, lon_in, lat_in, mask_in,
    sol, resid,
    source, kappa, lon_diff, lat_diff, mask, in_sem,
    raw0, src0, l0, raw1, l1, raw2, l2, raw3, l3, raw4, l4, l5, t0, t1, t2, t3, t4, q1,
    a_ew, a_ns, a_rew, a_rns, a_rd,
    b_pk, b_ns, b_nc, b_rpk, b_rns, b_rnc,
    f_p, f_rp,
    k_blk, k_z, k_ev,
    p_pk, p_ns, p_nc, p_rpk, p_rns, p_rnc, q_p, q_rp, g_p, g_rp, h_blk, h_z, h_ev, h_od,
    o_ew, o_ns, o_rew, o_rns, o_rd,
    send_sem, recv_sem,
):
    mx, my = lax.axis_index("tx"), lax.axis_index("ty")
    odd = lax.rem(mx, 2) == 1
    counter = [0]
    pending = []
    places = {}

    def shifted(axis, here, shift, count):
        shift = shift % count
        if (axis, shift) not in places:
            there = here + shift
            places[axis, shift] = jnp.where(there >= count, there - count, there) if shift else here
        return places[axis, shift]

    def device(dx, dy):
        return (shifted(0, mx, dx, NTX), shifted(1, my, dy, NTY))

    def copy(src, dst, dx, dy):
        i = counter[0]
        counter[0] += 1
        made = pltpu.make_async_remote_copy(
            src_ref=src, dst_ref=dst, send_sem=send_sem.at[i], recv_sem=recv_sem.at[i],
            device_id=device(dx, dy),
            device_id_type=MESH,
        )
        made.start()
        pending.append(made)
        return made

    def arrive(copies):
        for made in copies:
            made.wait_recv()

    lev0 = Level(NZ, 0, l0)
    lev1 = Level(NZ, 0, l1)
    lev2 = Level(HZ, 64, l2)
    lev3 = Level(HZ, 64, l3)
    lev4 = Level(HZ, 64, l4)
    lev5 = Level(QZ, 32, l5)

    fetched = [
        pltpu.make_async_copy(src, dst, in_sem.at[i])
        for i, (src, dst) in enumerate((
            (mask_in, mask), (lon_in, lon_diff), (lat_in, lat_diff), (kappa_in, kappa), (source_in, source)
        ))
    ]
    for made in fetched:
        made.start()

    peers = [(2 * k, 0) for k in range(1, 16)] + [(1, 0), (-1, 0), (3, 0), (-3, 0)]
    peers += [(0, d) for d in (1, 2, 3, -1, -2, -3)] + list(DIAGONALS)
    barrier = pltpu.get_barrier_semaphore()
    for dx, dy in peers:
        pl.semaphore_signal(
            barrier, inc=1,
            device_id=device(dx, dy),
            device_id_type=MESH,
        )

    lane16 = iota((16, 128), 1)
    place = ((1, 0), (0, 0), (0, 60), (1, 60))
    edge_n = [jnp.zeros((16, 128), F32)] * 4
    edge_s = [jnp.zeros((16, 128), F32)] * 4
    own0 = (
        lambda z: kappa[z],
        lambda z: mask[z].astype(F32) * lon_diff[z],
        lambda z: mask[z].astype(F32) * lat_diff[z],
        lambda z: source[z],
    )
    for f, needed in ((1, (0, 1)), (2, (2,)), (0, (3,)), (3, (4,))):
        for i in needed:
            fetched[i].wait()
        for z in range(NZ):
            x = own0[f](z)
            raw0[f, z, 0:16, 0:128] = x
            a_ew[0, f * NZ + z] = x[0:2]
            a_ew[1, f * NZ + z] = x[14:16]
            if f == 1:
                a_ew[0, 4 * NZ + z // 2, z % 2:z % 2 + 1] = x[2:3]
                a_ew[1, 4 * NZ + z // 2, z % 2:z % 2 + 1] = x[13:14]
            start = place[f][1] + 3 * z
            edge_n[f] = jnp.where(lane16 >= start, roll(x, start - 125, 1), edge_n[f])
            edge_s[f] = jnp.where(lane16 >= start, roll(x, start, 1), edge_s[f])
    for pair, (f, g) in enumerate(((1, 2), (0, 3))):
        a_ns[0, pair] = jnp.where(lane16 < 60, edge_n[f], edge_n[g])
        a_ns[1, pair] = jnp.where(lane16 < 60, edge_s[f], edge_s[g])

    pl.semaphore_wait(barrier, len(peers))

    def send_edges(ew, ns, rew, rns, rd):
        made = [copy(ns.at[0, :, 8:16, :], rd.at[0], 1, 1)]
        made.append(copy(ns.at[0, :, 0:8, :], rd.at[1], -1, 1))
        made.append(copy(ns.at[1, :, 8:16, :], rd.at[2], 1, -1))
        made.append(copy(ns.at[1, :, 0:8, :], rd.at[3], -1, -1))
        made += [copy(ew.at[0], rew.at[0], -1, 0), copy(ew.at[1], rew.at[1], 1, 0)]
        made += [copy(ns.at[0], rns.at[0], 0, 1), copy(ns.at[1], rns.at[1], 0, -1)]
        return made

    has_s, has_n = my > 0, my < NTY - 1

    def merge_edges(f, base, rns, rd, put_rows, put_side):
        sub = iota((8, 128), 0)
        south = jnp.concatenate([rns[0, f], jnp.where(sub < 4, rd[1, f], rd[0, f])], axis=0)
        north = jnp.concatenate([rns[1, f], jnp.where(sub < 4, rd[3, f], rd[2, f])], axis=0)
        lane = iota((24, 128), 1)
        south = jnp.where(has_s, south, 0.0)
        north = jnp.where(has_n, north, 0.0)
        for z in range(NZ):
            put_rows(z)
            start = base + 3 * z
            side = jnp.where(lane < 3, roll(north, -start, 1), roll(south, 125 - start, 1))
            put_side(z, jnp.where((lane < 3) | (lane >= 125), side, 0.0))

    sent_a = send_edges(a_ew, a_ns, a_rew, a_rns, a_rd)
    for f in range(4):
        for z in range(NZ):
            raw0[f, z, 16:24, 0:128] = jnp.zeros((8, 128), F32)

    m0 = restrict_0()

    def down_0(x):
        t1[...] = mm(x.reshape(NZ * 16, 128), m0).reshape(NZ, 16, 128)
        return t1[:, pl.ds(0, 8, stride=2), :] + t1[:, pl.ds(1, 8, stride=2), :]

    def pack_1(x, f, pk, ns, nc):
        lane = iota((8, 128), 1)
        for k in range(HZ):
            pk[f * HZ + k] = jnp.where(lane < 64, roll(x[k], -32, 1), roll(x[k + HZ], 32, 1))
        for k in range(5):
            group = [x[k + 5 * j] for j in range(4)]
            for side, base in ((0, 64), (1, 32)):
                edge = pack_edge(group, 32, base, 4)
                ns[side, f * 5 + k] = edge
                nc[side, 0, f * 5 + k] = edge[0:4]
                nc[side, 1, f * 5 + k] = edge[4:8]

    def send_1(pk, ns, nc, rpk, rns, rnc):
        made = [copy(nc.at[0, 1], rnc.at[0, 1], 1, 1)]
        made.append(copy(nc.at[0, 0], rnc.at[0, 0], -1, 1))
        made.append(copy(nc.at[1, 1], rnc.at[1, 1], 1, -1))
        made.append(copy(nc.at[1, 0], rnc.at[1, 0], -1, -1))
        made += [copy(pk, rpk.at[0], -1, 0), copy(pk, rpk.at[1], 1, 0)]
        made += [copy(ns.at[0], rns.at[0], 0, 1), copy(ns.at[1], rns.at[1], 0, -1)]
        return made

    def merge_1(f, own, rpk, rns, rnc, put, first):
        lane = iota((8, 128), 1)
        blank = jnp.zeros((4, 128), F32)

        def edges(z, pieces):
            south = jnp.where(has_s, roll(pieces[0], -32 * (z // 5), 1), 0.0)
            north = jnp.where(has_n, roll(pieces[1], 96 - 32 * (z // 5), 1), 0.0)
            return south, north

        for z in range(NZ):
            at = f * 5 + z % 5
            if first:
                k, shift = (z, 32) if z < HZ else (z - HZ, -32)
                south, north = edges(z, (rns[0, at], rns[1, at]))
                put(z, 8, jnp.where(lane < 32, south, jnp.where(lane < 96, own(z), north)))
                put(z, 16, roll(rpk[0, f * HZ + k], shift, 1))
                put(z, 0, roll(rpk[1, f * HZ + k], shift, 1))
            else:
                for i, start in ((0, 16), (1, 0)):
                    pieces = [rnc[side, i, at] for side in range(2)]
                    pieces = [jnp.concatenate([p, blank] if i == 0 else [blank, p], axis=0) for p in pieces]
                    south, north = edges(z, pieces)
                    put(z, start, jnp.where(lane < 32, south, jnp.where(lane < 96, own(z)[start:start + 8], north)))

    own1 = [
        down_0(kappa[...]),
        0.25 * down_0(lon_diff[...]),
        0.25 * down_0(lat_diff[...]),
        (down_0(mask[...].astype(F32)) > 0.0).astype(F32),
    ]

    m1 = restrict_1()

    def down_1(x):
        pair = jnp.concatenate([x[0:HZ], x[HZ:NZ]], axis=2).reshape(HZ * 8, 256)
        t2[...] = mm(pair, m1).reshape(HZ, 8, 128)
        return t2[:, pl.ds(0, 4, stride=2), :] + t2[:, pl.ds(1, 4, stride=2), :]

    own2 = [
        down_1(own1[0]),
        0.25 * down_1(own1[1]),
        0.25 * down_1(own1[2]),
        (down_1(own1[3]) > 0.0).astype(F32),
    ]
    for f in range(4):
        g_p[f * HZ:(f + 1) * HZ] = own2[f]
        for k in range(5):
            q_p[f * 5 + k] = own2[f][k] + roll(own2[f][k + 5], 32, 1)
    sent_q = [copy(q_p, q_rp.at[0], 0, 1), copy(q_p, q_rp.at[1], 0, -1)]

    for f, x in enumerate((own1[0], own1[3] * own1[1], own1[3] * own1[2])):
        pack_1(x, f, p_pk, p_ns, p_nc)
        raw1[f, :, 8:16, :] = x
    sent_p1 = send_1(p_pk, p_ns, p_nc, p_rpk, p_rns, p_rnc)

    def send_z(blk, slots):
        slots[3] = blk[...]
        return [copy(blk, slots.at[3 - d], 0, d) for d in (3, -3, 2, -2, 1, -1)]

    def window_row(slots, count):
        row = jnp.zeros((count, 128), F32)
        for s in range(7):
            inside = (my + (s - 3) >= 0) & (my + (s - 3) < NTY)
            row = row + jnp.where(inside, roll(slots[s], 8 * (s - 3), 1), 0.0)
        return row

    def folded_window_row(slots):
        part = iota((8, 128), 1) & 63
        out = [jnp.zeros((8, 128), F32)] * 3
        for s in range(7):
            inside = (my + (s - 3) >= 0) & (my + (s - 3) < NTY)
            block = jnp.where(inside, slots[s], 0.0)
            for i in range(3):
                pick = (part >= 24 + 8 * i) & (part < 32 + 8 * i)
                out[i] = out[i] + roll(jnp.where(pick, block, 0.0), 8 * (s - 3 - i), 1)
        return jnp.concatenate(out, axis=0)

    def send_plane(row, ev, count):
        own = pl.ds(8 * count, count)
        ev[own, :] = row
        return [
            copy(ev.at[own], ev.at[pl.ds(((8 - k) % 16) * count, count)], 2 * k, 0)
            for k in (10, 6, 9, 7, 11, 5, 2, 14, 8, 3, 13, 1, 15, 4, 12)
        ]

    def send_sibling(ev, od):
        i = counter[0]
        counter[0] += 1
        made = pltpu.make_async_remote_copy(
            src_ref=ev, dst_ref=od, send_sem=send_sem.at[i], recv_sem=recv_sem.at[i],
            device_id=(mx + 1 - 2 * lax.rem(mx, 2), my), device_id_type=MESH,
        )
        made.start()
        pending.append(made)
        return [made]

    def window_slab(ev, od, index, count, put):
        put(pl.ds(0, 16, stride=2), ev[pl.ds(index, 16, stride=count), :])
        other = od[pl.ds(index, 16, stride=count), :]
        put(pl.ds(1, 16, stride=2), jnp.where(odd, roll(other, -1, 0), other))

    arrive(sent_a)
    for f in range(4):
        def put_rows(z):
            raw0[f, z, 16:18, 0:128] = a_rew[0, f * NZ + z]
            raw0[f, z, 22:24, 0:128] = a_rew[1, f * NZ + z]
            if f == 1:
                pick = slice(z % 2, z % 2 + 1)
                raw0[f, z, 18:19, 0:128] = a_rew[0, 4 * NZ + z // 2, pick]
                raw0[f, z, 21:22, 0:128] = a_rew[1, 4 * NZ + z // 2, pick]

        def put_side(z, x):
            raw0[f, z, :, 128:256] = x

        merge_edges(place[f][0], place[f][1], a_rns, a_rd, put_rows, put_side)

    def send_2(p, rp):
        return [copy(p, rp.at[3 - d], d, 0) for d in (3, -3, 2, -2, 1, -1)]

    arrive(sent_q)
    part = iota((4, 128), 1) & 63
    for f in range(4):
        for k in range(HZ):
            south = roll(q_rp[0, f * 5 + k % 5], -32 if k < 5 else -64, 1)
            north = roll(q_rp[1, f * 5 + k % 5], 32 if k < 5 else 0, 1)
            south = jnp.where(has_s, south, 0.0)
            north = jnp.where(has_n, north, 0.0)
            g_p[f * HZ + k] = jnp.where(part < 16, south, jnp.where(part < 48, g_p[f * HZ + k], north))
    sent_p2 = send_2(g_p, g_rp)

    def sea0(z):
        return (raw0[1, z] > 0.0).astype(F32)

    lev0.faces(lambda z: raw0[0, z], lambda z: raw0[1, z], lambda z: raw0[2, z], sea0, UNROLL, lambda z: raw0[3, z])
    lev0.clear_ends()


    lev0.sweep(lev0.c, lev0.w, UNROLL)

    def remain0(z, u, total):
        r = raw0[3, z] - (lev0.d[z] * u - total)
        t0[z] = r[0:16, 0:128]

    lev0.stencil(lev0.w, UNROLL, remain0)
    b1 = down_0(t0[...])

    arrive(sent_p1)

    def put1(f):
        def put(z, start, x):
            raw1[f, z, start:start + 8, :] = x

        return put

    def sea_1(z):
        return (raw1[1, z] > 0.0).astype(F32)

    for f in range(3):
        merge_1(f, lambda z: raw1[f, z, 8:16, :], p_rpk, p_rns, p_rnc, put1(f), True)
    middle = slice(8, 16)
    c1 = []
    for z in range(NZ):
        s, lw, tw = sea_1(z), raw1[1, z], raw1[2, z, middle, :]
        here = s[middle]
        east = 0.5 * (lw * roll(s, -1, 0) + s * roll(lw, -1, 0))
        north = 0.5 * (tw * roll(here, -1, 1) + here * roll(tw, -1, 1))
        faces = roll(east, 1, 0)[middle] + east[middle] + roll(north, 1, 1) + north
        for other in (z - 1, z + 1):
            if 0 <= other < NZ:
                faces = faces + here * sea_1(other)[middle]
        c1.append(OMEGA / (here * raw1[0, z, middle, :] + faces + (1.0 - here)) * b1[z])
    c1 = jnp.stack(c1)
    q1[...] = c1
    pack_1(c1, 0, b_pk, b_ns, b_nc)
    sent_b = send_1(b_pk, b_ns, b_nc, b_rpk, b_rns, b_rnc)

    for f in range(3):
        merge_1(f, lambda z: raw1[f, z], None, p_rns, p_rnc, put1(f), False)
    lev1.faces(lambda z: raw1[0, z], lambda z: raw1[1, z], lambda z: raw1[2, z], sea_1, UNROLL)
    lev1.clear_ends()

    edge_n = jnp.zeros((16, 128), F32)
    edge_s = jnp.zeros((16, 128), F32)
    for z in range(NZ):
        x = lev0.w[z + 1, 0:16, 0:128]
        o_ew[0, z] = x[0:4]
        o_ew[1, z] = x[12:16]
        edge_n = jnp.where(lane16 >= 3 * z, roll(x, 3 * z - 125, 1), edge_n)
        edge_s = jnp.where(lane16 >= 3 * z, roll(x, 3 * z, 1), edge_s)
    o_ns[0, 0] = edge_n
    o_ns[1, 0] = edge_s

    mall = restrict_all()

    def down_all(x):
        pair = jnp.concatenate([x[0:HZ], x[HZ:NZ]], axis=2).reshape(HZ * 16, 256)
        return jnp.sum(mm(pair, mall).reshape(HZ, 16, 128), axis=1)

    sea4 = (down_all(mask[...].astype(F32)) > 0.0).astype(F32)
    h_blk[0:10, :] = down_all(kappa[...])
    h_blk[10:20, :] = sea4 * (down_all(lon_diff[...]) * (1.0 / 256))
    h_blk[20:30, :] = sea4 * (down_all(lat_diff[...]) * (1.0 / 256))
    h_blk[30:32, :] = jnp.zeros((2, 128), F32)

    arrive(sent_p2)
    for f in range(4):
        for s in range(7):
            piece = g_p if s == 3 else g_rp.at[s]
            raw2[f, :, 4 * s:4 * s + 4, :] = piece[f * HZ:(f + 1) * HZ]
        raw2[f, :, 28:32, :] = jnp.zeros((HZ, 4, 128), F32)
    lev2.faces(lambda z: raw2[0, z], lambda z: raw2[1, z], lambda z: raw2[2, z], lambda z: raw2[3, z], UNROLL)

    m2 = restrict_2()

    def down_2(x):
        t3[...] = mm(x.reshape(HZ * 32, 128), m2).reshape(HZ, 32, 128)
        return t3[:, pl.ds(0, 16, stride=2), :] + t3[:, pl.ds(1, 16, stride=2), :]

    raw3[0] = down_2(raw2[0])
    raw3[1] = 0.25 * down_2(raw2[1])
    raw3[2] = 0.25 * down_2(raw2[2])
    raw3[3] = (down_2(raw2[3]) > 0.0).astype(F32)
    lev3.faces(lambda z: raw3[0, z], lambda z: raw3[1, z], lambda z: raw3[2, z], lambda z: raw3[3, z], UNROLL)

    arrive(sent_b)
    sent_hz = send_z(h_blk, h_z)

    def put1c(z, start, x):
        lev1.c[z + 1, start:start + 8, :] = x

    merge_1(0, lambda z: q1[z], b_rpk, b_rns, b_rnc, put1c, True)
    merge_1(0, lambda z: lev1.c[z + 1], None, b_rns, b_rnc, put1c, False)
    lev1.sweep(lev1.c, lev1.w, UNROLL)

    def remain1(z, r):
        q1[z] = r[8:16]

    lev1.remain(lev1.w, UNROLL, remain1)
    b2 = down_1(q1[...])

    f_p[...] = lev2.g[:, 12:16, :] * b2
    sent_c = send_2(f_p, f_rp)

    arrive(sent_hz)
    row_h = window_row(h_z, 32)
    arrive(sent_c)
    sent_hp = send_plane(row_h, h_ev, 32)
    sent_o = send_edges(o_ew, o_ns, o_rew, o_rns, o_rd)
    for s in range(7):
        piece = f_p if s == 3 else f_rp.at[s]
        lev2.c[1:HZ + 1, 4 * s:4 * s + 4, :] = piece[...]
    lev2.c[1:HZ + 1, 28:32, :] = jnp.zeros((HZ, 4, 128), F32)
    lev2.wrap(lev2.c)
    lev2.sweep(lev2.c, lev2.w, UNROLL, first=1)

    def remain2(z, r):
        t4[z] = r

    lev2.remain(lev2.w, UNROLL, remain2, 2)

    lev3.c[1:HZ + 1] = lev3.g[...] * down_2(t4[...])
    lev3.wrap(lev3.c)
    lev3.sweep(lev3.c, lev3.w, UNROLL, first=1)

    def remain3(z, r):
        t3[z, 0:16, :] = r

    lev3.remain(lev3.w, UNROLL, remain3, 2)
    m3 = restrict_3()
    t3[:, 0:16, :] = mm(t3[:, 0:16, :].reshape(HZ * 16, 128), m3).reshape(HZ, 16, 128)
    for z in range(8):
        row = t3[z, 6:7, :] + t3[z, 7:8, :] + roll(t3[z, 8:9, :] + t3[z, 9:10, :], 8, 1)
        if z < 4:
            at = 6 if z < 2 else 8
            last = t3[8 + z % 2, at:at + 1, :] + t3[8 + z % 2, at + 1:at + 2, :]
            row = row + roll(last, 16, 1)
        k_blk[z:z + 1, :] = row
    sent_kz = send_z(k_blk, k_z)

    arrive(sent_hp)
    sent_hs = send_sibling(h_ev, h_od)

    arrive(sent_kz)
    sent_kp = send_plane(folded_window_row(k_z), k_ev, 24)

    arrive(sent_hs)
    for f in range(3):
        for z in range(HZ):
            def put4(rows, x):
                raw4[f, z, rows, :] = x

            window_slab(h_ev, h_od, f * HZ + z, 32, put4)

    def sea_4(z):
        return (raw4[1, z] > 0.0).astype(F32)

    lev4.faces(lambda z: raw4[0, z], lambda z: raw4[1, z], lambda z: raw4[2, z], sea_4, UNROLL)
    group = iota((32, 128), 1) & 32

    def fold(lower, upper):
        return jnp.where(group == 0, roll(lower, -12, 1), roll(upper, 20, 1))

    for k in range(QZ):
        lev5.e[k] = fold(lev4.e[k], lev4.e[k + QZ])
        lev5.n[k] = fold(lev4.n[k], lev4.n[k + QZ])
        lev5.g[k] = fold(lev4.g[k], lev4.g[k + QZ])
        lev5.v[k + 1] = fold(lev4.v[k + 1], lev4.v[k + QZ + 1])
    lev5.v[0] = roll(lev5.v[QZ], 32, 1)

    arrive(sent_o)

    def put_rows0(z):
        lev0.w[z + 1, 16:20, 0:128] = o_rew[0, z]
        lev0.w[z + 1, 20:24, 0:128] = o_rew[1, z]

    def put_side0(z, x):
        lev0.w[z + 1, :, 128:256] = x

    merge_edges(0, 0, o_rns, o_rd, put_rows0, put_side0)
    arrive(sent_kp)
    for z in range(HZ):
        for i in range(2):
            at = 8 * i + z if z < 8 else 16 + 2 * i + z - 8
            lev4.c[z + 1, pl.ds(i, 16, stride=2), :] = k_ev[pl.ds(at, 16, stride=24), :]
    for z in range(HZ):
        lev4.c[z + 1] = lev4.g[z] * lev4.c[z + 1]
    lev4.wrap(lev4.c)
    for k in range(QZ):
        lev5.c[k + 1] = fold(lev4.c[k + 1], lev4.c[k + QZ + 1])
    lev4.sweep(lev4.c, lev4.w, HZ, first=1)

    def four(step, carry):
        for i in range(2):
            lev4.sweep(lev4.w, lev4.u, HZ, first=2 + 2 * i)
            lev4.sweep(lev4.u, lev4.w, HZ, first=3 + 2 * i)
        return carry

    lax.fori_loop(0, 2, four, 0)
    for k in range(QZ):
        lev5.u[k + 1] = fold(lev4.w[k + 1], lev4.w[k + QZ + 1])
    lev5.wrap(lev5.u)
    for i in range(10):
        src, dst = (lev5.u, lev5.w) if i % 2 == 0 else (lev5.w, lev5.u)
        lev5.sweep(src, dst, QZ, slice(None) if i < 5 else slice(8, 24), first=(i + 1) % QZ)

    up = mm(lev5.u[1:QZ + 1, 13:21, :].reshape(QZ * 8, 128), prolong_3()).reshape(QZ, 8, 256)
    for start in range(2):
        t3[0:QZ, pl.ds(start, 8, stride=2), :] = up[:, :, 0:128]
        t3[QZ:HZ, pl.ds(start, 8, stride=2), :] = up[:, :, 128:256]

    def add3(z):
        lev3.w[z + 1] = lev3.w[z + 1] + t3[z, 0:16, :]

    lev3.each(add3, UNROLL)
    lev3.wrap(lev3.w)
    lev3.sweep(lev3.w, lev3.u, UNROLL, first=1)
    lev3.sweep(lev3.u, lev3.w, UNROLL, first=2)

    up = mm(lev3.w[1:HZ + 1].reshape(HZ * 16, 128), prolong_2()).reshape(HZ, 16, 128)
    for start in range(2):
        t3[:, pl.ds(start, 16, stride=2), :] = up

    def add2(z):
        lev2.w[z + 1] = lev2.w[z + 1] + t3[z]

    lev2.each(add2, UNROLL)
    lev2.wrap(lev2.w)
    lev2.sweep(lev2.w, lev2.u, UNROLL, first=1)
    lev2.sweep(lev2.u, lev2.w, UNROLL, first=2)

    t3[:, 0:16, :] = lev2.w[1:HZ + 1, 8:24, :]
    up = mm(t3[:, 0:16, :].reshape(HZ * 16, 128), prolong_1()).reshape(HZ, 16, 256)
    for start in range(2):
        t1[0:HZ, :, :] = up[:, :, 0:128]
        t1[HZ:NZ, :, :] = up[:, :, 128:256]
    for z in range(NZ):
        for start in range(2):
            q = pl.ds(start, 12, stride=2)
            raw1[0, z, q, :] = t1[z, 0:12, :]

    def add1(z):
        lev1.w[z + 1] = lev1.w[z + 1] + raw1[0, z]

    lev1.each(add1, UNROLL)
    lev1.sweep(lev1.w, lev1.u, UNROLL)
    lev1.sweep(lev1.u, lev1.w, UNROLL)

    for z in range(NZ):
        t1[z, 0:8, :] = lev1.w[z + 1, 8:16, :]
        t1[z, 8:10, :] = lev1.w[z + 1, 16:18, :]
        t1[z, 10:12, :] = lev1.w[z + 1, 6:8, :]
        t1[z, 12:16, :] = jnp.zeros((4, 128), F32)
    up = mm(t1[...].reshape(NZ * 16, 128), prolong_0()).reshape(NZ, 16, 256)
    for z in range(NZ):
        for half in range(2):
            part = up[z, 0:12, 128 * half:128 * half + 128]
            for start in range(2):
                raw1[half, z, pl.ds(start, 12, stride=2), :] = part

    def add0(z):
        for half in range(2):
            lanes = slice(128 * half, 128 * half + 128)
            lev0.w[z + 1, :, lanes] = lev0.w[z + 1, :, lanes] + raw1[half, z]

    lev0.each(add0, UNROLL)
    lev0.sweep(lev0.w, lev0.u, UNROLL)
    lev0.sweep(lev0.u, lev0.w, UNROLL)

    def last0(z, u, total):
        r = raw0[3, z] - (lev0.d[z] * u - total)
        sol[z] = u[0:16, 0:128]
        resid[z] = r[0:16, 0:128]

    lev0.stencil(lev0.w, UNROLL, last0)

    for made in pending:
        made.wait_send()


def level_scratch(slabs, rows, lanes):
    def vmem(count):
        return pltpu.VMEM((count, rows, lanes), F32)

    return [vmem(slabs), vmem(slabs), vmem(slabs + 1), vmem(slabs), vmem(slabs), vmem(slabs + 2), vmem(slabs + 2), vmem(slabs + 2)]


def shards(source, kappa_sq, lon_diff, lat_diff, sea_mask):
    def vmem(*shape):
        return pltpu.VMEM(shape, F32)

    scratch = [
        vmem(NZ, 16, 128), vmem(NZ, 16, 128), vmem(NZ, 16, 128), vmem(NZ, 16, 128),
        pltpu.VMEM((NZ, 16, 128), jnp.int32), pltpu.SemaphoreType.DMA((5,)),
        vmem(4, NZ, 24, 256), vmem(8, 128), level_scratch(NZ, 24, 256),
        vmem(3, NZ, 24, 128), level_scratch(NZ, 24, 128),
        vmem(4, HZ, 32, 128), level_scratch(HZ, 32, 128),
        vmem(4, HZ, 16, 128), level_scratch(HZ, 16, 128),
        vmem(3, HZ, 32, 128), level_scratch(HZ, 32, 128), level_scratch(QZ, 32, 128),
        vmem(NZ, 16, 128), vmem(NZ, 16, 128), vmem(HZ, 8, 128), vmem(HZ, 32, 128), vmem(HZ, 32, 128), vmem(NZ, 8, 128),
        vmem(2, 4 * NZ + HZ, 2, 128), vmem(2, 2, 16, 128), vmem(2, 4 * NZ + HZ, 2, 128), vmem(2, 2, 16, 128), vmem(4, 2, 8, 128),
        vmem(HZ, 8, 128), vmem(2, 5, 8, 128), vmem(2, 2, 5, 4, 128),
        vmem(2, HZ, 8, 128), vmem(2, 5, 8, 128), vmem(2, 2, 5, 4, 128),
        vmem(HZ, 4, 128), vmem(7, HZ, 4, 128),
        vmem(8, 128), vmem(7, 8, 128), vmem(16 * 24, 128),
        vmem(3 * HZ, 8, 128), vmem(2, 15, 8, 128), vmem(2, 2, 15, 4, 128),
        vmem(2, 3 * HZ, 8, 128), vmem(2, 15, 8, 128), vmem(2, 2, 15, 4, 128),
        vmem(20, 4, 128), vmem(2, 20, 4, 128),
        vmem(4 * HZ, 4, 128), vmem(7, 4 * HZ, 4, 128),
        vmem(32, 128), vmem(7, 32, 128), vmem(16 * 32, 128), vmem(16 * 32, 128),
        vmem(2, NZ, 4, 128), vmem(2, 1, 16, 128), vmem(2, NZ, 4, 128), vmem(2, 1, 16, 128), vmem(4, 1, 8, 128),
        pltpu.SemaphoreType.DMA((96,)), pltpu.SemaphoreType.DMA((96,)),
    ]
    shape = jax.ShapeDtypeStruct(source.shape, F32)
    anywhere = pl.BlockSpec(memory_space=pl.ANY)
    return pl.pallas_call(
        body,
        out_shape=(shape, shape),
        in_specs=[anywhere] * 5,
        out_specs=[pl.BlockSpec(memory_space=pltpu.VMEM)] * 2,
        scratch_shapes=scratch,
        compiler_params=pltpu.CompilerParams(
            collective_id=0, has_side_effects=True, vmem_limit_bytes=54848 * 1024
        ),
    )(source, kappa_sq, lon_diff, lat_diff, sea_mask)

def solution(mesh):
    spec = P(None, "tx", "ty")
    return jax.shard_map(
        shards, mesh=mesh, in_specs=(spec,) * 5, out_specs=(spec, spec), check_vma=False
    )
```

```python
import jax
import jax.numpy as jnp
from jax import lax
from jax.experimental import pallas as pl
from jax.experimental.pallas import tpu as pltpu
from jax.sharding import PartitionSpec as P

NZ = 20
HZ = 10
QZ = 5
NTX = 32
NTY = 16
OMEGA = 0.8
UNROLL = 20
MESH = pl.DeviceIdType.MESH
F32 = jnp.float32

DIAGONALS = ((1, 1), (-1, 1), (1, -1), (-1, -1))


def iota(shape, dim):
    return lax.broadcasted_iota(jnp.int32, shape, dim)


def mm(x, m):
    high = x.astype(jnp.bfloat16)
    low = (x - high.astype(F32)).astype(jnp.bfloat16)
    m = m.astype(jnp.bfloat16)
    return lax.dot_general(
        jnp.concatenate([high, low], axis=1), jnp.concatenate([m, m], axis=0),
        (((1,), (0,)), ((), ())), preferred_element_type=F32,
    )


def roll(x, shift, axis):
    shift = shift % x.shape[axis]
    return x if shift == 0 else pltpu.roll(x, shift, axis)


def one_hot(shape, hit, value=1.0):
    row, col = iota(shape, 0), iota(shape, 1)
    return jnp.where(hit(row, col), F32(value), F32(0.0))


def restrict_0():
    return one_hot((128, 128), lambda n, m: m == 32 + (n >> 1), 0.25)


def restrict_1():
    return one_hot((256, 128), lambda n, m: m == n >> 1, 0.25)


def restrict_2():
    return one_hot((128, 128), lambda n, m: m == (n & 64) + 8 + ((n & 63) >> 1), 0.25)


def restrict_3():
    def hit(n, m):
        q = n & 63
        return (m == (n & 64) + 16 + (q >> 1)) & (q >= 16) & (q < 32)

    return one_hot((128, 128), hit, 0.25)


def restrict_24():
    def hit(n, m):
        q = n & 63
        return (m == (n & 64) + 20 + (q >> 2)) & (q >= 16) & (q < 48)

    return one_hot((128, 128), hit, 1.0 / 16)


def prolong_3():
    def hit(m, n):
        q = n & 63
        return (m == (n & 64) + ((n & 128) >> 2) + 4 + (q >> 1)) & (q < 56)

    return one_hot((128, 256), hit)


def prolong_2():
    return one_hot((128, 128), lambda m, n: m == (n & 64) + 8 + ((n & 63) >> 1))


def prolong_1():
    return one_hot((128, 256), lambda m, n: m == n >> 1)


def prolong_0():
    def hit(m, n):
        rel = jnp.where(n >= 192, n - 256, n)
        return (m == 32 + (rel >> 1)) & (rel < 132) & (rel >= -4)

    return one_hot((128, 256), hit)


class Level:
    def __init__(self, slabs, seam, refs):
        self.slabs = slabs
        self.seam = seam
        self.e, self.n, self.v, self.g, self.d, self.c, self.u, self.w = refs

    def each(self, body, unroll):
        def step(z, carry):
            body(z)
            return carry

        lax.fori_loop(0, self.slabs, step, 0, unroll=min(unroll, self.slabs))

    def wrap(self, ref, rows=slice(None)):
        if self.seam:
            ref[0, rows] = roll(ref[self.slabs, rows], self.seam, 1)
            ref[self.slabs + 1, rows] = roll(ref[1, rows], -self.seam, 1)

    def clear_ends(self):
        if not self.seam:
            for ref in (self.c, self.u, self.w):
                ref[0] = jnp.zeros_like(ref[0])
                ref[self.slabs + 1] = jnp.zeros_like(ref[0])

    def faces(self, kap, lond, latd, sea, unroll, right=None):
        top = self.slabs - 1
        first = sea(0)
        if self.seam:
            low = iota(self.v.shape[1:], 1) < 64
            face_top = jnp.where(low, sea(top) * roll(first, 64, 1), 0.0)
            face_first = roll(face_top, 64, 1)
        else:
            face_top = face_first = jnp.zeros_like(first)
        self.v[0] = face_first

        def slab(z, s, face_below, face_above):
            lw = s * lond(z)
            tw = s * latd(z)
            east = 0.5 * (lw * roll(s, -1, 0) + s * roll(lw, -1, 0))
            north = 0.5 * (tw * roll(s, -1, 1) + s * roll(tw, -1, 1))
            west = roll(east, 1, 0)
            south = roll(north, 1, 1)
            diag = s * kap(z) + (west + east + south + north + face_below + face_above) + (1.0 - s)
            scale = OMEGA / diag
            self.v[z + 1] = face_above
            self.e[z] = east
            self.n[z] = north
            self.d[z] = diag
            self.g[z] = scale
            if right is not None:
                self.c[z + 1] = scale * right(z)

        def step(z, carry):
            s, face_below = carry
            s_above = sea(z + 1)
            face_above = s * s_above
            slab(z, s, face_below, face_above)
            return s_above, face_above

        s, face_below = lax.fori_loop(0, top, step, (first, face_first), unroll=min(unroll, top))
        slab(top, s, face_below, face_top)

    def stencil(self, src, unroll, use, rows=slice(None), first=0):
        def step(z, carry):
            below, u, face_below = carry
            above = src[z + 2, rows]
            face_above = self.v[z + 1, rows]
            e = self.e[z, rows]
            n = self.n[z, rows]
            use(z, u, (
                roll(e * u, 1, 0)
                + e * roll(u, -1, 0)
                + roll(n * u, 1, 1)
                + n * roll(u, -1, 1)
                + face_below * below
                + face_above * above
            ))
            return u, above, face_above

        def start(z):
            return src[z, rows], src[z + 1, rows], self.v[z, rows]

        if self.seam:
            for i in range(self.slabs):
                z = (first + i) % self.slabs
                carry = step(z, start(z) if i == 0 or z == 0 else carry)
        else:
            lax.fori_loop(0, self.slabs, step, start(0), unroll=min(unroll, self.slabs))

    def sweep(self, src, dst, unroll, rows=slice(None), first=0):
        def use(z, u, total):
            new = (1.0 - OMEGA) * u + self.c[z + 1, rows] + self.g[z, rows] * total
            dst[z + 1, rows] = new
            if self.seam and z == 0:
                dst[self.slabs + 1, rows] = roll(new, -self.seam, 1)
            if self.seam and z == self.slabs - 1:
                dst[0, rows] = roll(new, self.seam, 1)

        self.stencil(src, unroll, use, rows, first)

    def remain(self, src, unroll, put, first=0):
        def use(z, u, total):
            put(z, self.d[z] * (1.25 * self.c[z + 1] - u) + total)

        self.stencil(src, unroll, use, first=first)


def pack_edge(slabs, width, base, count):
    lane = iota(slabs[0].shape, 1)
    out = roll(slabs[0], -base, 1)
    for i in range(1, count):
        out = jnp.where(lane >= width * i, roll(slabs[i], width * i - base, 1), out)
    return out


def body(
    source_in, kappa_in, lon_in, lat_in, mask_in,
    sol, resid,
    source, kappa, lon_diff, lat_diff, mask, in_sem,
    raw0, src0, l0, raw1, l1, raw2, l2, raw3, l3, raw4, l4, l5, t0, t1, t2, t3, t4, q1,
    a_ew, a_ns, a_rew, a_rns, a_rd,
    b_pk, b_ns, b_nc, b_rpk, b_rns, b_rnc,
    f_p, f_rp,
    k_rows, k_blk, k_z, k_ev,
    p_pk, p_ns, p_nc, p_rpk, p_rns, p_rnc, q_p, q_rp, g_p, g_rp, h_blk, h_z, h_ev, h_od,
    o_ew, o_ns, o_rew, o_rns, o_rd,
    send_sem, recv_sem,
):
    mx, my = lax.axis_index("tx"), lax.axis_index("ty")
    odd = lax.rem(mx, 2) == 1
    counter = [0]
    pending = []
    places = {}

    def shifted(axis, here, shift, count):
        shift = shift % count
        if (axis, shift) not in places:
            there = here + shift
            places[axis, shift] = jnp.where(there >= count, there - count, there) if shift else here
        return places[axis, shift]

    def device(dx, dy):
        return (shifted(0, mx, dx, NTX), shifted(1, my, dy, NTY))

    def copy(src, dst, dx, dy):
        i = counter[0]
        counter[0] += 1
        made = pltpu.make_async_remote_copy(
            src_ref=src, dst_ref=dst, send_sem=send_sem.at[i], recv_sem=recv_sem.at[i],
            device_id=device(dx, dy),
            device_id_type=MESH,
        )
        made.start()
        pending.append(made)
        return made

    def arrive(copies):
        for made in copies:
            made.wait_recv()

    lev0 = Level(NZ, 0, l0)
    lev1 = Level(NZ, 0, l1)
    lev2 = Level(HZ, 64, l2)
    lev3 = Level(HZ, 64, l3)
    lev4 = Level(HZ, 64, l4)
    lev5 = Level(QZ, 32, l5)

    fetched = [
        pltpu.make_async_copy(src, dst, in_sem.at[i])
        for i, (src, dst) in enumerate((
            (mask_in, mask), (lon_in, lon_diff), (lat_in, lat_diff), (kappa_in, kappa), (source_in, source)
        ))
    ]
    for made in fetched:
        made.start()

    peers = [(2 * k, 0) for k in range(1, 16)] + [(1, 0), (-1, 0), (3, 0), (-3, 0)]
    peers += [(0, d) for d in (1, 2, 3, -1, -2, -3)] + list(DIAGONALS)
    barrier = pltpu.get_barrier_semaphore()
    for dx, dy in peers:
        pl.semaphore_signal(
            barrier, inc=1,
            device_id=device(dx, dy),
            device_id_type=MESH,
        )

    lane16 = iota((16, 128), 1)
    place = ((1, 0), (0, 0), (0, 60), (1, 60))
    edge_n = [jnp.zeros((16, 128), F32)] * 4
    edge_s = [jnp.zeros((16, 128), F32)] * 4
    own0 = (
        lambda z: kappa[z],
        lambda z: mask[z].astype(F32) * lon_diff[z],
        lambda z: mask[z].astype(F32) * lat_diff[z],
        lambda z: source[z],
    )
    for f, needed in ((1, (0, 1)), (2, (2,)), (0, (3,)), (3, (4,))):
        for i in needed:
            fetched[i].wait()
        for z in range(NZ):
            x = own0[f](z)
            raw0[f, z, 0:16, 0:128] = x
            a_ew[0, f * NZ + z] = x[0:2]
            a_ew[1, f * NZ + z] = x[14:16]
            if f == 1:
                a_ew[0, 4 * NZ + z // 2, z % 2:z % 2 + 1] = x[2:3]
                a_ew[1, 4 * NZ + z // 2, z % 2:z % 2 + 1] = x[13:14]
            start = place[f][1] + 3 * z
            edge_n[f] = jnp.where(lane16 >= start, roll(x, start - 125, 1), edge_n[f])
            edge_s[f] = jnp.where(lane16 >= start, roll(x, start, 1), edge_s[f])
    for pair, (f, g) in enumerate(((1, 2), (0, 3))):
        a_ns[0, pair] = jnp.where(lane16 < 60, edge_n[f], edge_n[g])
        a_ns[1, pair] = jnp.where(lane16 < 60, edge_s[f], edge_s[g])

    pl.semaphore_wait(barrier, len(peers))

    def send_edges(ew, ns, rew, rns, rd):
        made = [copy(ns.at[0, :, 8:16, :], rd.at[0], 1, 1)]
        made.append(copy(ns.at[0, :, 0:8, :], rd.at[1], -1, 1))
        made.append(copy(ns.at[1, :, 8:16, :], rd.at[2], 1, -1))
        made.append(copy(ns.at[1, :, 0:8, :], rd.at[3], -1, -1))
        made += [copy(ew.at[0], rew.at[0], -1, 0), copy(ew.at[1], rew.at[1], 1, 0)]
        made += [copy(ns.at[0], rns.at[0], 0, 1), copy(ns.at[1], rns.at[1], 0, -1)]
        return made

    has_s, has_n = my > 0, my < NTY - 1

    def merge_edges(f, base, rns, rd, put_rows, put_side):
        sub = iota((8, 128), 0)
        south = jnp.concatenate([rns[0, f], jnp.where(sub < 4, rd[1, f], rd[0, f])], axis=0)
        north = jnp.concatenate([rns[1, f], jnp.where(sub < 4, rd[3, f], rd[2, f])], axis=0)
        lane = iota((24, 128), 1)
        south = jnp.where(has_s, south, 0.0)
        north = jnp.where(has_n, north, 0.0)
        for z in range(NZ):
            put_rows(z)
            start = base + 3 * z
            side = jnp.where(lane < 3, roll(north, -start, 1), roll(south, 125 - start, 1))
            put_side(z, jnp.where((lane < 3) | (lane >= 125), side, 0.0))

    sent_a = send_edges(a_ew, a_ns, a_rew, a_rns, a_rd)
    for f in range(4):
        for z in range(NZ):
            raw0[f, z, 16:24, 0:128] = jnp.zeros((8, 128), F32)

    m0 = restrict_0()

    def pair_rows(ref, count):
        return ref[:, pl.ds(0, count, stride=2), :] + ref[:, pl.ds(1, count, stride=2), :]

    def down_0(x):
        return mm(x.reshape(NZ * 8, 128), m0).reshape(NZ, 8, 128)

    def pack_1(x, f, pk, ns, nc):
        lane = iota((8, 128), 1)
        for k in range(HZ):
            pk[f * HZ + k] = jnp.where(lane < 64, roll(x[k], -32, 1), roll(x[k + HZ], 32, 1))
        for k in range(5):
            group = [x[k + 5 * j] for j in range(4)]
            for side, base in ((0, 64), (1, 32)):
                edge = pack_edge(group, 32, base, 4)
                ns[side, f * 5 + k] = edge
                nc[side, 0, f * 5 + k] = edge[0:4]
                nc[side, 1, f * 5 + k] = edge[4:8]

    def send_1(pk, ns, nc, rpk, rns, rnc):
        made = [copy(nc.at[0, 1], rnc.at[0, 1], 1, 1)]
        made.append(copy(nc.at[0, 0], rnc.at[0, 0], -1, 1))
        made.append(copy(nc.at[1, 1], rnc.at[1, 1], 1, -1))
        made.append(copy(nc.at[1, 0], rnc.at[1, 0], -1, -1))
        made += [copy(pk, rpk.at[0], -1, 0), copy(pk, rpk.at[1], 1, 0)]
        made += [copy(ns.at[0], rns.at[0], 0, 1), copy(ns.at[1], rns.at[1], 0, -1)]
        return made

    def merge_1(f, own, rpk, rns, rnc, put):
        lane = iota((8, 128), 1)
        blank = jnp.zeros((4, 128), F32)

        def edge(side, i, at):
            if i == 0:
                return rns[side, at]
            if i == 1:
                return jnp.concatenate([rnc[side, 0, at], blank], axis=0)
            return jnp.concatenate([blank, rnc[side, 1, at]], axis=0)

        for z in range(NZ):
            k, shift = (z, 32) if z < HZ else (z - HZ, -32)
            middle = (own(z), roll(rpk[0, f * HZ + k], shift, 1), roll(rpk[1, f * HZ + k], shift, 1))
            for i, start in ((0, 8), (1, 16), (2, 0)):
                south = jnp.where(has_s, roll(edge(0, i, f * 5 + z % 5), -32 * (z // 5), 1), 0.0)
                north = jnp.where(has_n, roll(edge(1, i, f * 5 + z % 5), 96 - 32 * (z // 5), 1), 0.0)
                put(z, start, jnp.where(lane < 32, south, jnp.where(lane < 96, middle[i], north)))

    own1 = [
        down_0(pair_rows(kappa, 8)),
        0.25 * down_0(pair_rows(lon_diff, 8)),
        0.25 * down_0(pair_rows(lat_diff, 8)),
        (down_0(pair_rows(mask, 8).astype(F32)) > 0.0).astype(F32),
    ]

    m1 = restrict_1()

    def down_1(x):
        pair = jnp.concatenate([x[0:HZ], x[HZ:NZ]], axis=2).reshape(HZ * 8, 256)
        t2[...] = mm(pair, m1).reshape(HZ, 8, 128)
        return t2[:, pl.ds(0, 4, stride=2), :] + t2[:, pl.ds(1, 4, stride=2), :]

    own2 = []
    rows4 = []
    for f, scale in enumerate((1.0, 0.25, 0.25, 1.0)):
        x = down_1(own1[f])
        own2.append((x > 0.0).astype(F32) if f == 3 else scale * x)
        flat = t2.reshape(HZ * 8, 128)
        rows4.append(sum(flat[pl.ds(i, HZ, stride=8), :] for i in range(8)))
    for f in range(4):
        g_p[f * HZ:(f + 1) * HZ] = own2[f]
        for k in range(5):
            q_p[f * 5 + k] = own2[f][k] + roll(own2[f][k + 5], 32, 1)
    sent_q = [copy(q_p, q_rp.at[0], 0, 1), copy(q_p, q_rp.at[1], 0, -1)]

    for f, x in enumerate((own1[0], own1[3] * own1[1], own1[3] * own1[2])):
        pack_1(x, f, p_pk, p_ns, p_nc)
        raw1[f, :, 8:16, :] = x
    sent_p1 = send_1(p_pk, p_ns, p_nc, p_rpk, p_rns, p_rnc)

    def send_z(blk, slots):
        slots[3] = blk[...]
        return [copy(blk, slots.at[3 - d], 0, d) for d in (3, -3, 2, -2, 1, -1)]

    def window_row(slots, count):
        row = jnp.zeros((count, 128), F32)
        for s in range(7):
            inside = (my + (s - 3) >= 0) & (my + (s - 3) < NTY)
            row = row + jnp.where(inside, roll(slots[s], 8 * (s - 3), 1), 0.0)
        return row

    def folded_window_row(slots):
        part = iota((8, 128), 1) & 63
        out = [jnp.zeros((8, 128), F32)] * 3
        for s in range(7):
            inside = (my + (s - 3) >= 0) & (my + (s - 3) < NTY)
            block = jnp.where(inside, slots[s], 0.0)
            for i in range(3):
                pick = (part >= 24 + 8 * i) & (part < 32 + 8 * i)
                out[i] = out[i] + roll(jnp.where(pick, block, 0.0), 8 * (s - 3 - i), 1)
        return jnp.concatenate(out, axis=0)

    def send_plane(row, ev, count):
        own = pl.ds(8 * count, count)
        ev[own, :] = row
        return [
            copy(ev.at[own], ev.at[pl.ds(((8 - k) % 16) * count, count)], 2 * k, 0)
            for k in (10, 6, 9, 7, 11, 5, 2, 14, 8, 3, 13, 1, 15, 4, 12)
        ]

    def send_sibling(ev, od):
        i = counter[0]
        counter[0] += 1
        made = pltpu.make_async_remote_copy(
            src_ref=ev, dst_ref=od, send_sem=send_sem.at[i], recv_sem=recv_sem.at[i],
            device_id=(mx + 1 - 2 * lax.rem(mx, 2), my), device_id_type=MESH,
        )
        made.start()
        pending.append(made)
        return [made]

    def window_slab(ev, od, index, count, put):
        put(pl.ds(0, 16, stride=2), ev[pl.ds(index, 16, stride=count), :])
        other = od[pl.ds(index, 16, stride=count), :]
        put(pl.ds(1, 16, stride=2), jnp.where(odd, roll(other, -1, 0), other))

    arrive(sent_a)
    for f in range(4):
        def put_rows(z):
            raw0[f, z, 16:18, 0:128] = a_rew[0, f * NZ + z]
            raw0[f, z, 22:24, 0:128] = a_rew[1, f * NZ + z]
            if f == 1:
                pick = slice(z % 2, z % 2 + 1)
                raw0[f, z, 18:19, 0:128] = a_rew[0, 4 * NZ + z // 2, pick]
                raw0[f, z, 21:22, 0:128] = a_rew[1, 4 * NZ + z // 2, pick]

        def put_side(z, x):
            raw0[f, z, :, 128:256] = x

        merge_edges(place[f][0], place[f][1], a_rns, a_rd, put_rows, put_side)

    def send_2(p, rp):
        return [copy(p, rp.at[3 - d], d, 0) for d in (3, -3, 2, -2, 1, -1)]

    arrive(sent_q)
    part = iota((4, 128), 1) & 63
    for f in range(4):
        for k in range(HZ):
            south = roll(q_rp[0, f * 5 + k % 5], -32 if k < 5 else -64, 1)
            north = roll(q_rp[1, f * 5 + k % 5], 32 if k < 5 else 0, 1)
            south = jnp.where(has_s, south, 0.0)
            north = jnp.where(has_n, north, 0.0)
            g_p[f * HZ + k] = jnp.where(part < 16, south, jnp.where(part < 48, g_p[f * HZ + k], north))
    sent_p2 = send_2(g_p, g_rp)

    def sea0(z):
        return (raw0[1, z] > 0.0).astype(F32)

    lev0.faces(lambda z: raw0[0, z], lambda z: raw0[1, z], lambda z: raw0[2, z], sea0, UNROLL, lambda z: raw0[3, z])
    lev0.clear_ends()


    lev0.sweep(lev0.c, lev0.w, UNROLL)

    def remain0(z, u, total):
        r = raw0[3, z] - (lev0.d[z] * u - total)
        t0[z] = r[0:16, 0:128]

    lev0.stencil(lev0.w, UNROLL, remain0)
    b1 = down_0(pair_rows(t0, 8))

    arrive(sent_p1)

    def sea_1(z):
        return (raw1[1, z] > 0.0).astype(F32)

    for f in range(3):
        def put1(z, start, x):
            raw1[f, z, start:start + 8, :] = x

        merge_1(f, lambda z: raw1[f, z, 8:16, :], p_rpk, p_rns, p_rnc, put1)
    lev1.faces(lambda z: raw1[0, z], lambda z: raw1[1, z], lambda z: raw1[2, z], sea_1, UNROLL)
    lev1.clear_ends()
    c1 = lev1.g[:, 8:16, :] * b1
    q1[...] = c1
    pack_1(c1, 0, b_pk, b_ns, b_nc)
    sent_b = send_1(b_pk, b_ns, b_nc, b_rpk, b_rns, b_rnc)

    edge_n = jnp.zeros((16, 128), F32)
    edge_s = jnp.zeros((16, 128), F32)
    for z in range(NZ):
        x = lev0.w[z + 1, 0:16, 0:128]
        o_ew[0, z] = x[0:4]
        o_ew[1, z] = x[12:16]
        edge_n = jnp.where(lane16 >= 3 * z, roll(x, 3 * z - 125, 1), edge_n)
        edge_s = jnp.where(lane16 >= 3 * z, roll(x, 3 * z, 1), edge_s)
    o_ns[0, 0] = edge_n
    o_ns[1, 0] = edge_s

    padding = jnp.zeros((16 - HZ, 128), F32)
    every = mm(jnp.concatenate([part for x in rows4 for part in (x, padding)], axis=0), restrict_24())
    sea4 = (every[48:58] > 0.0).astype(F32)
    h_blk[0:10, :] = every[0:10]
    h_blk[10:20, :] = sea4 * every[16:26] * (1.0 / 64)
    h_blk[20:30, :] = sea4 * every[32:42] * (1.0 / 64)
    h_blk[30:32, :] = jnp.zeros((2, 128), F32)

    arrive(sent_p2)
    for f in range(4):
        for s in range(7):
            piece = g_p if s == 3 else g_rp.at[s]
            raw2[f, :, 4 * s:4 * s + 4, :] = piece[f * HZ:(f + 1) * HZ]
        raw2[f, :, 28:32, :] = jnp.zeros((HZ, 4, 128), F32)
    lev2.faces(lambda z: raw2[0, z], lambda z: raw2[1, z], lambda z: raw2[2, z], lambda z: raw2[3, z], UNROLL)

    m2 = restrict_2()

    def down_2(ref):
        return mm(pair_rows(ref, 16).reshape(HZ * 16, 128), m2).reshape(HZ, 16, 128)

    raw3[0] = down_2(raw2.at[0])
    raw3[1] = 0.25 * down_2(raw2.at[1])
    raw3[2] = 0.25 * down_2(raw2.at[2])
    raw3[3] = (down_2(raw2.at[3]) > 0.0).astype(F32)
    lev3.faces(lambda z: raw3[0, z], lambda z: raw3[1, z], lambda z: raw3[2, z], lambda z: raw3[3, z], UNROLL)

    arrive(sent_b)
    sent_hz = send_z(h_blk, h_z)

    def put1c(z, start, x):
        lev1.c[z + 1, start:start + 8, :] = x

    merge_1(0, lambda z: q1[z], b_rpk, b_rns, b_rnc, put1c)
    lev1.sweep(lev1.c, lev1.w, UNROLL)

    def remain1(z, r):
        q1[z] = r[8:16]

    lev1.remain(lev1.w, UNROLL, remain1)
    b2 = down_1(q1[...])

    f_p[...] = lev2.g[:, 12:16, :] * b2
    sent_c = send_2(f_p, f_rp)

    arrive(sent_hz)
    row_h = window_row(h_z, 32)
    arrive(sent_c)
    sent_hp = send_plane(row_h, h_ev, 32)
    sent_o = send_edges(o_ew, o_ns, o_rew, o_rns, o_rd)
    for s in range(7):
        piece = f_p if s == 3 else f_rp.at[s]
        lev2.c[1:HZ + 1, 4 * s:4 * s + 4, :] = piece[...]
    lev2.c[1:HZ + 1, 28:32, :] = jnp.zeros((HZ, 4, 128), F32)
    lev2.wrap(lev2.c)
    lev2.sweep(lev2.c, lev2.w, UNROLL, first=1)

    def remain2(z, r):
        t4[z] = r

    lev2.remain(lev2.w, UNROLL, remain2, 2)

    lev3.c[1:HZ + 1] = lev3.g[...] * down_2(t4)
    lev3.wrap(lev3.c)
    lev3.sweep(lev3.c, lev3.w, UNROLL, first=1)

    def remain3(z, r):
        k_rows[16 * z:16 * z + 16, :] = r

    lev3.remain(lev3.w, UNROLL, remain3, 2)
    own_cell = k_rows[pl.ds(6, HZ, stride=16), :] + k_rows[pl.ds(7, HZ, stride=16), :]
    east_cell = k_rows[pl.ds(8, HZ, stride=16), :] + k_rows[pl.ds(9, HZ, stride=16), :]
    cells = mm(jnp.concatenate([own_cell, padding, east_cell, padding], axis=0), restrict_3())
    last = jnp.concatenate([cells[8:10], cells[24:26], jnp.zeros((4, 128), F32)], axis=0)
    k_blk[...] = cells[0:8] + roll(cells[16:24], 8, 1) + roll(last, 16, 1)
    sent_kz = send_z(k_blk, k_z)

    arrive(sent_hp)
    sent_hs = send_sibling(h_ev, h_od)

    arrive(sent_kz)
    sent_kp = send_plane(folded_window_row(k_z), k_ev, 24)

    arrive(sent_hs)
    for f in range(3):
        for z in range(HZ):
            def put4(rows, x):
                raw4[f, z, rows, :] = x

            window_slab(h_ev, h_od, f * HZ + z, 32, put4)

    def sea_4(z):
        return (raw4[1, z] > 0.0).astype(F32)

    lev4.faces(lambda z: raw4[0, z], lambda z: raw4[1, z], lambda z: raw4[2, z], sea_4, UNROLL)
    group = iota((32, 128), 1) & 32

    def fold(lower, upper):
        return jnp.where(group == 0, roll(lower, -12, 1), roll(upper, 20, 1))

    for k in range(QZ):
        lev5.e[k] = fold(lev4.e[k], lev4.e[k + QZ])
        lev5.n[k] = fold(lev4.n[k], lev4.n[k + QZ])
        lev5.g[k] = fold(lev4.g[k], lev4.g[k + QZ])
        lev5.v[k + 1] = fold(lev4.v[k + 1], lev4.v[k + QZ + 1])
    lev5.v[0] = roll(lev5.v[QZ], 32, 1)

    arrive(sent_o)

    def put_rows0(z):
        lev0.w[z + 1, 16:20, 0:128] = o_rew[0, z]
        lev0.w[z + 1, 20:24, 0:128] = o_rew[1, z]

    def put_side0(z, x):
        lev0.w[z + 1, :, 128:256] = x

    merge_edges(0, 0, o_rns, o_rd, put_rows0, put_side0)
    arrive(sent_kp)
    for z in range(HZ):
        for i in range(2):
            at = 8 * i + z if z < 8 else 16 + 2 * i + z - 8
            lev4.c[z + 1, pl.ds(i, 16, stride=2), :] = k_ev[pl.ds(at, 16, stride=24), :]
    for z in range(HZ):
        lev4.c[z + 1] = lev4.g[z] * lev4.c[z + 1]
    lev4.wrap(lev4.c)
    for k in range(QZ):
        lev5.c[k + 1] = fold(lev4.c[k + 1], lev4.c[k + QZ + 1])
    lev4.sweep(lev4.c, lev4.w, HZ, first=1)

    def four(step, carry):
        for i in range(2):
            lev4.sweep(lev4.w, lev4.u, HZ, first=2 + 2 * i)
            lev4.sweep(lev4.u, lev4.w, HZ, first=3 + 2 * i)
        return carry

    lax.fori_loop(0, 2, four, 0)
    for k in range(QZ):
        lev5.u[k + 1] = fold(lev4.w[k + 1], lev4.w[k + QZ + 1])
    lev5.wrap(lev5.u)
    for i in range(10):
        src, dst = (lev5.u, lev5.w) if i % 2 == 0 else (lev5.w, lev5.u)
        lev5.sweep(src, dst, QZ, slice(None) if i < 5 else slice(8, 24), first=(i + 1) % QZ)

    up = mm(lev5.u[1:QZ + 1, 13:21, :].reshape(QZ * 8, 128), prolong_3()).reshape(QZ, 8, 256)
    for start in range(2):
        t3[0:QZ, pl.ds(start, 8, stride=2), :] = up[:, :, 0:128]
        t3[QZ:HZ, pl.ds(start, 8, stride=2), :] = up[:, :, 128:256]

    def add3(z):
        lev3.w[z + 1] = lev3.w[z + 1] + t3[z, 0:16, :]

    lev3.each(add3, UNROLL)
    lev3.wrap(lev3.w)
    lev3.sweep(lev3.w, lev3.u, UNROLL, first=1)
    lev3.sweep(lev3.u, lev3.w, UNROLL, first=2)

    up = mm(lev3.w[1:HZ + 1].reshape(HZ * 16, 128), prolong_2()).reshape(HZ, 16, 128)
    for start in range(2):
        t3[:, pl.ds(start, 16, stride=2), :] = up

    def add2(z):
        lev2.w[z + 1] = lev2.w[z + 1] + t3[z]

    lev2.each(add2, UNROLL)
    lev2.wrap(lev2.w)
    lev2.sweep(lev2.w, lev2.u, UNROLL, first=1)
    lev2.sweep(lev2.u, lev2.w, UNROLL, first=2)

    t3[:, 0:16, :] = lev2.w[1:HZ + 1, 8:24, :]
    up = mm(t3[:, 0:16, :].reshape(HZ * 16, 128), prolong_1()).reshape(HZ, 16, 256)
    for start in range(2):
        t1[0:HZ, :, :] = up[:, :, 0:128]
        t1[HZ:NZ, :, :] = up[:, :, 128:256]
    for z in range(NZ):
        for start in range(2):
            q = pl.ds(start, 12, stride=2)
            raw1[0, z, q, :] = t1[z, 0:12, :]

    def add1(z):
        lev1.w[z + 1] = lev1.w[z + 1] + raw1[0, z]

    lev1.each(add1, UNROLL)
    lev1.sweep(lev1.w, lev1.u, UNROLL)
    lev1.sweep(lev1.u, lev1.w, UNROLL)

    for z in range(NZ):
        t1[z, 0:8, :] = lev1.w[z + 1, 8:16, :]
        t1[z, 8:10, :] = lev1.w[z + 1, 16:18, :]
        t1[z, 10:12, :] = lev1.w[z + 1, 6:8, :]
        t1[z, 12:16, :] = jnp.zeros((4, 128), F32)
    up = mm(t1[...].reshape(NZ * 16, 128), prolong_0()).reshape(NZ, 16, 256)
    for z in range(NZ):
        for half in range(2):
            part = up[z, 0:12, 128 * half:128 * half + 128]
            for start in range(2):
                raw1[half, z, pl.ds(start, 12, stride=2), :] = part

    def add0(z):
        for half in range(2):
            lanes = slice(128 * half, 128 * half + 128)
            lev0.w[z + 1, :, lanes] = lev0.w[z + 1, :, lanes] + raw1[half, z]

    lev0.each(add0, UNROLL)
    lev0.sweep(lev0.w, lev0.u, UNROLL)
    lev0.sweep(lev0.u, lev0.w, UNROLL)

    def last0(z, u, total):
        r = raw0[3, z] - (lev0.d[z] * u - total)
        sol[z] = u[0:16, 0:128]
        resid[z] = r[0:16, 0:128]

    lev0.stencil(lev0.w, UNROLL, last0)

    for made in pending:
        made.wait_send()


def level_scratch(slabs, rows, lanes):
    def vmem(count):
        return pltpu.VMEM((count, rows, lanes), F32)

    return [vmem(slabs), vmem(slabs), vmem(slabs + 1), vmem(slabs), vmem(slabs), vmem(slabs + 2), vmem(slabs + 2), vmem(slabs + 2)]


def shards(source, kappa_sq, lon_diff, lat_diff, sea_mask):
    def vmem(*shape):
        return pltpu.VMEM(shape, F32)

    scratch = [
        vmem(NZ, 16, 128), vmem(NZ, 16, 128), vmem(NZ, 16, 128), vmem(NZ, 16, 128),
        pltpu.VMEM((NZ, 16, 128), jnp.int32), pltpu.SemaphoreType.DMA((5,)),
        vmem(4, NZ, 24, 256), vmem(8, 128), level_scratch(NZ, 24, 256),
        vmem(3, NZ, 24, 128), level_scratch(NZ, 24, 128),
        vmem(4, HZ, 32, 128), level_scratch(HZ, 32, 128),
        vmem(4, HZ, 16, 128), level_scratch(HZ, 16, 128),
        vmem(3, HZ, 32, 128), level_scratch(HZ, 32, 128), level_scratch(QZ, 32, 128),
        vmem(NZ, 16, 128), vmem(NZ, 16, 128), vmem(HZ, 8, 128), vmem(HZ, 32, 128), vmem(HZ, 32, 128), vmem(NZ, 8, 128),
        vmem(2, 4 * NZ + HZ, 2, 128), vmem(2, 2, 16, 128), vmem(2, 4 * NZ + HZ, 2, 128), vmem(2, 2, 16, 128), vmem(4, 2, 8, 128),
        vmem(HZ, 8, 128), vmem(2, 5, 8, 128), vmem(2, 2, 5, 4, 128),
        vmem(2, HZ, 8, 128), vmem(2, 5, 8, 128), vmem(2, 2, 5, 4, 128),
        vmem(HZ, 4, 128), vmem(7, HZ, 4, 128),
        vmem(HZ * 16, 128), vmem(8, 128), vmem(7, 8, 128), vmem(16 * 24, 128),
        vmem(3 * HZ, 8, 128), vmem(2, 15, 8, 128), vmem(2, 2, 15, 4, 128),
        vmem(2, 3 * HZ, 8, 128), vmem(2, 15, 8, 128), vmem(2, 2, 15, 4, 128),
        vmem(20, 4, 128), vmem(2, 20, 4, 128),
        vmem(4 * HZ, 4, 128), vmem(7, 4 * HZ, 4, 128),
        vmem(32, 128), vmem(7, 32, 128), vmem(16 * 32, 128), vmem(16 * 32, 128),
        vmem(2, NZ, 4, 128), vmem(2, 1, 16, 128), vmem(2, NZ, 4, 128), vmem(2, 1, 16, 128), vmem(4, 1, 8, 128),
        pltpu.SemaphoreType.DMA((96,)), pltpu.SemaphoreType.DMA((96,)),
    ]
    shape = jax.ShapeDtypeStruct(source.shape, F32)
    anywhere = pl.BlockSpec(memory_space=pl.ANY)
    return pl.pallas_call(
        body,
        out_shape=(shape, shape),
        in_specs=[anywhere] * 5,
        out_specs=[pl.BlockSpec(memory_space=pltpu.VMEM)] * 2,
        scratch_shapes=scratch,
        compiler_params=pltpu.CompilerParams(
            collective_id=0, has_side_effects=True, vmem_limit_bytes=54848 * 1024
        ),
    )(source, kappa_sq, lon_diff, lat_diff, sea_mask)

def solution(mesh):
    spec = P(None, "tx", "ty")
    return jax.shard_map(
        shards, mesh=mesh, in_specs=(spec,) * 5, out_specs=(spec, spec), check_vma=False
    )
```

```python
import jax
import jax.numpy as jnp
from jax import lax
from jax.experimental import pallas as pl
from jax.experimental.pallas import tpu as pltpu
from jax.sharding import PartitionSpec as P

NZ = 20
HZ = 10
QZ = 5
NTX = 32
NTY = 16
OMEGA = 0.8
UNROLL = 20
MESH = pl.DeviceIdType.MESH
F32 = jnp.float32

DIAGONALS = ((1, 1), (-1, 1), (1, -1), (-1, -1))


def iota(shape, dim):
    return lax.broadcasted_iota(jnp.int32, shape, dim)


def mm(x, m):
    high = x.astype(jnp.bfloat16)
    low = (x - high.astype(F32)).astype(jnp.bfloat16)
    m = m.astype(jnp.bfloat16)
    return lax.dot_general(
        jnp.concatenate([high, low], axis=1), jnp.concatenate([m, m], axis=0),
        (((1,), (0,)), ((), ())), preferred_element_type=F32,
    )


def roll(x, shift, axis):
    shift = shift % x.shape[axis]
    return x if shift == 0 else pltpu.roll(x, shift, axis)


def one_hot(shape, hit, value=1.0):
    row, col = iota(shape, 0), iota(shape, 1)
    return jnp.where(hit(row, col), F32(value), F32(0.0))


def restrict_0():
    return one_hot((128, 128), lambda n, m: m == 32 + (n >> 1), 0.25)


def restrict_1():
    return one_hot((256, 128), lambda n, m: m == n >> 1, 0.25)


def restrict_2():
    return one_hot((128, 128), lambda n, m: m == (n & 64) + 8 + ((n & 63) >> 1), 0.25)


def restrict_3():
    def hit(n, m):
        q = n & 63
        return (m == (n & 64) + 16 + (q >> 1)) & (q >= 16) & (q < 32)

    return one_hot((128, 128), hit, 0.25)


def restrict_24():
    def hit(n, m):
        q = n & 63
        return (m == (n & 64) + 20 + (q >> 2)) & (q >= 16) & (q < 48)

    return one_hot((128, 128), hit, 1.0 / 16)


def prolong_3():
    def hit(m, n):
        q = n & 63
        return (m == (n & 64) + ((n & 128) >> 2) + 4 + (q >> 1)) & (q < 56)

    return one_hot((128, 256), hit)


def prolong_2():
    return one_hot((128, 128), lambda m, n: m == (n & 64) + 8 + ((n & 63) >> 1))


def prolong_1():
    return one_hot((128, 256), lambda m, n: m == n >> 1)


def prolong_0():
    def hit(m, n):
        rel = jnp.where(n >= 192, n - 256, n)
        return (m == 32 + (rel >> 1)) & (rel < 132) & (rel >= -4)

    return one_hot((128, 256), hit)


class Level:
    def __init__(self, slabs, seam, refs):
        self.slabs = slabs
        self.seam = seam
        self.e, self.n, self.v, self.g, self.d, self.c, self.u, self.w = refs

    def each(self, body, unroll):
        def step(z, carry):
            body(z)
            return carry

        lax.fori_loop(0, self.slabs, step, 0, unroll=min(unroll, self.slabs))

    def wrap(self, ref, rows=slice(None)):
        if self.seam:
            ref[0, rows] = roll(ref[self.slabs, rows], self.seam, 1)
            ref[self.slabs + 1, rows] = roll(ref[1, rows], -self.seam, 1)

    def clear_ends(self):
        if not self.seam:
            for ref in (self.c, self.u, self.w):
                ref[0] = jnp.zeros_like(ref[0])
                ref[self.slabs + 1] = jnp.zeros_like(ref[0])

    def faces(self, kap, lond, latd, sea, unroll, right=None):
        top = self.slabs - 1
        first = sea(0)
        if self.seam:
            low = iota(self.v.shape[1:], 1) < 64
            face_top = jnp.where(low, sea(top) * roll(first, 64, 1), 0.0)
            face_first = roll(face_top, 64, 1)
        else:
            face_top = face_first = jnp.zeros_like(first)
        self.v[0] = face_first

        def slab(z, s, face_below, face_above):
            lw = s * lond(z)
            tw = s * latd(z)
            east = 0.5 * (lw * roll(s, -1, 0) + s * roll(lw, -1, 0))
            north = 0.5 * (tw * roll(s, -1, 1) + s * roll(tw, -1, 1))
            west = roll(east, 1, 0)
            south = roll(north, 1, 1)
            diag = s * kap(z) + (west + east + south + north + face_below + face_above) + (1.0 - s)
            scale = OMEGA / diag
            self.v[z + 1] = face_above
            self.e[z] = east
            self.n[z] = north
            self.d[z] = diag
            self.g[z] = scale
            if right is not None:
                self.c[z + 1] = scale * right(z)

        def step(z, carry):
            s, face_below = carry
            s_above = sea(z + 1)
            face_above = s * s_above
            slab(z, s, face_below, face_above)
            return s_above, face_above

        s, face_below = lax.fori_loop(0, top, step, (first, face_first), unroll=min(unroll, top))
        slab(top, s, face_below, face_top)

    def stencil(self, src, unroll, use, rows=slice(None), first=0):
        def step(z, carry):
            below, u, face_below = carry
            above = src[z + 2, rows]
            face_above = self.v[z + 1, rows]
            e = self.e[z, rows]
            n = self.n[z, rows]
            use(z, u, (
                roll(e * u, 1, 0)
                + e * roll(u, -1, 0)
                + roll(n * u, 1, 1)
                + n * roll(u, -1, 1)
                + face_below * below
                + face_above * above
            ))
            return u, above, face_above

        def start(z):
            return src[z, rows], src[z + 1, rows], self.v[z, rows]

        if self.seam:
            for i in range(self.slabs):
                z = (first + i) % self.slabs
                carry = step(z, start(z) if i == 0 or z == 0 else carry)
        else:
            lax.fori_loop(0, self.slabs, step, start(0), unroll=min(unroll, self.slabs))

    def sweep(self, src, dst, unroll, rows=slice(None), first=0):
        def use(z, u, total):
            new = (1.0 - OMEGA) * u + self.c[z + 1, rows] + self.g[z, rows] * total
            dst[z + 1, rows] = new
            if self.seam and z == 0:
                dst[self.slabs + 1, rows] = roll(new, -self.seam, 1)
            if self.seam and z == self.slabs - 1:
                dst[0, rows] = roll(new, self.seam, 1)

        self.stencil(src, unroll, use, rows, first)

    def remain(self, src, unroll, put, first=0):
        def use(z, u, total):
            put(z, self.d[z] * (1.25 * self.c[z + 1] - u) + total)

        self.stencil(src, unroll, use, first=first)


def pack_edge(slabs, width, base, count):
    lane = iota(slabs[0].shape, 1)
    out = roll(slabs[0], -base, 1)
    for i in range(1, count):
        out = jnp.where(lane >= width * i, roll(slabs[i], width * i - base, 1), out)
    return out


def body(
    source_in, kappa_in, lon_in, lat_in, mask_in,
    sol, resid,
    source, kappa, lon_diff, lat_diff, mask, in_sem,
    raw0, src0, l0, raw1, l1, raw2, l2, raw3, l3, raw4, l4, l5, t0, t1, t2, t3, t4, q1,
    a_ew, a_ns, a_rew, a_rns, a_rd,
    b_pk, b_ns, b_nc, b_rpk, b_rns, b_rnc,
    f_p, f_rp,
    k_rows, k_blk, k_z, k_ev,
    p_pk, p_ns, p_nc, p_rpk, p_rns, p_rnc, q_p, q_rp, g_p, g_rp, h_blk, h_z, h_ev, h_od,
    o_ew, o_ns, o_rew, o_rns, o_rd,
    send_sem, recv_sem,
):
    mx, my = lax.axis_index("tx"), lax.axis_index("ty")
    odd = lax.rem(mx, 2) == 1
    counter = [0]
    pending = []
    places = {}

    def shifted(axis, here, shift, count):
        shift = shift % count
        if (axis, shift) not in places:
            there = here + shift
            places[axis, shift] = jnp.where(there >= count, there - count, there) if shift else here
        return places[axis, shift]

    def device(dx, dy):
        return (shifted(0, mx, dx, NTX), shifted(1, my, dy, NTY))

    def copy(src, dst, dx, dy):
        i = counter[0]
        counter[0] += 1
        made = pltpu.make_async_remote_copy(
            src_ref=src, dst_ref=dst, send_sem=send_sem.at[i], recv_sem=recv_sem.at[i],
            device_id=device(dx, dy),
            device_id_type=MESH,
        )
        made.start()
        pending.append(made)
        return made

    def arrive(copies):
        for made in copies:
            made.wait_recv()

    lev0 = Level(NZ, 0, l0)
    lev1 = Level(NZ, 0, l1)
    lev2 = Level(HZ, 64, l2)
    lev3 = Level(HZ, 64, l3)
    lev4 = Level(HZ, 64, l4)
    lev5 = Level(QZ, 32, l5)

    fetched = [
        pltpu.make_async_copy(src, dst, in_sem.at[i])
        for i, (src, dst) in enumerate((
            (mask_in, mask), (lon_in, lon_diff), (lat_in, lat_diff), (kappa_in, kappa), (source_in, source)
        ))
    ]
    for made in fetched:
        made.start()

    peers = [(2 * k, 0) for k in range(1, 16)] + [(1, 0), (-1, 0), (3, 0), (-3, 0)]
    peers += [(0, d) for d in (1, 2, 3, -1, -2, -3)] + list(DIAGONALS)
    barrier = pltpu.get_barrier_semaphore()
    for dx, dy in peers:
        pl.semaphore_signal(
            barrier, inc=1,
            device_id=device(dx, dy),
            device_id_type=MESH,
        )

    lane16 = iota((16, 128), 1)
    place = ((1, 0), (0, 0), (0, 60), (1, 60))
    edge_n = [jnp.zeros((16, 128), F32)] * 4
    edge_s = [jnp.zeros((16, 128), F32)] * 4
    own0 = (
        lambda z: kappa[z],
        lambda z: mask[z].astype(F32) * lon_diff[z],
        lambda z: mask[z].astype(F32) * lat_diff[z],
        lambda z: source[z],
    )
    for f, needed in ((1, (0, 1)), (2, (2,)), (0, (3,)), (3, (4,))):
        for i in needed:
            fetched[i].wait()
        for z in range(NZ):
            x = own0[f](z)
            raw0[f, z, 0:16, 0:128] = x
            a_ew[0, f * NZ + z] = x[0:2]
            a_ew[1, f * NZ + z] = x[14:16]
            if f == 1:
                a_ew[0, 4 * NZ + z // 2, z % 2:z % 2 + 1] = x[2:3]
                a_ew[1, 4 * NZ + z // 2, z % 2:z % 2 + 1] = x[13:14]
            start = place[f][1] + 3 * z
            edge_n[f] = jnp.where(lane16 >= start, roll(x, start - 125, 1), edge_n[f])
            edge_s[f] = jnp.where(lane16 >= start, roll(x, start, 1), edge_s[f])
    for pair, (f, g) in enumerate(((1, 2), (0, 3))):
        a_ns[0, pair] = jnp.where(lane16 < 60, edge_n[f], edge_n[g])
        a_ns[1, pair] = jnp.where(lane16 < 60, edge_s[f], edge_s[g])

    pl.semaphore_wait(barrier, len(peers))

    def send_edges(ew, ns, rew, rns, rd):
        made = [copy(ns.at[0, :, 8:16, :], rd.at[0], 1, 1)]
        made.append(copy(ns.at[0, :, 0:8, :], rd.at[1], -1, 1))
        made.append(copy(ns.at[1, :, 8:16, :], rd.at[2], 1, -1))
        made.append(copy(ns.at[1, :, 0:8, :], rd.at[3], -1, -1))
        made += [copy(ew.at[0], rew.at[0], -1, 0), copy(ew.at[1], rew.at[1], 1, 0)]
        made += [copy(ns.at[0], rns.at[0], 0, 1), copy(ns.at[1], rns.at[1], 0, -1)]
        return made

    has_s, has_n = my > 0, my < NTY - 1

    def merge_edges(f, base, rns, rd, put_rows, put_side):
        sub = iota((8, 128), 0)
        south = jnp.concatenate([rns[0, f], jnp.where(sub < 4, rd[1, f], rd[0, f])], axis=0)
        north = jnp.concatenate([rns[1, f], jnp.where(sub < 4, rd[3, f], rd[2, f])], axis=0)
        lane = iota((24, 128), 1)
        south = jnp.where(has_s, south, 0.0)
        north = jnp.where(has_n, north, 0.0)
        for z in range(NZ):
            put_rows(z)
            start = base + 3 * z
            side = jnp.where(lane < 3, roll(north, -start, 1), roll(south, 125 - start, 1))
            put_side(z, jnp.where((lane < 3) | (lane >= 125), side, 0.0))

    sent_a = send_edges(a_ew, a_ns, a_rew, a_rns, a_rd)
    for f in range(4):
        for z in range(NZ):
            raw0[f, z, 16:24, 0:128] = jnp.zeros((8, 128), F32)

    m0 = restrict_0()

    def pair_rows(ref, count):
        return ref[:, pl.ds(0, count, stride=2), :] + ref[:, pl.ds(1, count, stride=2), :]

    def down_0(x):
        return mm(x.reshape(NZ * 8, 128), m0).reshape(NZ, 8, 128)

    def pack_1(x, f, pk, ns, nc):
        lane = iota((8, 128), 1)
        for k in range(HZ):
            pk[f * HZ + k] = jnp.where(lane < 64, roll(x[k], -32, 1), roll(x[k + HZ], 32, 1))
        for k in range(5):
            group = [x[k + 5 * j] for j in range(4)]
            for side, base in ((0, 64), (1, 32)):
                edge = pack_edge(group, 32, base, 4)
                ns[side, f * 5 + k] = edge
                nc[side, 0, f * 5 + k] = edge[0:4]
                nc[side, 1, f * 5 + k] = edge[4:8]

    def send_1(pk, ns, nc, rpk, rns, rnc):
        made = [copy(nc.at[0, 1], rnc.at[0, 1], 1, 1)]
        made.append(copy(nc.at[0, 0], rnc.at[0, 0], -1, 1))
        made.append(copy(nc.at[1, 1], rnc.at[1, 1], 1, -1))
        made.append(copy(nc.at[1, 0], rnc.at[1, 0], -1, -1))
        made += [copy(pk, rpk.at[0], -1, 0), copy(pk, rpk.at[1], 1, 0)]
        made += [copy(ns.at[0], rns.at[0], 0, 1), copy(ns.at[1], rns.at[1], 0, -1)]
        return made

    def merge_1(f, own, rpk, rns, rnc, put):
        lane = iota((8, 128), 1)
        blank = jnp.zeros((4, 128), F32)

        def edge(side, i, at):
            if i == 0:
                return rns[side, at]
            if i == 1:
                return jnp.concatenate([rnc[side, 0, at], blank], axis=0)
            return jnp.concatenate([blank, rnc[side, 1, at]], axis=0)

        for z in range(NZ):
            k, shift = (z, 32) if z < HZ else (z - HZ, -32)
            middle = (own(z), roll(rpk[0, f * HZ + k], shift, 1), roll(rpk[1, f * HZ + k], shift, 1))
            for i, start in ((0, 8), (1, 16), (2, 0)):
                south = jnp.where(has_s, roll(edge(0, i, f * 5 + z % 5), -32 * (z // 5), 1), 0.0)
                north = jnp.where(has_n, roll(edge(1, i, f * 5 + z % 5), 96 - 32 * (z // 5), 1), 0.0)
                put(z, start, jnp.where(lane < 32, south, jnp.where(lane < 96, middle[i], north)))

    own1 = [
        down_0(pair_rows(kappa, 8)),
        0.25 * down_0(pair_rows(lon_diff, 8)),
        0.25 * down_0(pair_rows(lat_diff, 8)),
        (down_0(pair_rows(mask, 8).astype(F32)) > 0.0).astype(F32),
    ]

    m1 = restrict_1()

    def down_1(x):
        pair = jnp.concatenate([x[0:HZ], x[HZ:NZ]], axis=2).reshape(HZ * 8, 256)
        t2[...] = mm(pair, m1).reshape(HZ, 8, 128)
        return t2[:, pl.ds(0, 4, stride=2), :] + t2[:, pl.ds(1, 4, stride=2), :]

    own2 = []
    rows4 = []
    for f, scale in enumerate((1.0, 0.25, 0.25, 1.0)):
        x = down_1(own1[f])
        own2.append((x > 0.0).astype(F32) if f == 3 else scale * x)
        flat = t2.reshape(HZ * 8, 128)
        rows4.append(sum(flat[pl.ds(i, HZ, stride=8), :] for i in range(8)))
    for f in range(4):
        g_p[f * HZ:(f + 1) * HZ] = own2[f]
        for k in range(5):
            q_p[f * 5 + k] = own2[f][k] + roll(own2[f][k + 5], 32, 1)
    sent_q = [copy(q_p, q_rp.at[0], 0, 1), copy(q_p, q_rp.at[1], 0, -1)]

    for f, x in enumerate((own1[0], own1[3] * own1[1], own1[3] * own1[2])):
        pack_1(x, f, p_pk, p_ns, p_nc)
        raw1[f, :, 8:16, :] = x
    sent_p1 = send_1(p_pk, p_ns, p_nc, p_rpk, p_rns, p_rnc)

    def send_z(blk, slots):
        slots[3] = blk[...]
        return [copy(blk, slots.at[3 - d], 0, d) for d in (3, -3, 2, -2, 1, -1)]

    def window_row(slots, count):
        row = jnp.zeros((count, 128), F32)
        for s in range(7):
            inside = (my + (s - 3) >= 0) & (my + (s - 3) < NTY)
            row = row + jnp.where(inside, roll(slots[s], 8 * (s - 3), 1), 0.0)
        return row

    def folded_window_row(slots):
        part = iota((8, 128), 1) & 63
        out = [jnp.zeros((8, 128), F32)] * 3
        for s in range(7):
            inside = (my + (s - 3) >= 0) & (my + (s - 3) < NTY)
            block = jnp.where(inside, slots[s], 0.0)
            for i in range(3):
                pick = (part >= 24 + 8 * i) & (part < 32 + 8 * i)
                out[i] = out[i] + roll(jnp.where(pick, block, 0.0), 8 * (s - 3 - i), 1)
        return jnp.concatenate(out, axis=0)

    def send_plane(row, ev, count):
        own = pl.ds(8 * count, count)
        ev[own, :] = row
        return [
            copy(ev.at[own], ev.at[pl.ds(((8 - k) % 16) * count, count)], 2 * k, 0)
            for k in (10, 6, 9, 7, 11, 5, 2, 14, 8, 3, 13, 1, 15, 4, 12)
        ]

    def send_sibling(ev, od):
        i = counter[0]
        counter[0] += 1
        made = pltpu.make_async_remote_copy(
            src_ref=ev, dst_ref=od, send_sem=send_sem.at[i], recv_sem=recv_sem.at[i],
            device_id=(mx + 1 - 2 * lax.rem(mx, 2), my), device_id_type=MESH,
        )
        made.start()
        pending.append(made)
        return [made]

    def window_slab(ev, od, index, count, put):
        put(pl.ds(0, 16, stride=2), ev[pl.ds(index, 16, stride=count), :])
        other = od[pl.ds(index, 16, stride=count), :]
        put(pl.ds(1, 16, stride=2), jnp.where(odd, roll(other, -1, 0), other))

    arrive(sent_a)
    for f in range(4):
        def put_rows(z):
            raw0[f, z, 16:18, 0:128] = a_rew[0, f * NZ + z]
            raw0[f, z, 22:24, 0:128] = a_rew[1, f * NZ + z]
            if f == 1:
                pick = slice(z % 2, z % 2 + 1)
                raw0[f, z, 18:19, 0:128] = a_rew[0, 4 * NZ + z // 2, pick]
                raw0[f, z, 21:22, 0:128] = a_rew[1, 4 * NZ + z // 2, pick]

        def put_side(z, x):
            raw0[f, z, :, 128:256] = x

        merge_edges(place[f][0], place[f][1], a_rns, a_rd, put_rows, put_side)

    def send_2(p, rp):
        return [copy(p, rp.at[3 - d], d, 0) for d in (3, -3, 2, -2, 1, -1)]

    arrive(sent_q)
    part = iota((4, 128), 1) & 63
    for f in range(4):
        for k in range(HZ):
            south = roll(q_rp[0, f * 5 + k % 5], -32 if k < 5 else -64, 1)
            north = roll(q_rp[1, f * 5 + k % 5], 32 if k < 5 else 0, 1)
            south = jnp.where(has_s, south, 0.0)
            north = jnp.where(has_n, north, 0.0)
            g_p[f * HZ + k] = jnp.where(part < 16, south, jnp.where(part < 48, g_p[f * HZ + k], north))
    sent_p2 = send_2(g_p, g_rp)

    def sea0(z):
        return (raw0[1, z] > 0.0).astype(F32)

    lev0.faces(lambda z: raw0[0, z], lambda z: raw0[1, z], lambda z: raw0[2, z], sea0, UNROLL, lambda z: raw0[3, z])
    lev0.clear_ends()


    lev0.sweep(lev0.c, lev0.w, UNROLL)

    def remain0(z, u, total):
        r = raw0[3, z] - (lev0.d[z] * u - total)
        t0[z] = r[0:16, 0:128]

    lev0.stencil(lev0.w, UNROLL, remain0)
    b1 = down_0(pair_rows(t0, 8))

    arrive(sent_p1)

    def sea_1(z):
        return (raw1[1, z] > 0.0).astype(F32)

    for f in range(3):
        def put1(z, start, x):
            raw1[f, z, start:start + 8, :] = x

        merge_1(f, lambda z: raw1[f, z, 8:16, :], p_rpk, p_rns, p_rnc, put1)
    lev1.faces(lambda z: raw1[0, z], lambda z: raw1[1, z], lambda z: raw1[2, z], sea_1, UNROLL)
    lev1.clear_ends()
    c1 = lev1.g[:, 8:16, :] * b1
    q1[...] = c1
    pack_1(c1, 0, b_pk, b_ns, b_nc)
    sent_b = send_1(b_pk, b_ns, b_nc, b_rpk, b_rns, b_rnc)

    padding = jnp.zeros((16 - HZ, 128), F32)
    every = mm(jnp.concatenate([part for x in rows4 for part in (x, padding)], axis=0), restrict_24())
    sea4 = (every[48:58] > 0.0).astype(F32)
    h_blk[0:10, :] = every[0:10]
    h_blk[10:20, :] = sea4 * every[16:26] * (1.0 / 64)
    h_blk[20:30, :] = sea4 * every[32:42] * (1.0 / 64)
    h_blk[30:32, :] = jnp.zeros((2, 128), F32)

    arrive(sent_p2)
    for f in range(4):
        for s in range(7):
            piece = g_p if s == 3 else g_rp.at[s]
            raw2[f, :, 4 * s:4 * s + 4, :] = piece[f * HZ:(f + 1) * HZ]
        raw2[f, :, 28:32, :] = jnp.zeros((HZ, 4, 128), F32)
    lev2.faces(lambda z: raw2[0, z], lambda z: raw2[1, z], lambda z: raw2[2, z], lambda z: raw2[3, z], UNROLL)

    arrive(sent_b)
    sent_hz = send_z(h_blk, h_z)

    def put1c(z, start, x):
        lev1.c[z + 1, start:start + 8, :] = x

    merge_1(0, lambda z: q1[z], b_rpk, b_rns, b_rnc, put1c)
    lev1.sweep(lev1.c, lev1.w, UNROLL)

    def remain1(z, r):
        q1[z] = r[8:16]

    lev1.remain(lev1.w, UNROLL, remain1)
    b2 = down_1(q1[...])

    f_p[...] = lev2.g[:, 12:16, :] * b2
    sent_c = send_2(f_p, f_rp)

    m2 = restrict_2()

    def down_2(ref):
        return mm(pair_rows(ref, 16).reshape(HZ * 16, 128), m2).reshape(HZ, 16, 128)

    raw3[0] = down_2(raw2.at[0])
    raw3[1] = 0.25 * down_2(raw2.at[1])
    raw3[2] = 0.25 * down_2(raw2.at[2])
    raw3[3] = (down_2(raw2.at[3]) > 0.0).astype(F32)
    lev3.faces(lambda z: raw3[0, z], lambda z: raw3[1, z], lambda z: raw3[2, z], lambda z: raw3[3, z], UNROLL)

    edge_n = jnp.zeros((16, 128), F32)
    edge_s = jnp.zeros((16, 128), F32)
    for z in range(NZ):
        x = lev0.w[z + 1, 0:16, 0:128]
        o_ew[0, z] = x[0:4]
        o_ew[1, z] = x[12:16]
        edge_n = jnp.where(lane16 >= 3 * z, roll(x, 3 * z - 125, 1), edge_n)
        edge_s = jnp.where(lane16 >= 3 * z, roll(x, 3 * z, 1), edge_s)
    o_ns[0, 0] = edge_n
    o_ns[1, 0] = edge_s

    arrive(sent_hz)
    row_h = window_row(h_z, 32)

    arrive(sent_c)
    sent_o = send_edges(o_ew, o_ns, o_rew, o_rns, o_rd)
    sent_hp = send_plane(row_h, h_ev, 32)
    for s in range(7):
        piece = f_p if s == 3 else f_rp.at[s]
        lev2.c[1:HZ + 1, 4 * s:4 * s + 4, :] = piece[...]
    lev2.c[1:HZ + 1, 28:32, :] = jnp.zeros((HZ, 4, 128), F32)
    lev2.wrap(lev2.c)
    lev2.sweep(lev2.c, lev2.w, UNROLL, first=1)

    def remain2(z, r):
        t4[z] = r

    lev2.remain(lev2.w, UNROLL, remain2, 2)

    lev3.c[1:HZ + 1] = lev3.g[...] * down_2(t4)
    lev3.wrap(lev3.c)
    lev3.sweep(lev3.c, lev3.w, UNROLL, first=1)

    def remain3(z, r):
        k_rows[16 * z:16 * z + 16, :] = r

    lev3.remain(lev3.w, UNROLL, remain3, 2)
    own_cell = k_rows[pl.ds(6, HZ, stride=16), :] + k_rows[pl.ds(7, HZ, stride=16), :]
    east_cell = k_rows[pl.ds(8, HZ, stride=16), :] + k_rows[pl.ds(9, HZ, stride=16), :]
    cells = mm(jnp.concatenate([own_cell, padding, east_cell, padding], axis=0), restrict_3())
    last = jnp.concatenate([cells[8:10], cells[24:26], jnp.zeros((4, 128), F32)], axis=0)
    k_blk[...] = cells[0:8] + roll(cells[16:24], 8, 1) + roll(last, 16, 1)
    sent_kz = send_z(k_blk, k_z)

    arrive(sent_o)

    def put_rows0(z):
        lev0.w[z + 1, 16:20, 0:128] = o_rew[0, z]
        lev0.w[z + 1, 20:24, 0:128] = o_rew[1, z]

    def put_side0(z, x):
        lev0.w[z + 1, :, 128:256] = x

    merge_edges(0, 0, o_rns, o_rd, put_rows0, put_side0)
    arrive(sent_hp)
    sent_hs = send_sibling(h_ev, h_od)

    arrive(sent_kz)
    sent_kp = send_plane(folded_window_row(k_z), k_ev, 24)

    arrive(sent_hs)
    for f in range(3):
        for z in range(HZ):
            def put4(rows, x):
                raw4[f, z, rows, :] = x

            window_slab(h_ev, h_od, f * HZ + z, 32, put4)

    def sea_4(z):
        return (raw4[1, z] > 0.0).astype(F32)

    lev4.faces(lambda z: raw4[0, z], lambda z: raw4[1, z], lambda z: raw4[2, z], sea_4, UNROLL)
    group = iota((32, 128), 1) & 32

    def fold(lower, upper):
        return jnp.where(group == 0, roll(lower, -12, 1), roll(upper, 20, 1))

    for k in range(QZ):
        lev5.e[k] = fold(lev4.e[k], lev4.e[k + QZ])
        lev5.n[k] = fold(lev4.n[k], lev4.n[k + QZ])
        lev5.g[k] = fold(lev4.g[k], lev4.g[k + QZ])
        lev5.v[k + 1] = fold(lev4.v[k + 1], lev4.v[k + QZ + 1])
    lev5.v[0] = roll(lev5.v[QZ], 32, 1)

    arrive(sent_kp)
    for z in range(HZ):
        for i in range(2):
            at = 8 * i + z if z < 8 else 16 + 2 * i + z - 8
            lev4.c[z + 1, pl.ds(i, 16, stride=2), :] = k_ev[pl.ds(at, 16, stride=24), :]
    for z in range(HZ):
        lev4.c[z + 1] = lev4.g[z] * lev4.c[z + 1]
    lev4.wrap(lev4.c)
    for k in range(QZ):
        lev5.c[k + 1] = fold(lev4.c[k + 1], lev4.c[k + QZ + 1])
    lev4.sweep(lev4.c, lev4.w, HZ, first=1)

    def four(step, carry):
        for i in range(2):
            lev4.sweep(lev4.w, lev4.u, HZ, first=2 + 2 * i)
            lev4.sweep(lev4.u, lev4.w, HZ, first=3 + 2 * i)
        return carry

    lax.fori_loop(0, 2, four, 0)
    for k in range(QZ):
        lev5.u[k + 1] = fold(lev4.w[k + 1], lev4.w[k + QZ + 1])
    lev5.wrap(lev5.u)
    for i in range(10):
        src, dst = (lev5.u, lev5.w) if i % 2 == 0 else (lev5.w, lev5.u)
        lev5.sweep(src, dst, QZ, slice(None) if i < 5 else slice(8, 24), first=(i + 1) % QZ)

    up = mm(lev5.u[1:QZ + 1, 13:21, :].reshape(QZ * 8, 128), prolong_3()).reshape(QZ, 8, 256)
    for start in range(2):
        t3[0:QZ, pl.ds(start, 8, stride=2), :] = up[:, :, 0:128]
        t3[QZ:HZ, pl.ds(start, 8, stride=2), :] = up[:, :, 128:256]

    def add3(z):
        lev3.w[z + 1] = lev3.w[z + 1] + t3[z, 0:16, :]

    lev3.each(add3, UNROLL)
    lev3.wrap(lev3.w)
    lev3.sweep(lev3.w, lev3.u, UNROLL, first=1)
    lev3.sweep(lev3.u, lev3.w, UNROLL, first=2)

    up = mm(lev3.w[1:HZ + 1].reshape(HZ * 16, 128), prolong_2()).reshape(HZ, 16, 128)
    for start in range(2):
        t3[:, pl.ds(start, 16, stride=2), :] = up

    def add2(z):
        lev2.w[z + 1] = lev2.w[z + 1] + t3[z]

    lev2.each(add2, UNROLL)
    lev2.wrap(lev2.w)
    lev2.sweep(lev2.w, lev2.u, UNROLL, first=1)
    lev2.sweep(lev2.u, lev2.w, UNROLL, first=2)

    t3[:, 0:16, :] = lev2.w[1:HZ + 1, 8:24, :]
    up = mm(t3[:, 0:16, :].reshape(HZ * 16, 128), prolong_1()).reshape(HZ, 16, 256)
    for start in range(2):
        t1[0:HZ, :, :] = up[:, :, 0:128]
        t1[HZ:NZ, :, :] = up[:, :, 128:256]
    for z in range(NZ):
        for start in range(2):
            q = pl.ds(start, 12, stride=2)
            raw1[0, z, q, :] = t1[z, 0:12, :]

    def add1(z):
        lev1.w[z + 1] = lev1.w[z + 1] + raw1[0, z]

    lev1.each(add1, UNROLL)
    lev1.sweep(lev1.w, lev1.u, UNROLL)
    lev1.sweep(lev1.u, lev1.w, UNROLL)

    for z in range(NZ):
        t1[z, 0:8, :] = lev1.w[z + 1, 8:16, :]
        t1[z, 8:10, :] = lev1.w[z + 1, 16:18, :]
        t1[z, 10:12, :] = lev1.w[z + 1, 6:8, :]
        t1[z, 12:16, :] = jnp.zeros((4, 128), F32)
    up = mm(t1[...].reshape(NZ * 16, 128), prolong_0()).reshape(NZ, 16, 256)
    for z in range(NZ):
        for half in range(2):
            part = up[z, 0:12, 128 * half:128 * half + 128]
            for start in range(2):
                raw1[half, z, pl.ds(start, 12, stride=2), :] = part

    def add0(z):
        for half in range(2):
            lanes = slice(128 * half, 128 * half + 128)
            lev0.w[z + 1, :, lanes] = lev0.w[z + 1, :, lanes] + raw1[half, z]

    lev0.each(add0, UNROLL)
    lev0.sweep(lev0.w, lev0.u, UNROLL)
    lev0.sweep(lev0.u, lev0.w, UNROLL)

    def last0(z, u, total):
        r = raw0[3, z] - (lev0.d[z] * u - total)
        sol[z] = u[0:16, 0:128]
        resid[z] = r[0:16, 0:128]

    lev0.stencil(lev0.w, UNROLL, last0)

    for made in pending:
        made.wait_send()


def level_scratch(slabs, rows, lanes):
    def vmem(count):
        return pltpu.VMEM((count, rows, lanes), F32)

    return [vmem(slabs), vmem(slabs), vmem(slabs + 1), vmem(slabs), vmem(slabs), vmem(slabs + 2), vmem(slabs + 2), vmem(slabs + 2)]


def shards(source, kappa_sq, lon_diff, lat_diff, sea_mask):
    def vmem(*shape):
        return pltpu.VMEM(shape, F32)

    scratch = [
        vmem(NZ, 16, 128), vmem(NZ, 16, 128), vmem(NZ, 16, 128), vmem(NZ, 16, 128),
        pltpu.VMEM((NZ, 16, 128), jnp.int32), pltpu.SemaphoreType.DMA((5,)),
        vmem(4, NZ, 24, 256), vmem(8, 128), level_scratch(NZ, 24, 256),
        vmem(3, NZ, 24, 128), level_scratch(NZ, 24, 128),
        vmem(4, HZ, 32, 128), level_scratch(HZ, 32, 128),
        vmem(4, HZ, 16, 128), level_scratch(HZ, 16, 128),
        vmem(3, HZ, 32, 128), level_scratch(HZ, 32, 128), level_scratch(QZ, 32, 128),
        vmem(NZ, 16, 128), vmem(NZ, 16, 128), vmem(HZ, 8, 128), vmem(HZ, 32, 128), vmem(HZ, 32, 128), vmem(NZ, 8, 128),
        vmem(2, 4 * NZ + HZ, 2, 128), vmem(2, 2, 16, 128), vmem(2, 4 * NZ + HZ, 2, 128), vmem(2, 2, 16, 128), vmem(4, 2, 8, 128),
        vmem(HZ, 8, 128), vmem(2, 5, 8, 128), vmem(2, 2, 5, 4, 128),
        vmem(2, HZ, 8, 128), vmem(2, 5, 8, 128), vmem(2, 2, 5, 4, 128),
        vmem(HZ, 4, 128), vmem(7, HZ, 4, 128),
        vmem(HZ * 16, 128), vmem(8, 128), vmem(7, 8, 128), vmem(16 * 24, 128),
        vmem(3 * HZ, 8, 128), vmem(2, 15, 8, 128), vmem(2, 2, 15, 4, 128),
        vmem(2, 3 * HZ, 8, 128), vmem(2, 15, 8, 128), vmem(2, 2, 15, 4, 128),
        vmem(20, 4, 128), vmem(2, 20, 4, 128),
        vmem(4 * HZ, 4, 128), vmem(7, 4 * HZ, 4, 128),
        vmem(32, 128), vmem(7, 32, 128), vmem(16 * 32, 128), vmem(16 * 32, 128),
        vmem(2, NZ, 4, 128), vmem(2, 1, 16, 128), vmem(2, NZ, 4, 128), vmem(2, 1, 16, 128), vmem(4, 1, 8, 128),
        pltpu.SemaphoreType.DMA((96,)), pltpu.SemaphoreType.DMA((96,)),
    ]
    shape = jax.ShapeDtypeStruct(source.shape, F32)
    anywhere = pl.BlockSpec(memory_space=pl.ANY)
    return pl.pallas_call(
        body,
        out_shape=(shape, shape),
        in_specs=[anywhere] * 5,
        out_specs=[pl.BlockSpec(memory_space=pltpu.VMEM)] * 2,
        scratch_shapes=scratch,
        compiler_params=pltpu.CompilerParams(
            collective_id=0, has_side_effects=True, vmem_limit_bytes=54848 * 1024
        ),
    )(source, kappa_sq, lon_diff, lat_diff, sea_mask)

def solution(mesh):
    spec = P(None, "tx", "ty")
    return jax.shard_map(
        shards, mesh=mesh, in_specs=(spec,) * 5, out_specs=(spec, spec), check_vma=False
    )
```

```python
import jax
import jax.numpy as jnp
from jax import lax
from jax.experimental import pallas as pl
from jax.experimental.pallas import tpu as pltpu
from jax.sharding import PartitionSpec as P

NZ = 20
HZ = 10
QZ = 5
NTX = 32
NTY = 16
OMEGA = 0.8
UNROLL = 20
MESH = pl.DeviceIdType.MESH
F32 = jnp.float32

DIAGONALS = ((1, 1), (-1, 1), (1, -1), (-1, -1))


def iota(shape, dim):
    return lax.broadcasted_iota(jnp.int32, shape, dim)


def mm(x, m):
    high = x.astype(jnp.bfloat16)
    low = (x - high.astype(F32)).astype(jnp.bfloat16)
    m = m.astype(jnp.bfloat16)
    return lax.dot_general(
        jnp.concatenate([high, low], axis=1), jnp.concatenate([m, m], axis=0),
        (((1,), (0,)), ((), ())), preferred_element_type=F32,
    )


def roll(x, shift, axis):
    shift = shift % x.shape[axis]
    return x if shift == 0 else pltpu.roll(x, shift, axis)


def one_hot(shape, hit, value=1.0):
    row, col = iota(shape, 0), iota(shape, 1)
    return jnp.where(hit(row, col), F32(value), F32(0.0))


def restrict_0():
    return one_hot((128, 128), lambda n, m: m == 32 + (n >> 1), 0.25)


def restrict_1():
    return one_hot((256, 128), lambda n, m: m == n >> 1, 0.25)


def restrict_2():
    return one_hot((128, 128), lambda n, m: m == (n & 64) + 8 + ((n & 63) >> 1), 0.25)


def restrict_3():
    def hit(n, m):
        q = n & 63
        return (m == (n & 64) + 16 + (q >> 1)) & (q >= 16) & (q < 32)

    return one_hot((128, 128), hit, 0.25)


def restrict_24():
    def hit(n, m):
        q = n & 63
        return (m == (n & 64) + 20 + (q >> 2)) & (q >= 16) & (q < 48)

    return one_hot((128, 128), hit, 1.0 / 16)


def prolong_3():
    def hit(m, n):
        q = n & 63
        return (m == (n & 64) + ((n & 128) >> 2) + 4 + (q >> 1)) & (q < 56)

    return one_hot((128, 256), hit)


def prolong_2():
    return one_hot((128, 128), lambda m, n: m == (n & 64) + 8 + ((n & 63) >> 1))


def prolong_1():
    return one_hot((128, 256), lambda m, n: m == n >> 1)


def prolong_0():
    def hit(m, n):
        rel = jnp.where(n >= 192, n - 256, n)
        return (m == 32 + (rel >> 1)) & (rel < 132) & (rel >= -4)

    return one_hot((128, 256), hit)


class Level:
    def __init__(self, slabs, seam, refs):
        self.slabs = slabs
        self.seam = seam
        self.e, self.n, self.v, self.g, self.d, self.c, self.u, self.w = refs

    def each(self, body, unroll):
        def step(z, carry):
            body(z)
            return carry

        lax.fori_loop(0, self.slabs, step, 0, unroll=min(unroll, self.slabs))

    def wrap(self, ref, rows=slice(None)):
        if self.seam:
            ref[0, rows] = roll(ref[self.slabs, rows], self.seam, 1)
            ref[self.slabs + 1, rows] = roll(ref[1, rows], -self.seam, 1)

    def clear_ends(self):
        if not self.seam:
            for ref in (self.c, self.u, self.w):
                ref[0] = jnp.zeros_like(ref[0])
                ref[self.slabs + 1] = jnp.zeros_like(ref[0])

    def faces(self, kap, lond, latd, sea, unroll, right=None):
        top = self.slabs - 1
        first = sea(0)
        if self.seam:
            low = iota(self.v.shape[1:], 1) < 64
            face_top = jnp.where(low, sea(top) * roll(first, 64, 1), 0.0)
            face_first = roll(face_top, 64, 1)
        else:
            face_top = face_first = jnp.zeros_like(first)
        self.v[0] = face_first

        def slab(z, s, face_below, face_above):
            lw = s * lond(z)
            tw = s * latd(z)
            east = 0.5 * (lw * roll(s, -1, 0) + s * roll(lw, -1, 0))
            north = 0.5 * (tw * roll(s, -1, 1) + s * roll(tw, -1, 1))
            west = roll(east, 1, 0)
            south = roll(north, 1, 1)
            diag = s * kap(z) + (west + east + south + north + face_below + face_above) + (1.0 - s)
            scale = OMEGA / diag
            self.v[z + 1] = face_above
            self.e[z] = east
            self.n[z] = north
            self.d[z] = diag
            self.g[z] = scale
            if right is not None:
                self.c[z + 1] = scale * right(z)

        def step(z, carry):
            s, face_below = carry
            s_above = sea(z + 1)
            face_above = s * s_above
            slab(z, s, face_below, face_above)
            return s_above, face_above

        s, face_below = lax.fori_loop(0, top, step, (first, face_first), unroll=min(unroll, top))
        slab(top, s, face_below, face_top)

    def stencil(self, src, unroll, use, rows=slice(None), first=0):
        def step(z, carry):
            below, u, face_below = carry
            above = src[z + 2, rows]
            face_above = self.v[z + 1, rows]
            e = self.e[z, rows]
            n = self.n[z, rows]
            use(z, u, (
                roll(e * u, 1, 0)
                + e * roll(u, -1, 0)
                + roll(n * u, 1, 1)
                + n * roll(u, -1, 1)
                + face_below * below
                + face_above * above
            ))
            return u, above, face_above

        def start(z):
            return src[z, rows], src[z + 1, rows], self.v[z, rows]

        if self.seam:
            for i in range(self.slabs):
                z = (first + i) % self.slabs
                carry = step(z, start(z) if i == 0 or z == 0 else carry)
        else:
            lax.fori_loop(0, self.slabs, step, start(0), unroll=min(unroll, self.slabs))

    def sweep(self, src, dst, unroll, rows=slice(None), first=0):
        def use(z, u, total):
            new = (1.0 - OMEGA) * u + self.c[z + 1, rows] + self.g[z, rows] * total
            dst[z + 1, rows] = new
            if self.seam and z == 0:
                dst[self.slabs + 1, rows] = roll(new, -self.seam, 1)
            if self.seam and z == self.slabs - 1:
                dst[0, rows] = roll(new, self.seam, 1)

        self.stencil(src, unroll, use, rows, first)

    def remain(self, src, unroll, put, first=0):
        def use(z, u, total):
            put(z, self.d[z] * (1.25 * self.c[z + 1] - u) + total)

        self.stencil(src, unroll, use, first=first)


def pack_edge(slabs, width, base, count):
    lane = iota(slabs[0].shape, 1)
    out = roll(slabs[0], -base, 1)
    for i in range(1, count):
        out = jnp.where(lane >= width * i, roll(slabs[i], width * i - base, 1), out)
    return out


def body(
    source_in, kappa_in, lon_in, lat_in, mask_in,
    sol, resid,
    source, kappa, lon_diff, lat_diff, mask, in_sem,
    raw0, src0, l0, raw1, l1, raw2, l2, raw3, l3, raw4, l4, l5, t0, t1, t2, t3, t4, q1,
    a_ew, a_ns, a_rew, a_rns, a_rd,
    b_pk, b_ns, b_nc, b_rpk, b_rns, b_rnc,
    f_p, f_rp,
    k_rows, k_blk, k_z, k_ev,
    p_pk, p_ns, p_nc, p_rpk, p_rns, p_rnc, q_p, q_rp, g_p, g_rp, h_blk, h_z, h_ev, h_od,
    o_ew, o_ns, o_rew, o_rns, o_rd,
    send_sem, recv_sem,
):
    mx, my = lax.axis_index("tx"), lax.axis_index("ty")
    odd = lax.rem(mx, 2) == 1
    counter = [0]
    pending = []
    places = {}

    def shifted(axis, here, shift, count):
        shift = shift % count
        if (axis, shift) not in places:
            there = here + shift
            places[axis, shift] = jnp.where(there >= count, there - count, there) if shift else here
        return places[axis, shift]

    def device(dx, dy):
        return (shifted(0, mx, dx, NTX), shifted(1, my, dy, NTY))

    def copy(src, dst, dx, dy):
        i = counter[0]
        counter[0] += 1
        made = pltpu.make_async_remote_copy(
            src_ref=src, dst_ref=dst, send_sem=send_sem.at[i], recv_sem=recv_sem.at[i],
            device_id=device(dx, dy),
            device_id_type=MESH,
        )
        made.start()
        pending.append(made)
        return made

    def arrive(copies):
        for made in copies:
            made.wait_recv()

    lev0 = Level(NZ, 0, l0)
    lev1 = Level(NZ, 0, l1)
    lev2 = Level(HZ, 64, l2)
    lev3 = Level(HZ, 64, l3)
    lev4 = Level(HZ, 64, l4)
    lev5 = Level(QZ, 32, l5)

    fetched = [
        pltpu.make_async_copy(src, dst, in_sem.at[i])
        for i, (src, dst) in enumerate((
            (mask_in, mask), (lon_in, lon_diff), (lat_in, lat_diff), (kappa_in, kappa), (source_in, source)
        ))
    ]
    for made in fetched:
        made.start()

    peers = [(2 * k, 0) for k in range(1, 16)] + [(1, 0), (-1, 0), (3, 0), (-3, 0)]
    peers += [(0, d) for d in (1, 2, 3, -1, -2, -3)] + list(DIAGONALS)
    barrier = pltpu.get_barrier_semaphore()
    for dx, dy in peers:
        pl.semaphore_signal(
            barrier, inc=1,
            device_id=device(dx, dy),
            device_id_type=MESH,
        )

    lane16 = iota((16, 128), 1)
    place = ((1, 0), (0, 0), (0, 60), (1, 60))
    edge_n = [jnp.zeros((16, 128), F32)] * 4
    edge_s = [jnp.zeros((16, 128), F32)] * 4
    own0 = (
        lambda z: kappa[z],
        lambda z: mask[z].astype(F32) * lon_diff[z],
        lambda z: mask[z].astype(F32) * lat_diff[z],
        lambda z: source[z],
    )
    for f, needed in ((1, (0, 1)), (2, (2,)), (0, (3,)), (3, (4,))):
        for i in needed:
            fetched[i].wait()
        for z in range(NZ):
            x = own0[f](z)
            raw0[f, z, 0:16, 0:128] = x
            a_ew[0, f * NZ + z] = x[0:2]
            a_ew[1, f * NZ + z] = x[14:16]
            if f == 1:
                a_ew[0, 4 * NZ + z // 2, z % 2:z % 2 + 1] = x[2:3]
                a_ew[1, 4 * NZ + z // 2, z % 2:z % 2 + 1] = x[13:14]
            start = place[f][1] + 3 * z
            edge_n[f] = jnp.where(lane16 >= start, roll(x, start - 125, 1), edge_n[f])
            edge_s[f] = jnp.where(lane16 >= start, roll(x, start, 1), edge_s[f])
    for pair, (f, g) in enumerate(((1, 2), (0, 3))):
        a_ns[0, pair] = jnp.where(lane16 < 60, edge_n[f], edge_n[g])
        a_ns[1, pair] = jnp.where(lane16 < 60, edge_s[f], edge_s[g])

    pl.semaphore_wait(barrier, len(peers))

    def send_edges(ew, ns, rew, rns, rd):
        made = [copy(ns.at[0, :, 8:16, :], rd.at[0], 1, 1)]
        made.append(copy(ns.at[0, :, 0:8, :], rd.at[1], -1, 1))
        made.append(copy(ns.at[1, :, 8:16, :], rd.at[2], 1, -1))
        made.append(copy(ns.at[1, :, 0:8, :], rd.at[3], -1, -1))
        made += [copy(ew.at[0], rew.at[0], -1, 0), copy(ew.at[1], rew.at[1], 1, 0)]
        made += [copy(ns.at[0], rns.at[0], 0, 1), copy(ns.at[1], rns.at[1], 0, -1)]
        return made

    has_s, has_n = my > 0, my < NTY - 1

    def merge_edges(f, base, rns, rd, put_rows, put_side):
        sub = iota((8, 128), 0)
        south = jnp.concatenate([rns[0, f], jnp.where(sub < 4, rd[1, f], rd[0, f])], axis=0)
        north = jnp.concatenate([rns[1, f], jnp.where(sub < 4, rd[3, f], rd[2, f])], axis=0)
        lane = iota((24, 128), 1)
        south = jnp.where(has_s, south, 0.0)
        north = jnp.where(has_n, north, 0.0)
        for z in range(NZ):
            put_rows(z)
            start = base + 3 * z
            side = jnp.where(lane < 3, roll(north, -start, 1), roll(south, 125 - start, 1))
            put_side(z, jnp.where((lane < 3) | (lane >= 125), side, 0.0))

    sent_a = send_edges(a_ew, a_ns, a_rew, a_rns, a_rd)
    for f in range(4):
        for z in range(NZ):
            raw0[f, z, 16:24, 0:128] = jnp.zeros((8, 128), F32)

    m0 = restrict_0()

    def pair_rows(ref, count):
        return ref[:, pl.ds(0, count, stride=2), :] + ref[:, pl.ds(1, count, stride=2), :]

    def down_0(x):
        return mm(x.reshape(NZ * 8, 128), m0).reshape(NZ, 8, 128)

    def pack_1(x, f, pk, ns, nc):
        lane = iota((8, 128), 1)
        for k in range(HZ):
            pk[f * HZ + k] = jnp.where(lane < 64, roll(x[k], -32, 1), roll(x[k + HZ], 32, 1))
        for k in range(5):
            group = [x[k + 5 * j] for j in range(4)]
            for side, base in ((0, 64), (1, 32)):
                edge = pack_edge(group, 32, base, 4)
                ns[side, f * 5 + k] = edge
                nc[side, 0, f * 5 + k] = edge[0:4]
                nc[side, 1, f * 5 + k] = edge[4:8]

    def send_1(pk, ns, nc, rpk, rns, rnc):
        made = [copy(nc.at[0, 1], rnc.at[0, 1], 1, 1)]
        made.append(copy(nc.at[0, 0], rnc.at[0, 0], -1, 1))
        made.append(copy(nc.at[1, 1], rnc.at[1, 1], 1, -1))
        made.append(copy(nc.at[1, 0], rnc.at[1, 0], -1, -1))
        made += [copy(pk, rpk.at[0], -1, 0), copy(pk, rpk.at[1], 1, 0)]
        made += [copy(ns.at[0], rns.at[0], 0, 1), copy(ns.at[1], rns.at[1], 0, -1)]
        return made

    def merge_1(f, own, rpk, rns, rnc, put):
        lane = iota((8, 128), 1)
        blank = jnp.zeros((4, 128), F32)

        def edge(side, i, at):
            if i == 0:
                return rns[side, at]
            if i == 1:
                return jnp.concatenate([rnc[side, 0, at], blank], axis=0)
            return jnp.concatenate([blank, rnc[side, 1, at]], axis=0)

        for z in range(NZ):
            k, shift = (z, 32) if z < HZ else (z - HZ, -32)
            middle = (own(z), roll(rpk[0, f * HZ + k], shift, 1), roll(rpk[1, f * HZ + k], shift, 1))
            for i, start in ((0, 8), (1, 16), (2, 0)):
                south = jnp.where(has_s, roll(edge(0, i, f * 5 + z % 5), -32 * (z // 5), 1), 0.0)
                north = jnp.where(has_n, roll(edge(1, i, f * 5 + z % 5), 96 - 32 * (z // 5), 1), 0.0)
                put(z, start, jnp.where(lane < 32, south, jnp.where(lane < 96, middle[i], north)))

    own1 = [
        down_0(pair_rows(kappa, 8)),
        0.25 * down_0(pair_rows(lon_diff, 8)),
        0.25 * down_0(pair_rows(lat_diff, 8)),
        (down_0(pair_rows(mask, 8).astype(F32)) > 0.0).astype(F32),
    ]

    m1 = restrict_1()

    def down_1(x):
        pair = jnp.concatenate([x[0:HZ], x[HZ:NZ]], axis=2).reshape(HZ * 8, 256)
        t2[...] = mm(pair, m1).reshape(HZ, 8, 128)
        return t2[:, pl.ds(0, 4, stride=2), :] + t2[:, pl.ds(1, 4, stride=2), :]

    own2 = []
    rows4 = []
    for f, scale in enumerate((1.0, 0.25, 0.25, 1.0)):
        x = down_1(own1[f])
        own2.append((x > 0.0).astype(F32) if f == 3 else scale * x)
        flat = t2.reshape(HZ * 8, 128)
        rows4.append(sum(flat[pl.ds(i, HZ, stride=8), :] for i in range(8)))
    for f in range(4):
        g_p[f * HZ:(f + 1) * HZ] = own2[f]
        for k in range(5):
            q_p[f * 5 + k] = own2[f][k] + roll(own2[f][k + 5], 32, 1)
    sent_q = [copy(q_p, q_rp.at[0], 0, 1), copy(q_p, q_rp.at[1], 0, -1)]

    for f, x in enumerate((own1[0], own1[3] * own1[1], own1[3] * own1[2])):
        pack_1(x, f, p_pk, p_ns, p_nc)
        raw1[f, :, 8:16, :] = x
    sent_p1 = send_1(p_pk, p_ns, p_nc, p_rpk, p_rns, p_rnc)

    def send_z(blk, slots):
        slots[3] = blk[...]
        return [copy(blk, slots.at[3 - d], 0, d) for d in (3, -3, 2, -2, 1, -1)]

    def window_row(slots, count):
        row = jnp.zeros((count, 128), F32)
        for s in range(7):
            inside = (my + (s - 3) >= 0) & (my + (s - 3) < NTY)
            row = row + jnp.where(inside, roll(slots[s], 8 * (s - 3), 1), 0.0)
        return row

    def folded_window_row(slots):
        part = iota((8, 128), 1) & 63
        out = [jnp.zeros((8, 128), F32)] * 3
        for s in range(7):
            inside = (my + (s - 3) >= 0) & (my + (s - 3) < NTY)
            block = jnp.where(inside, slots[s], 0.0)
            for i in range(3):
                pick = (part >= 24 + 8 * i) & (part < 32 + 8 * i)
                out[i] = out[i] + roll(jnp.where(pick, block, 0.0), 8 * (s - 3 - i), 1)
        sub = iota((8, 128), 0)
        lane = iota((8, 128), 1)
        spare = (((lane + 11) & 63) < 13)
        rows = []
        for i in range(2):
            ends = jnp.where(sub < 4, out[2][2 * i:2 * i + 1], out[2][2 * i + 1:2 * i + 2])
            pieces = roll(ends, 50, 1)
            for c in range(1, 4):
                pieces = jnp.where((sub & 3) == c, roll(ends, 50 - 13 * c, 1), pieces)
            rows.append(jnp.where(spare, pieces, out[i]))
        return jnp.concatenate(rows, axis=0)

    def send_plane(row, ev, count):
        own = pl.ds(8 * count, count)
        ev[own, :] = row
        return [
            copy(ev.at[own], ev.at[pl.ds(((8 - k) % 16) * count, count)], 2 * k, 0)
            for k in (10, 6, 9, 7, 11, 5, 2, 14, 8, 3, 13, 1, 15, 4, 12)
        ]

    def send_sibling(ev, od):
        i = counter[0]
        counter[0] += 1
        made = pltpu.make_async_remote_copy(
            src_ref=ev, dst_ref=od, send_sem=send_sem.at[i], recv_sem=recv_sem.at[i],
            device_id=(mx + 1 - 2 * lax.rem(mx, 2), my), device_id_type=MESH,
        )
        made.start()
        pending.append(made)
        return [made]

    def window_slab(ev, od, index, count, put):
        put(pl.ds(0, 16, stride=2), ev[pl.ds(index, 16, stride=count), :])
        other = od[pl.ds(index, 16, stride=count), :]
        put(pl.ds(1, 16, stride=2), jnp.where(odd, roll(other, -1, 0), other))

    def send_2(p, rp):
        return [copy(p, rp.at[3 - d], d, 0) for d in (3, -3, 2, -2, 1, -1)]

    arrive(sent_q)
    part = iota((4, 128), 1) & 63
    for f in range(4):
        for k in range(HZ):
            south = roll(q_rp[0, f * 5 + k % 5], -32 if k < 5 else -64, 1)
            north = roll(q_rp[1, f * 5 + k % 5], 32 if k < 5 else 0, 1)
            south = jnp.where(has_s, south, 0.0)
            north = jnp.where(has_n, north, 0.0)
            g_p[f * HZ + k] = jnp.where(part < 16, south, jnp.where(part < 48, g_p[f * HZ + k], north))
    sent_p2 = send_2(g_p, g_rp)

    arrive(sent_a)
    for f in range(4):
        def put_rows(z):
            raw0[f, z, 16:18, 0:128] = a_rew[0, f * NZ + z]
            raw0[f, z, 22:24, 0:128] = a_rew[1, f * NZ + z]
            if f == 1:
                pick = slice(z % 2, z % 2 + 1)
                raw0[f, z, 18:19, 0:128] = a_rew[0, 4 * NZ + z // 2, pick]
                raw0[f, z, 21:22, 0:128] = a_rew[1, 4 * NZ + z // 2, pick]

        def put_side(z, x):
            raw0[f, z, :, 128:256] = x

        merge_edges(place[f][0], place[f][1], a_rns, a_rd, put_rows, put_side)

    def sea0(z):
        return (raw0[1, z] > 0.0).astype(F32)

    lev0.faces(lambda z: raw0[0, z], lambda z: raw0[1, z], lambda z: raw0[2, z], sea0, UNROLL, lambda z: raw0[3, z])
    lev0.clear_ends()


    lev0.sweep(lev0.c, lev0.w, UNROLL)

    def remain0(z, u, total):
        r = raw0[3, z] - (lev0.d[z] * u - total)
        t0[z] = r[0:16, 0:128]

    lev0.stencil(lev0.w, UNROLL, remain0)
    b1 = down_0(pair_rows(t0, 8))

    arrive(sent_p1)

    def sea_1(z):
        return (raw1[1, z] > 0.0).astype(F32)

    for f in range(3):
        def put1(z, start, x):
            raw1[f, z, start:start + 8, :] = x

        merge_1(f, lambda z: raw1[f, z, 8:16, :], p_rpk, p_rns, p_rnc, put1)
    lev1.faces(lambda z: raw1[0, z], lambda z: raw1[1, z], lambda z: raw1[2, z], sea_1, UNROLL)
    lev1.clear_ends()
    c1 = lev1.g[:, 8:16, :] * b1
    q1[...] = c1
    pack_1(c1, 0, b_pk, b_ns, b_nc)
    sent_b = send_1(b_pk, b_ns, b_nc, b_rpk, b_rns, b_rnc)

    padding = jnp.zeros((16 - HZ, 128), F32)
    every = mm(jnp.concatenate([part for x in rows4 for part in (x, padding)], axis=0), restrict_24())
    sea4 = (every[48:58] > 0.0).astype(F32)
    h_blk[0:10, :] = every[0:10]
    h_blk[10:20, :] = sea4 * every[16:26] * (1.0 / 64)
    h_blk[20:30, :] = sea4 * every[32:42] * (1.0 / 64)
    h_blk[30:32, :] = jnp.zeros((2, 128), F32)

    arrive(sent_p2)
    for f in range(4):
        for s in range(7):
            piece = g_p if s == 3 else g_rp.at[s]
            raw2[f, :, 4 * s:4 * s + 4, :] = piece[f * HZ:(f + 1) * HZ]
        raw2[f, :, 28:32, :] = jnp.zeros((HZ, 4, 128), F32)
    lev2.faces(lambda z: raw2[0, z], lambda z: raw2[1, z], lambda z: raw2[2, z], lambda z: raw2[3, z], UNROLL)

    arrive(sent_b)
    sent_hz = send_z(h_blk, h_z)

    def put1c(z, start, x):
        lev1.c[z + 1, start:start + 8, :] = x

    merge_1(0, lambda z: q1[z], b_rpk, b_rns, b_rnc, put1c)
    lev1.sweep(lev1.c, lev1.w, UNROLL)

    def remain1(z, r):
        q1[z] = r[8:16]

    lev1.remain(lev1.w, UNROLL, remain1)
    b2 = down_1(q1[...])

    f_p[...] = lev2.g[:, 12:16, :] * b2
    sent_c = send_2(f_p, f_rp)

    m2 = restrict_2()

    def down_2(ref):
        return mm(pair_rows(ref, 16).reshape(HZ * 16, 128), m2).reshape(HZ, 16, 128)

    raw3[0] = down_2(raw2.at[0])
    raw3[1] = 0.25 * down_2(raw2.at[1])
    raw3[2] = 0.25 * down_2(raw2.at[2])
    raw3[3] = (down_2(raw2.at[3]) > 0.0).astype(F32)
    lev3.faces(lambda z: raw3[0, z], lambda z: raw3[1, z], lambda z: raw3[2, z], lambda z: raw3[3, z], UNROLL)

    edge_n = jnp.zeros((16, 128), F32)
    edge_s = jnp.zeros((16, 128), F32)
    for z in range(NZ):
        x = lev0.w[z + 1, 0:16, 0:128]
        o_ew[0, z] = x[0:4]
        o_ew[1, z] = x[12:16]
        edge_n = jnp.where(lane16 >= 3 * z, roll(x, 3 * z - 125, 1), edge_n)
        edge_s = jnp.where(lane16 >= 3 * z, roll(x, 3 * z, 1), edge_s)
    o_ns[0, 0] = edge_n
    o_ns[1, 0] = edge_s

    arrive(sent_hz)
    row_h = window_row(h_z, 32)

    arrive(sent_c)
    sent_o = send_edges(o_ew, o_ns, o_rew, o_rns, o_rd)
    sent_hp = send_plane(row_h, h_ev, 32)
    for s in range(7):
        piece = f_p if s == 3 else f_rp.at[s]
        lev2.c[1:HZ + 1, 4 * s:4 * s + 4, :] = piece[...]
    lev2.c[1:HZ + 1, 28:32, :] = jnp.zeros((HZ, 4, 128), F32)
    lev2.wrap(lev2.c)
    lev2.sweep(lev2.c, lev2.w, UNROLL, first=1)

    def remain2(z, r):
        t4[z] = r

    lev2.remain(lev2.w, UNROLL, remain2, 2)

    lev3.c[1:HZ + 1] = lev3.g[...] * down_2(t4)
    lev3.wrap(lev3.c)
    lev3.sweep(lev3.c, lev3.w, UNROLL, first=1)

    def remain3(z, r):
        k_rows[16 * z:16 * z + 16, :] = r

    lev3.remain(lev3.w, UNROLL, remain3, 2)
    own_cell = k_rows[pl.ds(6, HZ, stride=16), :] + k_rows[pl.ds(7, HZ, stride=16), :]
    east_cell = k_rows[pl.ds(8, HZ, stride=16), :] + k_rows[pl.ds(9, HZ, stride=16), :]
    cells = mm(jnp.concatenate([own_cell, padding, east_cell, padding], axis=0), restrict_3())
    last = jnp.concatenate([cells[8:10], cells[24:26], jnp.zeros((4, 128), F32)], axis=0)
    k_blk[...] = cells[0:8] + roll(cells[16:24], 8, 1) + roll(last, 16, 1)
    sent_kz = send_z(k_blk, k_z)

    arrive(sent_o)

    def put_rows0(z):
        lev0.w[z + 1, 16:20, 0:128] = o_rew[0, z]
        lev0.w[z + 1, 20:24, 0:128] = o_rew[1, z]

    def put_side0(z, x):
        lev0.w[z + 1, :, 128:256] = x

    merge_edges(0, 0, o_rns, o_rd, put_rows0, put_side0)
    arrive(sent_hp)
    sent_hs = send_sibling(h_ev, h_od)

    arrive(sent_kz)
    sent_kp = send_plane(folded_window_row(k_z), k_ev, 16)

    arrive(sent_hs)
    for f in range(3):
        for z in range(HZ):
            def put4(rows, x):
                raw4[f, z, rows, :] = x

            window_slab(h_ev, h_od, f * HZ + z, 32, put4)

    def sea_4(z):
        return (raw4[1, z] > 0.0).astype(F32)

    lev4.faces(lambda z: raw4[0, z], lambda z: raw4[1, z], lambda z: raw4[2, z], sea_4, UNROLL)
    group = iota((32, 128), 1) & 32

    def fold(lower, upper):
        return jnp.where(group == 0, roll(lower, -12, 1), roll(upper, 20, 1))

    for k in range(QZ):
        lev5.e[k] = fold(lev4.e[k], lev4.e[k + QZ])
        lev5.n[k] = fold(lev4.n[k], lev4.n[k + QZ])
        lev5.g[k] = fold(lev4.g[k], lev4.g[k + QZ])
        lev5.v[k + 1] = fold(lev4.v[k + 1], lev4.v[k + QZ + 1])
    lev5.v[0] = roll(lev5.v[QZ], 32, 1)

    arrive(sent_kp)
    place13 = ((iota((16, 128), 1) & 63) - 3)
    for i in range(2):
        rows = pl.ds(i, 16, stride=2)
        for z in range(8):
            lev4.c[z + 1, rows, :] = k_ev[pl.ds(8 * i + z, 16, stride=16), :]
        for z in range(8, HZ):
            found = jnp.zeros((16, 128), F32)
            for c in range(4):
                piece = roll(k_ev[pl.ds(8 * i + 4 * (z - 8) + c, 16, stride=16), :], 13 * c - 50, 1)
                found = jnp.where((place13 >= 13 * c) & (place13 < 13 * c + 13), piece, found)
            lev4.c[z + 1, rows, :] = found
    for z in range(HZ):
        lev4.c[z + 1] = lev4.g[z] * lev4.c[z + 1]
    lev4.wrap(lev4.c)
    for k in range(QZ):
        lev5.c[k + 1] = fold(lev4.c[k + 1], lev4.c[k + QZ + 1])
    lev4.sweep(lev4.c, lev4.w, HZ, first=1)

    def four(step, carry):
        for i in range(2):
            lev4.sweep(lev4.w, lev4.u, HZ, first=2 + 2 * i)
            lev4.sweep(lev4.u, lev4.w, HZ, first=3 + 2 * i)
        return carry

    lax.fori_loop(0, 2, four, 0)
    for k in range(QZ):
        lev5.u[k + 1] = fold(lev4.w[k + 1], lev4.w[k + QZ + 1])
    lev5.wrap(lev5.u)
    for i in range(10):
        src, dst = (lev5.u, lev5.w) if i % 2 == 0 else (lev5.w, lev5.u)
        lev5.sweep(src, dst, QZ, slice(None) if i < 5 else slice(8, 24), first=(i + 1) % QZ)

    up = mm(lev5.u[1:QZ + 1, 13:21, :].reshape(QZ * 8, 128), prolong_3()).reshape(QZ, 8, 256)
    for start in range(2):
        t3[0:QZ, pl.ds(start, 8, stride=2), :] = up[:, :, 0:128]
        t3[QZ:HZ, pl.ds(start, 8, stride=2), :] = up[:, :, 128:256]

    def add3(z):
        lev3.w[z + 1] = lev3.w[z + 1] + t3[z, 0:16, :]

    lev3.each(add3, UNROLL)
    lev3.wrap(lev3.w)
    lev3.sweep(lev3.w, lev3.u, UNROLL, first=1)
    lev3.sweep(lev3.u, lev3.w, UNROLL, first=2)

    up = mm(lev3.w[1:HZ + 1].reshape(HZ * 16, 128), prolong_2()).reshape(HZ, 16, 128)
    for start in range(2):
        t3[:, pl.ds(start, 16, stride=2), :] = up

    def add2(z):
        lev2.w[z + 1] = lev2.w[z + 1] + t3[z]

    lev2.each(add2, UNROLL)
    lev2.wrap(lev2.w)
    lev2.sweep(lev2.w, lev2.u, UNROLL, first=1)
    lev2.sweep(lev2.u, lev2.w, UNROLL, first=2)

    t3[:, 0:16, :] = lev2.w[1:HZ + 1, 8:24, :]
    up = mm(t3[:, 0:16, :].reshape(HZ * 16, 128), prolong_1()).reshape(HZ, 16, 256)
    for start in range(2):
        t1[0:HZ, :, :] = up[:, :, 0:128]
        t1[HZ:NZ, :, :] = up[:, :, 128:256]
    for z in range(NZ):
        for start in range(2):
            q = pl.ds(start, 12, stride=2)
            raw1[0, z, q, :] = t1[z, 0:12, :]

    def add1(z):
        lev1.w[z + 1] = lev1.w[z + 1] + raw1[0, z]

    lev1.each(add1, UNROLL)
    lev1.sweep(lev1.w, lev1.u, UNROLL)
    lev1.sweep(lev1.u, lev1.w, UNROLL)

    for z in range(NZ):
        t1[z, 0:8, :] = lev1.w[z + 1, 8:16, :]
        t1[z, 8:10, :] = lev1.w[z + 1, 16:18, :]
        t1[z, 10:12, :] = lev1.w[z + 1, 6:8, :]
        t1[z, 12:16, :] = jnp.zeros((4, 128), F32)
    up = mm(t1[...].reshape(NZ * 16, 128), prolong_0()).reshape(NZ, 16, 256)
    for z in range(NZ):
        for half in range(2):
            part = up[z, 0:12, 128 * half:128 * half + 128]
            for start in range(2):
                raw1[half, z, pl.ds(start, 12, stride=2), :] = part

    def add0(z):
        for half in range(2):
            lanes = slice(128 * half, 128 * half + 128)
            lev0.w[z + 1, :, lanes] = lev0.w[z + 1, :, lanes] + raw1[half, z]

    lev0.each(add0, UNROLL)
    lev0.sweep(lev0.w, lev0.u, UNROLL)
    lev0.sweep(lev0.u, lev0.w, UNROLL)

    def last0(z, u, total):
        r = raw0[3, z] - (lev0.d[z] * u - total)
        sol[z] = u[0:16, 0:128]
        resid[z] = r[0:16, 0:128]

    lev0.stencil(lev0.w, UNROLL, last0)

    for made in pending:
        made.wait_send()


def level_scratch(slabs, rows, lanes):
    def vmem(count):
        return pltpu.VMEM((count, rows, lanes), F32)

    return [vmem(slabs), vmem(slabs), vmem(slabs + 1), vmem(slabs), vmem(slabs), vmem(slabs + 2), vmem(slabs + 2), vmem(slabs + 2)]


def shards(source, kappa_sq, lon_diff, lat_diff, sea_mask):
    def vmem(*shape):
        return pltpu.VMEM(shape, F32)

    scratch = [
        vmem(NZ, 16, 128), vmem(NZ, 16, 128), vmem(NZ, 16, 128), vmem(NZ, 16, 128),
        pltpu.VMEM((NZ, 16, 128), jnp.int32), pltpu.SemaphoreType.DMA((5,)),
        vmem(4, NZ, 24, 256), vmem(8, 128), level_scratch(NZ, 24, 256),
        vmem(3, NZ, 24, 128), level_scratch(NZ, 24, 128),
        vmem(4, HZ, 32, 128), level_scratch(HZ, 32, 128),
        vmem(4, HZ, 16, 128), level_scratch(HZ, 16, 128),
        vmem(3, HZ, 32, 128), level_scratch(HZ, 32, 128), level_scratch(QZ, 32, 128),
        vmem(NZ, 16, 128), vmem(NZ, 16, 128), vmem(HZ, 8, 128), vmem(HZ, 32, 128), vmem(HZ, 32, 128), vmem(NZ, 8, 128),
        vmem(2, 4 * NZ + HZ, 2, 128), vmem(2, 2, 16, 128), vmem(2, 4 * NZ + HZ, 2, 128), vmem(2, 2, 16, 128), vmem(4, 2, 8, 128),
        vmem(HZ, 8, 128), vmem(2, 5, 8, 128), vmem(2, 2, 5, 4, 128),
        vmem(2, HZ, 8, 128), vmem(2, 5, 8, 128), vmem(2, 2, 5, 4, 128),
        vmem(HZ, 4, 128), vmem(7, HZ, 4, 128),
        vmem(HZ * 16, 128), vmem(8, 128), vmem(7, 8, 128), vmem(16 * 16, 128),
        vmem(3 * HZ, 8, 128), vmem(2, 15, 8, 128), vmem(2, 2, 15, 4, 128),
        vmem(2, 3 * HZ, 8, 128), vmem(2, 15, 8, 128), vmem(2, 2, 15, 4, 128),
        vmem(20, 4, 128), vmem(2, 20, 4, 128),
        vmem(4 * HZ, 4, 128), vmem(7, 4 * HZ, 4, 128),
        vmem(32, 128), vmem(7, 32, 128), vmem(16 * 32, 128), vmem(16 * 32, 128),
        vmem(2, NZ, 4, 128), vmem(2, 1, 16, 128), vmem(2, NZ, 4, 128), vmem(2, 1, 16, 128), vmem(4, 1, 8, 128),
        pltpu.SemaphoreType.DMA((96,)), pltpu.SemaphoreType.DMA((96,)),
    ]
    shape = jax.ShapeDtypeStruct(source.shape, F32)
    anywhere = pl.BlockSpec(memory_space=pl.ANY)
    return pl.pallas_call(
        body,
        out_shape=(shape, shape),
        in_specs=[anywhere] * 5,
        out_specs=[pl.BlockSpec(memory_space=pltpu.VMEM)] * 2,
        scratch_shapes=scratch,
        compiler_params=pltpu.CompilerParams(
            collective_id=0, has_side_effects=True, vmem_limit_bytes=54848 * 1024
        ),
    )(source, kappa_sq, lon_diff, lat_diff, sea_mask)

def solution(mesh):
    spec = P(None, "tx", "ty")
    return jax.shard_map(
        shards, mesh=mesh, in_specs=(spec,) * 5, out_specs=(spec, spec), check_vma=False
    )
```

```python
import jax
import jax.numpy as jnp
from jax import lax
from jax.experimental import pallas as pl
from jax.experimental.pallas import tpu as pltpu
from jax.sharding import PartitionSpec as P

NZ = 20
HZ = 10
QZ = 5
NTX = 32
NTY = 16
OMEGA = 0.8
UNROLL = 20
MESH = pl.DeviceIdType.MESH
F32 = jnp.float32

DIAGONALS = ((1, 1), (-1, 1), (1, -1), (-1, -1))


def iota(shape, dim):
    return lax.broadcasted_iota(jnp.int32, shape, dim)


def mm(x, m):
    high = x.astype(jnp.bfloat16)
    low = (x - high.astype(F32)).astype(jnp.bfloat16)
    m = m.astype(jnp.bfloat16)
    return lax.dot_general(
        jnp.concatenate([high, low], axis=1), jnp.concatenate([m, m], axis=0),
        (((1,), (0,)), ((), ())), preferred_element_type=F32,
    )


def roll(x, shift, axis):
    shift = shift % x.shape[axis]
    return x if shift == 0 else pltpu.roll(x, shift, axis)


def one_hot(shape, hit, value=1.0):
    row, col = iota(shape, 0), iota(shape, 1)
    return jnp.where(hit(row, col), F32(value), F32(0.0))


def restrict_0():
    return one_hot((128, 128), lambda n, m: m == 32 + (n >> 1), 0.25)


def restrict_1():
    return one_hot((256, 128), lambda n, m: m == n >> 1, 0.25)


def restrict_2():
    return one_hot((128, 128), lambda n, m: m == (n & 64) + 8 + ((n & 63) >> 1), 0.25)


def restrict_3():
    def hit(n, m):
        q = n & 63
        return (m == (n & 64) + 16 + (q >> 1)) & (q >= 16) & (q < 32)

    return one_hot((128, 128), hit, 0.25)


def restrict_24():
    def hit(n, m):
        q = n & 63
        return (m == (n & 64) + 20 + (q >> 2)) & (q >= 16) & (q < 48)

    return one_hot((128, 128), hit, 1.0 / 16)


def prolong_3():
    def hit(m, n):
        q = n & 63
        return (m == (n & 64) + ((n & 128) >> 2) + 4 + (q >> 1)) & (q < 56)

    return one_hot((128, 256), hit)


def prolong_2():
    return one_hot((128, 128), lambda m, n: m == (n & 64) + 8 + ((n & 63) >> 1))


def prolong_1():
    return one_hot((128, 256), lambda m, n: m == n >> 1)


def prolong_0():
    def hit(m, n):
        rel = jnp.where(n >= 192, n - 256, n)
        return (m == 32 + (rel >> 1)) & (rel < 132) & (rel >= -4)

    return one_hot((128, 256), hit)


class Level:
    def __init__(self, slabs, seam, refs):
        self.slabs = slabs
        self.seam = seam
        self.e, self.n, self.v, self.g, self.d, self.c, self.u, self.w = refs

    def each(self, body, unroll):
        def step(z, carry):
            body(z)
            return carry

        lax.fori_loop(0, self.slabs, step, 0, unroll=min(unroll, self.slabs))

    def wrap(self, ref, rows=slice(None)):
        if self.seam:
            ref[0, rows] = roll(ref[self.slabs, rows], self.seam, 1)
            ref[self.slabs + 1, rows] = roll(ref[1, rows], -self.seam, 1)

    def clear_ends(self):
        if not self.seam:
            for ref in (self.c, self.u, self.w):
                ref[0] = jnp.zeros_like(ref[0])
                ref[self.slabs + 1] = jnp.zeros_like(ref[0])

    def faces(self, kap, lond, latd, sea, unroll, right=None):
        top = self.slabs - 1
        first = sea(0)
        if self.seam:
            low = iota(self.v.shape[1:], 1) < 64
            face_top = jnp.where(low, sea(top) * roll(first, 64, 1), 0.0)
            face_first = roll(face_top, 64, 1)
        else:
            face_top = face_first = jnp.zeros_like(first)
        self.v[0] = face_first

        def slab(z, s, face_below, face_above):
            lw = s * lond(z)
            tw = s * latd(z)
            east = 0.5 * (lw * roll(s, -1, 0) + s * roll(lw, -1, 0))
            north = 0.5 * (tw * roll(s, -1, 1) + s * roll(tw, -1, 1))
            west = roll(east, 1, 0)
            south = roll(north, 1, 1)
            diag = s * kap(z) + (west + east + south + north + face_below + face_above) + (1.0 - s)
            scale = OMEGA / diag
            self.v[z + 1] = face_above
            self.e[z] = east
            self.n[z] = north
            self.d[z] = diag
            self.g[z] = scale
            if right is not None:
                self.c[z + 1] = scale * right(z)

        def step(z, carry):
            s, face_below = carry
            s_above = sea(z + 1)
            face_above = s * s_above
            slab(z, s, face_below, face_above)
            return s_above, face_above

        s, face_below = lax.fori_loop(0, top, step, (first, face_first), unroll=min(unroll, top))
        slab(top, s, face_below, face_top)

    def stencil(self, src, unroll, use, rows=slice(None), first=0):
        def step(z, carry):
            below, u, face_below = carry
            above = src[z + 2, rows]
            face_above = self.v[z + 1, rows]
            e = self.e[z, rows]
            n = self.n[z, rows]
            use(z, u, (
                roll(e * u, 1, 0)
                + e * roll(u, -1, 0)
                + roll(n * u, 1, 1)
                + n * roll(u, -1, 1)
                + face_below * below
                + face_above * above
            ))
            return u, above, face_above

        def start(z):
            return src[z, rows], src[z + 1, rows], self.v[z, rows]

        if self.seam:
            for i in range(self.slabs):
                z = (first + i) % self.slabs
                carry = step(z, start(z) if i == 0 or z == 0 else carry)
        else:
            lax.fori_loop(0, self.slabs, step, start(0), unroll=min(unroll, self.slabs))

    def sweep(self, src, dst, unroll, rows=slice(None), first=0):
        def use(z, u, total):
            new = (1.0 - OMEGA) * u + self.c[z + 1, rows] + self.g[z, rows] * total
            dst[z + 1, rows] = new
            if self.seam and z == 0:
                dst[self.slabs + 1, rows] = roll(new, -self.seam, 1)
            if self.seam and z == self.slabs - 1:
                dst[0, rows] = roll(new, self.seam, 1)

        self.stencil(src, unroll, use, rows, first)

    def remain(self, src, unroll, put, first=0):
        def use(z, u, total):
            put(z, self.d[z] * (1.25 * self.c[z + 1] - u) + total)

        self.stencil(src, unroll, use, first=first)


def pack_edge(slabs, width, base, count):
    lane = iota(slabs[0].shape, 1)
    out = roll(slabs[0], -base, 1)
    for i in range(1, count):
        out = jnp.where(lane >= width * i, roll(slabs[i], width * i - base, 1), out)
    return out


def body(
    source_in, kappa_in, lon_in, lat_in, mask_in,
    sol, resid,
    source, kappa, lon_diff, lat_diff, mask, in_sem,
    raw0, src0, l0, raw1, l1, raw2, l2, raw3, l3, raw4, l4, l5, t0, t1, t2, t3, t4, q1,
    a_ew, a_ns, a_rew, a_rns, a_rd,
    b_pk, b_ns, b_nc, b_rpk, b_rns, b_rnc,
    f_p, f_rp,
    k_rows, k_blk, k_z, k_ev,
    p_pk, p_ns, p_nc, p_rpk, p_rns, p_rnc, q_p, q_rp, g_p, g_rp, h_blk, h_z, h_ev, h_od,
    o_ew, o_ns, o_rew, o_rns, o_rd,
    send_sem, recv_sem,
):
    mx, my = lax.axis_index("tx"), lax.axis_index("ty")
    odd = lax.rem(mx, 2) == 1
    counter = [0]
    pending = []
    places = {}

    def shifted(axis, here, shift, count):
        shift = shift % count
        if (axis, shift) not in places:
            there = here + shift
            places[axis, shift] = jnp.where(there >= count, there - count, there) if shift else here
        return places[axis, shift]

    def device(dx, dy):
        return (shifted(0, mx, dx, NTX), shifted(1, my, dy, NTY))

    def copy(src, dst, dx, dy):
        i = counter[0]
        counter[0] += 1
        made = pltpu.make_async_remote_copy(
            src_ref=src, dst_ref=dst, send_sem=send_sem.at[i], recv_sem=recv_sem.at[i],
            device_id=device(dx, dy),
            device_id_type=MESH,
        )
        made.start()
        pending.append(made)
        return made

    def arrive(copies):
        for made in copies:
            made.wait_recv()

    lev0 = Level(NZ, 0, l0)
    lev1 = Level(NZ, 0, l1)
    lev2 = Level(HZ, 64, l2)
    lev3 = Level(HZ, 64, l3)
    lev4 = Level(HZ, 64, l4)
    lev5 = Level(QZ, 32, l5)

    fetched = [
        pltpu.make_async_copy(src, dst, in_sem.at[i])
        for i, (src, dst) in enumerate((
            (mask_in, mask), (lon_in, lon_diff), (lat_in, lat_diff), (kappa_in, kappa), (source_in, source)
        ))
    ]
    for made in fetched:
        made.start()

    peers = [(2 * k, 0) for k in range(1, 16)] + [(1, 0), (-1, 0), (3, 0), (-3, 0)]
    peers += [(0, d) for d in (1, 2, 3, -1, -2, -3)] + list(DIAGONALS)
    barrier = pltpu.get_barrier_semaphore()
    for dx, dy in peers:
        pl.semaphore_signal(
            barrier, inc=1,
            device_id=device(dx, dy),
            device_id_type=MESH,
        )

    lane16 = iota((16, 128), 1)
    place = ((1, 0), (0, 0), (0, 60), (1, 60))
    edge_n = [jnp.zeros((16, 128), F32)] * 4
    edge_s = [jnp.zeros((16, 128), F32)] * 4
    own0 = (
        lambda z: kappa[z],
        lambda z: mask[z].astype(F32) * lon_diff[z],
        lambda z: mask[z].astype(F32) * lat_diff[z],
        lambda z: source[z],
    )
    for f, needed in ((1, (0, 1)), (2, (2,)), (0, (3,)), (3, (4,))):
        for i in needed:
            fetched[i].wait()
        for z in range(NZ):
            x = own0[f](z)
            raw0[f, z, 0:16, 0:128] = x
            a_ew[0, f * NZ + z] = x[0:2]
            a_ew[1, f * NZ + z] = x[14:16]
            if f == 1:
                a_ew[0, 4 * NZ + z // 2, z % 2:z % 2 + 1] = x[2:3]
                a_ew[1, 4 * NZ + z // 2, z % 2:z % 2 + 1] = x[13:14]
            start = place[f][1] + 3 * z
            edge_n[f] = jnp.where(lane16 >= start, roll(x, start - 125, 1), edge_n[f])
            edge_s[f] = jnp.where(lane16 >= start, roll(x, start, 1), edge_s[f])
    for pair, (f, g) in enumerate(((1, 2), (0, 3))):
        a_ns[0, pair] = jnp.where(lane16 < 60, edge_n[f], edge_n[g])
        a_ns[1, pair] = jnp.where(lane16 < 60, edge_s[f], edge_s[g])

    pl.semaphore_wait(barrier, len(peers))

    def send_edges(ew, ns, rew, rns, rd):
        made = [copy(ns.at[0, :, 8:16, :], rd.at[0], 1, 1)]
        made.append(copy(ns.at[0, :, 0:8, :], rd.at[1], -1, 1))
        made.append(copy(ns.at[1, :, 8:16, :], rd.at[2], 1, -1))
        made.append(copy(ns.at[1, :, 0:8, :], rd.at[3], -1, -1))
        made += [copy(ew.at[0], rew.at[0], -1, 0), copy(ew.at[1], rew.at[1], 1, 0)]
        made += [copy(ns.at[0], rns.at[0], 0, 1), copy(ns.at[1], rns.at[1], 0, -1)]
        return made

    has_s, has_n = my > 0, my < NTY - 1

    def merge_edges(f, base, rns, rd, put_rows, put_side):
        sub = iota((8, 128), 0)
        south = jnp.concatenate([rns[0, f], jnp.where(sub < 4, rd[1, f], rd[0, f])], axis=0)
        north = jnp.concatenate([rns[1, f], jnp.where(sub < 4, rd[3, f], rd[2, f])], axis=0)
        lane = iota((24, 128), 1)
        south = jnp.where(has_s, south, 0.0)
        north = jnp.where(has_n, north, 0.0)
        for z in range(NZ):
            put_rows(z)
            start = base + 3 * z
            side = jnp.where(lane < 3, roll(north, -start, 1), roll(south, 125 - start, 1))
            put_side(z, jnp.where((lane < 3) | (lane >= 125), side, 0.0))

    sent_a = send_edges(a_ew, a_ns, a_rew, a_rns, a_rd)
    for f in range(4):
        for z in range(NZ):
            raw0[f, z, 16:24, 0:128] = jnp.zeros((8, 128), F32)

    m0 = restrict_0()

    def pair_rows(ref, count):
        return ref[:, pl.ds(0, count, stride=2), :] + ref[:, pl.ds(1, count, stride=2), :]

    def down_0(x):
        return mm(x.reshape(NZ * 8, 128), m0).reshape(NZ, 8, 128)

    def pack_1(x, f, pk, ns, nc):
        lane = iota((8, 128), 1)
        for k in range(HZ):
            pk[f * HZ + k] = jnp.where(lane < 64, roll(x[k], -32, 1), roll(x[k + HZ], 32, 1))
        for k in range(5):
            group = [x[k + 5 * j] for j in range(4)]
            for side, base in ((0, 64), (1, 32)):
                edge = pack_edge(group, 32, base, 4)
                ns[side, f * 5 + k] = edge
                nc[side, 0, f * 5 + k] = edge[0:4]
                nc[side, 1, f * 5 + k] = edge[4:8]

    def send_1(pk, ns, nc, rpk, rns, rnc):
        made = [copy(nc.at[0, 1], rnc.at[0, 1], 1, 1)]
        made.append(copy(nc.at[0, 0], rnc.at[0, 0], -1, 1))
        made.append(copy(nc.at[1, 1], rnc.at[1, 1], 1, -1))
        made.append(copy(nc.at[1, 0], rnc.at[1, 0], -1, -1))
        made += [copy(pk, rpk.at[0], -1, 0), copy(pk, rpk.at[1], 1, 0)]
        made += [copy(ns.at[0], rns.at[0], 0, 1), copy(ns.at[1], rns.at[1], 0, -1)]
        return made

    def merge_1(f, own, rpk, rns, rnc, put):
        lane = iota((8, 128), 1)
        blank = jnp.zeros((4, 128), F32)

        def edge(side, i, at):
            if i == 0:
                return rns[side, at]
            if i == 1:
                return jnp.concatenate([rnc[side, 0, at], blank], axis=0)
            return jnp.concatenate([blank, rnc[side, 1, at]], axis=0)

        for z in range(NZ):
            k, shift = (z, 32) if z < HZ else (z - HZ, -32)
            middle = (own(z), roll(rpk[0, f * HZ + k], shift, 1), roll(rpk[1, f * HZ + k], shift, 1))
            for i, start in ((0, 8), (1, 16), (2, 0)):
                south = jnp.where(has_s, roll(edge(0, i, f * 5 + z % 5), -32 * (z // 5), 1), 0.0)
                north = jnp.where(has_n, roll(edge(1, i, f * 5 + z % 5), 96 - 32 * (z // 5), 1), 0.0)
                put(z, start, jnp.where(lane < 32, south, jnp.where(lane < 96, middle[i], north)))

    own1 = [
        down_0(pair_rows(kappa, 8)),
        0.25 * down_0(pair_rows(lon_diff, 8)),
        0.25 * down_0(pair_rows(lat_diff, 8)),
        (down_0(pair_rows(mask, 8).astype(F32)) > 0.0).astype(F32),
    ]

    m1 = restrict_1()

    def down_1(x):
        pair = jnp.concatenate([x[0:HZ], x[HZ:NZ]], axis=2).reshape(HZ * 8, 256)
        t2[...] = mm(pair, m1).reshape(HZ, 8, 128)
        return t2[:, pl.ds(0, 4, stride=2), :] + t2[:, pl.ds(1, 4, stride=2), :]

    own2 = []
    rows4 = []
    for f, scale in enumerate((1.0, 0.25, 0.25, 1.0)):
        x = down_1(own1[f])
        own2.append((x > 0.0).astype(F32) if f == 3 else scale * x)
        flat = t2.reshape(HZ * 8, 128)
        rows4.append(sum(flat[pl.ds(i, HZ, stride=8), :] for i in range(8)))
    for f in range(4):
        g_p[f * HZ:(f + 1) * HZ] = own2[f]
        for k in range(5):
            q_p[f * 5 + k] = own2[f][k] + roll(own2[f][k + 5], 32, 1)
    sent_q = [copy(q_p, q_rp.at[0], 0, 1), copy(q_p, q_rp.at[1], 0, -1)]

    for f, x in enumerate((own1[0], own1[3] * own1[1], own1[3] * own1[2])):
        pack_1(x, f, p_pk, p_ns, p_nc)
        raw1[f, :, 8:16, :] = x
    sent_p1 = send_1(p_pk, p_ns, p_nc, p_rpk, p_rns, p_rnc)

    def send_z(blk, slots):
        slots[3] = blk[...]
        return [copy(blk, slots.at[3 - d], 0, d) for d in (3, -3, 2, -2, 1, -1)]

    padding = jnp.zeros((16 - HZ, 128), F32)
    every = mm(jnp.concatenate([part for x in rows4 for part in (x, padding)], axis=0), restrict_24())
    sea4 = (every[48:58] > 0.0).astype(F32)
    h_blk[0:10, :] = every[0:10]
    h_blk[10:20, :] = sea4 * every[16:26] * (1.0 / 64)
    h_blk[20:30, :] = sea4 * every[32:42] * (1.0 / 64)
    h_blk[30:32, :] = jnp.zeros((2, 128), F32)
    sent_hz = send_z(h_blk, h_z)

    def window_row(slots, count):
        row = jnp.zeros((count, 128), F32)
        for s in range(7):
            inside = (my + (s - 3) >= 0) & (my + (s - 3) < NTY)
            row = row + jnp.where(inside, roll(slots[s], 8 * (s - 3), 1), 0.0)
        return row

    def folded_window_row(slots):
        part = iota((8, 128), 1) & 63
        out = [jnp.zeros((8, 128), F32)] * 3
        for s in range(7):
            inside = (my + (s - 3) >= 0) & (my + (s - 3) < NTY)
            block = jnp.where(inside, slots[s], 0.0)
            for i in range(3):
                pick = (part >= 24 + 8 * i) & (part < 32 + 8 * i)
                out[i] = out[i] + roll(jnp.where(pick, block, 0.0), 8 * (s - 3 - i), 1)
        sub = iota((8, 128), 0)
        lane = iota((8, 128), 1)
        spare = (((lane + 11) & 63) < 13)
        rows = []
        for i in range(2):
            ends = jnp.where(sub < 4, out[2][2 * i:2 * i + 1], out[2][2 * i + 1:2 * i + 2])
            pieces = roll(ends, 50, 1)
            for c in range(1, 4):
                pieces = jnp.where((sub & 3) == c, roll(ends, 50 - 13 * c, 1), pieces)
            rows.append(jnp.where(spare, pieces, out[i]))
        return jnp.concatenate(rows, axis=0)

    def send_plane(row, ev, count):
        own = pl.ds(8 * count, count)
        ev[own, :] = row
        return [
            copy(ev.at[own], ev.at[pl.ds(((8 - k) % 16) * count, count)], 2 * k, 0)
            for k in (10, 6, 9, 7, 11, 5, 2, 14, 8, 3, 13, 1, 15, 4, 12)
        ]

    def send_sibling(ev, od):
        i = counter[0]
        counter[0] += 1
        made = pltpu.make_async_remote_copy(
            src_ref=ev, dst_ref=od, send_sem=send_sem.at[i], recv_sem=recv_sem.at[i],
            device_id=(mx + 1 - 2 * lax.rem(mx, 2), my), device_id_type=MESH,
        )
        made.start()
        pending.append(made)
        return [made]

    def window_slab(ev, od, index, count, put):
        put(pl.ds(0, 16, stride=2), ev[pl.ds(index, 16, stride=count), :])
        other = od[pl.ds(index, 16, stride=count), :]
        put(pl.ds(1, 16, stride=2), jnp.where(odd, roll(other, -1, 0), other))

    def send_2(p, rp):
        return [copy(p, rp.at[3 - d], d, 0) for d in (3, -3, 2, -2, 1, -1)]

    arrive(sent_q)
    part = iota((4, 128), 1) & 63
    for f in range(4):
        for k in range(HZ):
            south = roll(q_rp[0, f * 5 + k % 5], -32 if k < 5 else -64, 1)
            north = roll(q_rp[1, f * 5 + k % 5], 32 if k < 5 else 0, 1)
            south = jnp.where(has_s, south, 0.0)
            north = jnp.where(has_n, north, 0.0)
            g_p[f * HZ + k] = jnp.where(part < 16, south, jnp.where(part < 48, g_p[f * HZ + k], north))
    sent_p2 = send_2(g_p, g_rp)

    arrive(sent_a)
    for f in range(4):
        def put_rows(z):
            raw0[f, z, 16:18, 0:128] = a_rew[0, f * NZ + z]
            raw0[f, z, 22:24, 0:128] = a_rew[1, f * NZ + z]
            if f == 1:
                pick = slice(z % 2, z % 2 + 1)
                raw0[f, z, 18:19, 0:128] = a_rew[0, 4 * NZ + z // 2, pick]
                raw0[f, z, 21:22, 0:128] = a_rew[1, 4 * NZ + z // 2, pick]

        def put_side(z, x):
            raw0[f, z, :, 128:256] = x

        merge_edges(place[f][0], place[f][1], a_rns, a_rd, put_rows, put_side)

    def sea0(z):
        return (raw0[1, z] > 0.0).astype(F32)

    lev0.faces(lambda z: raw0[0, z], lambda z: raw0[1, z], lambda z: raw0[2, z], sea0, UNROLL, lambda z: raw0[3, z])
    lev0.clear_ends()


    lev0.sweep(lev0.c, lev0.w, UNROLL)

    def remain0(z, u, total):
        r = raw0[3, z] - (lev0.d[z] * u - total)
        t0[z] = r[0:16, 0:128]

    lev0.stencil(lev0.w, UNROLL, remain0)
    b1 = down_0(pair_rows(t0, 8))

    arrive(sent_p1)

    def sea_1(z):
        return (raw1[1, z] > 0.0).astype(F32)

    for f in range(3):
        def put1(z, start, x):
            raw1[f, z, start:start + 8, :] = x

        merge_1(f, lambda z: raw1[f, z, 8:16, :], p_rpk, p_rns, p_rnc, put1)
    lev1.faces(lambda z: raw1[0, z], lambda z: raw1[1, z], lambda z: raw1[2, z], sea_1, UNROLL)
    lev1.clear_ends()
    c1 = lev1.g[:, 8:16, :] * b1
    q1[...] = c1
    pack_1(c1, 0, b_pk, b_ns, b_nc)
    sent_b = send_1(b_pk, b_ns, b_nc, b_rpk, b_rns, b_rnc)

    arrive(sent_hz)
    sent_hp = send_plane(window_row(h_z, 32), h_ev, 32)

    arrive(sent_p2)
    for f in range(4):
        for s in range(7):
            piece = g_p if s == 3 else g_rp.at[s]
            raw2[f, :, 4 * s:4 * s + 4, :] = piece[f * HZ:(f + 1) * HZ]
        raw2[f, :, 28:32, :] = jnp.zeros((HZ, 4, 128), F32)
    lev2.faces(lambda z: raw2[0, z], lambda z: raw2[1, z], lambda z: raw2[2, z], lambda z: raw2[3, z], UNROLL)

    arrive(sent_b)

    def put1c(z, start, x):
        lev1.c[z + 1, start:start + 8, :] = x

    merge_1(0, lambda z: q1[z], b_rpk, b_rns, b_rnc, put1c)
    lev1.sweep(lev1.c, lev1.w, UNROLL)

    def remain1(z, r):
        q1[z] = r[8:16]

    lev1.remain(lev1.w, UNROLL, remain1)
    b2 = down_1(q1[...])

    f_p[...] = lev2.g[:, 12:16, :] * b2
    sent_c = send_2(f_p, f_rp)

    m2 = restrict_2()

    def down_2(ref):
        return mm(pair_rows(ref, 16).reshape(HZ * 16, 128), m2).reshape(HZ, 16, 128)

    raw3[0] = down_2(raw2.at[0])
    raw3[1] = 0.25 * down_2(raw2.at[1])
    raw3[2] = 0.25 * down_2(raw2.at[2])
    raw3[3] = (down_2(raw2.at[3]) > 0.0).astype(F32)
    lev3.faces(lambda z: raw3[0, z], lambda z: raw3[1, z], lambda z: raw3[2, z], lambda z: raw3[3, z], UNROLL)

    edge_n = jnp.zeros((16, 128), F32)
    edge_s = jnp.zeros((16, 128), F32)
    for z in range(NZ):
        x = lev0.w[z + 1, 0:16, 0:128]
        o_ew[0, z] = x[0:4]
        o_ew[1, z] = x[12:16]
        edge_n = jnp.where(lane16 >= 3 * z, roll(x, 3 * z - 125, 1), edge_n)
        edge_s = jnp.where(lane16 >= 3 * z, roll(x, 3 * z, 1), edge_s)
    o_ns[0, 0] = edge_n
    o_ns[1, 0] = edge_s


    arrive(sent_c)
    sent_o = send_edges(o_ew, o_ns, o_rew, o_rns, o_rd)
    for s in range(7):
        piece = f_p if s == 3 else f_rp.at[s]
        lev2.c[1:HZ + 1, 4 * s:4 * s + 4, :] = piece[...]
    lev2.c[1:HZ + 1, 28:32, :] = jnp.zeros((HZ, 4, 128), F32)
    lev2.wrap(lev2.c)
    lev2.sweep(lev2.c, lev2.w, UNROLL, first=1)

    def remain2(z, r):
        t4[z] = r

    lev2.remain(lev2.w, UNROLL, remain2, 2)

    lev3.c[1:HZ + 1] = lev3.g[...] * down_2(t4)
    lev3.wrap(lev3.c)
    lev3.sweep(lev3.c, lev3.w, UNROLL, first=1)

    def remain3(z, r):
        k_rows[16 * z:16 * z + 16, :] = r

    lev3.remain(lev3.w, UNROLL, remain3, 2)
    own_cell = k_rows[pl.ds(6, HZ, stride=16), :] + k_rows[pl.ds(7, HZ, stride=16), :]
    east_cell = k_rows[pl.ds(8, HZ, stride=16), :] + k_rows[pl.ds(9, HZ, stride=16), :]
    cells = mm(jnp.concatenate([own_cell, padding, east_cell, padding], axis=0), restrict_3())
    last = jnp.concatenate([cells[8:10], cells[24:26], jnp.zeros((4, 128), F32)], axis=0)
    k_blk[...] = cells[0:8] + roll(cells[16:24], 8, 1) + roll(last, 16, 1)
    sent_kz = send_z(k_blk, k_z)

    arrive(sent_hp)
    sent_hs = send_sibling(h_ev, h_od)

    arrive(sent_o)

    def put_rows0(z):
        lev0.w[z + 1, 16:20, 0:128] = o_rew[0, z]
        lev0.w[z + 1, 20:24, 0:128] = o_rew[1, z]

    def put_side0(z, x):
        lev0.w[z + 1, :, 128:256] = x

    merge_edges(0, 0, o_rns, o_rd, put_rows0, put_side0)
    arrive(sent_kz)
    sent_kp = send_plane(folded_window_row(k_z), k_ev, 16)

    arrive(sent_hs)
    for f in range(3):
        for z in range(HZ):
            def put4(rows, x):
                raw4[f, z, rows, :] = x

            window_slab(h_ev, h_od, f * HZ + z, 32, put4)

    def sea_4(z):
        return (raw4[1, z] > 0.0).astype(F32)

    lev4.faces(lambda z: raw4[0, z], lambda z: raw4[1, z], lambda z: raw4[2, z], sea_4, UNROLL)
    group = iota((32, 128), 1) & 32

    def fold(lower, upper):
        return jnp.where(group == 0, roll(lower, -12, 1), roll(upper, 20, 1))

    for k in range(QZ):
        lev5.e[k] = fold(lev4.e[k], lev4.e[k + QZ])
        lev5.n[k] = fold(lev4.n[k], lev4.n[k + QZ])
        lev5.g[k] = fold(lev4.g[k], lev4.g[k + QZ])
        lev5.v[k + 1] = fold(lev4.v[k + 1], lev4.v[k + QZ + 1])
    lev5.v[0] = roll(lev5.v[QZ], 32, 1)

    arrive(sent_kp)
    place13 = ((iota((16, 128), 1) & 63) - 3)
    for i in range(2):
        rows = pl.ds(i, 16, stride=2)
        for z in range(8):
            lev4.c[z + 1, rows, :] = k_ev[pl.ds(8 * i + z, 16, stride=16), :]
        for z in range(8, HZ):
            found = jnp.zeros((16, 128), F32)
            for c in range(4):
                piece = roll(k_ev[pl.ds(8 * i + 4 * (z - 8) + c, 16, stride=16), :], 13 * c - 50, 1)
                found = jnp.where((place13 >= 13 * c) & (place13 < 13 * c + 13), piece, found)
            lev4.c[z + 1, rows, :] = found
    for z in range(HZ):
        lev4.c[z + 1] = lev4.g[z] * lev4.c[z + 1]
    lev4.wrap(lev4.c)
    for k in range(QZ):
        lev5.c[k + 1] = fold(lev4.c[k + 1], lev4.c[k + QZ + 1])
    lev4.sweep(lev4.c, lev4.w, HZ, first=1)

    def four(step, carry):
        for i in range(2):
            lev4.sweep(lev4.w, lev4.u, HZ, first=2 + 2 * i)
            lev4.sweep(lev4.u, lev4.w, HZ, first=3 + 2 * i)
        return carry

    lax.fori_loop(0, 2, four, 0)
    for k in range(QZ):
        lev5.u[k + 1] = fold(lev4.w[k + 1], lev4.w[k + QZ + 1])
    lev5.wrap(lev5.u)
    for i in range(10):
        src, dst = (lev5.u, lev5.w) if i % 2 == 0 else (lev5.w, lev5.u)
        lev5.sweep(src, dst, QZ, slice(None) if i < 5 else slice(8, 24), first=(i + 1) % QZ)

    up = mm(lev5.u[1:QZ + 1, 13:21, :].reshape(QZ * 8, 128), prolong_3()).reshape(QZ, 8, 256)
    for start in range(2):
        t3[0:QZ, pl.ds(start, 8, stride=2), :] = up[:, :, 0:128]
        t3[QZ:HZ, pl.ds(start, 8, stride=2), :] = up[:, :, 128:256]

    def add3(z):
        lev3.w[z + 1] = lev3.w[z + 1] + t3[z, 0:16, :]

    lev3.each(add3, UNROLL)
    lev3.wrap(lev3.w)
    lev3.sweep(lev3.w, lev3.u, UNROLL, first=1)
    lev3.sweep(lev3.u, lev3.w, UNROLL, first=2)

    up = mm(lev3.w[1:HZ + 1].reshape(HZ * 16, 128), prolong_2()).reshape(HZ, 16, 128)
    for start in range(2):
        t3[:, pl.ds(start, 16, stride=2), :] = up

    def add2(z):
        lev2.w[z + 1] = lev2.w[z + 1] + t3[z]

    lev2.each(add2, UNROLL)
    lev2.wrap(lev2.w)
    lev2.sweep(lev2.w, lev2.u, UNROLL, first=1)
    lev2.sweep(lev2.u, lev2.w, UNROLL, first=2)

    t3[:, 0:16, :] = lev2.w[1:HZ + 1, 8:24, :]
    up = mm(t3[:, 0:16, :].reshape(HZ * 16, 128), prolong_1()).reshape(HZ, 16, 256)
    for start in range(2):
        t1[0:HZ, :, :] = up[:, :, 0:128]
        t1[HZ:NZ, :, :] = up[:, :, 128:256]
    for z in range(NZ):
        for start in range(2):
            q = pl.ds(start, 12, stride=2)
            raw1[0, z, q, :] = t1[z, 0:12, :]

    def add1(z):
        lev1.w[z + 1] = lev1.w[z + 1] + raw1[0, z]

    lev1.each(add1, UNROLL)
    lev1.sweep(lev1.w, lev1.u, UNROLL)
    lev1.sweep(lev1.u, lev1.w, UNROLL)

    for z in range(NZ):
        t1[z, 0:8, :] = lev1.w[z + 1, 8:16, :]
        t1[z, 8:10, :] = lev1.w[z + 1, 16:18, :]
        t1[z, 10:12, :] = lev1.w[z + 1, 6:8, :]
        t1[z, 12:16, :] = jnp.zeros((4, 128), F32)
    up = mm(t1[...].reshape(NZ * 16, 128), prolong_0()).reshape(NZ, 16, 256)
    for z in range(NZ):
        for half in range(2):
            part = up[z, 0:12, 128 * half:128 * half + 128]
            for start in range(2):
                raw1[half, z, pl.ds(start, 12, stride=2), :] = part

    def add0(z):
        for half in range(2):
            lanes = slice(128 * half, 128 * half + 128)
            lev0.w[z + 1, :, lanes] = lev0.w[z + 1, :, lanes] + raw1[half, z]

    lev0.each(add0, UNROLL)
    lev0.sweep(lev0.w, lev0.u, UNROLL)
    lev0.sweep(lev0.u, lev0.w, UNROLL)

    def last0(z, u, total):
        r = raw0[3, z] - (lev0.d[z] * u - total)
        sol[z] = u[0:16, 0:128]
        resid[z] = r[0:16, 0:128]

    lev0.stencil(lev0.w, UNROLL, last0)

    for made in pending:
        made.wait_send()


def level_scratch(slabs, rows, lanes):
    def vmem(count):
        return pltpu.VMEM((count, rows, lanes), F32)

    return [vmem(slabs), vmem(slabs), vmem(slabs + 1), vmem(slabs), vmem(slabs), vmem(slabs + 2), vmem(slabs + 2), vmem(slabs + 2)]


def shards(source, kappa_sq, lon_diff, lat_diff, sea_mask):
    def vmem(*shape):
        return pltpu.VMEM(shape, F32)

    scratch = [
        vmem(NZ, 16, 128), vmem(NZ, 16, 128), vmem(NZ, 16, 128), vmem(NZ, 16, 128),
        pltpu.VMEM((NZ, 16, 128), jnp.int32), pltpu.SemaphoreType.DMA((5,)),
        vmem(4, NZ, 24, 256), vmem(8, 128), level_scratch(NZ, 24, 256),
        vmem(3, NZ, 24, 128), level_scratch(NZ, 24, 128),
        vmem(4, HZ, 32, 128), level_scratch(HZ, 32, 128),
        vmem(4, HZ, 16, 128), level_scratch(HZ, 16, 128),
        vmem(3, HZ, 32, 128), level_scratch(HZ, 32, 128), level_scratch(QZ, 32, 128),
        vmem(NZ, 16, 128), vmem(NZ, 16, 128), vmem(HZ, 8, 128), vmem(HZ, 32, 128), vmem(HZ, 32, 128), vmem(NZ, 8, 128),
        vmem(2, 4 * NZ + HZ, 2, 128), vmem(2, 2, 16, 128), vmem(2, 4 * NZ + HZ, 2, 128), vmem(2, 2, 16, 128), vmem(4, 2, 8, 128),
        vmem(HZ, 8, 128), vmem(2, 5, 8, 128), vmem(2, 2, 5, 4, 128),
        vmem(2, HZ, 8, 128), vmem(2, 5, 8, 128), vmem(2, 2, 5, 4, 128),
        vmem(HZ, 4, 128), vmem(7, HZ, 4, 128),
        vmem(HZ * 16, 128), vmem(8, 128), vmem(7, 8, 128), vmem(16 * 16, 128),
        vmem(3 * HZ, 8, 128), vmem(2, 15, 8, 128), vmem(2, 2, 15, 4, 128),
        vmem(2, 3 * HZ, 8, 128), vmem(2, 15, 8, 128), vmem(2, 2, 15, 4, 128),
        vmem(20, 4, 128), vmem(2, 20, 4, 128),
        vmem(4 * HZ, 4, 128), vmem(7, 4 * HZ, 4, 128),
        vmem(32, 128), vmem(7, 32, 128), vmem(16 * 32, 128), vmem(16 * 32, 128),
        vmem(2, NZ, 4, 128), vmem(2, 1, 16, 128), vmem(2, NZ, 4, 128), vmem(2, 1, 16, 128), vmem(4, 1, 8, 128),
        pltpu.SemaphoreType.DMA((96,)), pltpu.SemaphoreType.DMA((96,)),
    ]
    shape = jax.ShapeDtypeStruct(source.shape, F32)
    anywhere = pl.BlockSpec(memory_space=pl.ANY)
    return pl.pallas_call(
        body,
        out_shape=(shape, shape),
        in_specs=[anywhere] * 5,
        out_specs=[pl.BlockSpec(memory_space=pltpu.VMEM)] * 2,
        scratch_shapes=scratch,
        compiler_params=pltpu.CompilerParams(
            collective_id=0, has_side_effects=True, vmem_limit_bytes=54848 * 1024
        ),
    )(source, kappa_sq, lon_diff, lat_diff, sea_mask)

def solution(mesh):
    spec = P(None, "tx", "ty")
    return jax.shard_map(
        shards, mesh=mesh, in_specs=(spec,) * 5, out_specs=(spec, spec), check_vma=False
    )
```

```python
import jax
import jax.numpy as jnp
from jax import lax
from jax.experimental import pallas as pl
from jax.experimental.pallas import tpu as pltpu
from jax.sharding import PartitionSpec as P

NZ = 20
HZ = 10
NTX = 32
NTY = 16
OMEGA = 0.8
UNROLL = 20
MESH = pl.DeviceIdType.MESH
F32 = jnp.float32

DIAGONALS = ((1, 1), (-1, 1), (1, -1), (-1, -1))


def iota(shape, dim):
    return lax.broadcasted_iota(jnp.int32, shape, dim)


def mm(x, m):
    high = x.astype(jnp.bfloat16)
    low = (x - high.astype(F32)).astype(jnp.bfloat16)
    m = m.astype(jnp.bfloat16)
    return lax.dot_general(
        jnp.concatenate([high, low], axis=1), jnp.concatenate([m, m], axis=0),
        (((1,), (0,)), ((), ())), preferred_element_type=F32,
    )


def roll(x, shift, axis):
    shift = shift % x.shape[axis]
    return x if shift == 0 else pltpu.roll(x, shift, axis)


def one_hot(shape, hit, value=1.0):
    row, col = iota(shape, 0), iota(shape, 1)
    return jnp.where(hit(row, col), F32(value), F32(0.0))


def restrict_0():
    return one_hot((128, 128), lambda n, m: m == 32 + (n >> 1), 0.25)


def restrict_1():
    return one_hot((256, 128), lambda n, m: m == n >> 1, 0.25)


def restrict_2():
    return one_hot((128, 128), lambda n, m: m == (n & 64) + 8 + ((n & 63) >> 1), 0.25)


def restrict_3():
    def hit(n, m):
        q = n & 63
        return (m == (n & 64) + 16 + (q >> 1)) & (q >= 16) & (q < 32)

    return one_hot((128, 128), hit, 0.25)


def restrict_all():
    return one_hot((256, 128), lambda n, m: m == ((n & 128) >> 1) + 24 + ((n & 127) >> 4), 1.0 / 256)


def prolong_3():
    return one_hot((128, 128), lambda m, n: m == (n & 64) + 16 + ((n & 63) >> 1))


def prolong_2():
    return one_hot((128, 128), lambda m, n: m == (n & 64) + 8 + ((n & 63) >> 1))


def prolong_1():
    return one_hot((128, 256), lambda m, n: m == n >> 1)


def prolong_0():
    def hit(m, n):
        rel = jnp.where(n >= 192, n - 256, n)
        return (m == 32 + (rel >> 1)) & (rel < 132) & (rel >= -4)

    return one_hot((128, 256), hit)


class Level:
    def __init__(self, slabs, folded, refs):
        self.slabs = slabs
        self.folded = folded
        self.e, self.n, self.v, self.g, self.d, self.c, self.u, self.w = refs

    def each(self, body, unroll):
        def step(z, carry):
            body(z)
            return carry

        lax.fori_loop(0, self.slabs, step, 0, unroll=min(unroll, self.slabs))

    def wrap(self, ref, rows=slice(None)):
        if self.folded:
            ref[0, rows] = roll(ref[self.slabs, rows], 64, 1)
            ref[self.slabs + 1, rows] = roll(ref[1, rows], 64, 1)

    def clear_ends(self):
        if not self.folded:
            for ref in (self.u, self.w):
                ref[0] = jnp.zeros_like(ref[0])
                ref[self.slabs + 1] = jnp.zeros_like(ref[0])

    def faces(self, kap, lond, latd, sea, unroll):
        top = self.slabs - 1

        def vertical(z):
            here = sea(z)
            self.v[z + 1] = here * sea(z + 1)

        lax.fori_loop(0, top, lambda z, c: (vertical(z), c)[1], 0, unroll=min(unroll, top))
        if self.folded:
            low = iota(self.v.shape[1:], 1) < 64
            self.v[self.slabs] = jnp.where(low, sea(top) * roll(sea(0), 64, 1), 0.0)
            self.v[0] = roll(self.v[self.slabs], 64, 1)
        else:
            self.v[0] = jnp.zeros_like(self.v[0])
            self.v[self.slabs] = jnp.zeros_like(self.v[0])

        def horizontal(z):
            s = sea(z)
            lw = s * lond(z)
            tw = s * latd(z)
            east = 0.5 * (lw * roll(s, -1, 0) + s * roll(lw, -1, 0))
            north = 0.5 * (tw * roll(s, -1, 1) + s * roll(tw, -1, 1))
            west = roll(east, 1, 0)
            south = roll(north, 1, 1)
            diag = s * kap(z) + (west + east + south + north + self.v[z] + self.v[z + 1]) + (1.0 - s)
            self.e[z] = east
            self.n[z] = north
            self.d[z] = diag
            guess = pl.reciprocal(diag, approx=True)
            self.g[z] = guess * (2.0 * OMEGA - OMEGA * (diag * guess))

        self.each(horizontal, unroll)

    def stencil(self, src, unroll, use, rows=slice(None)):
        def step(z, carry):
            below, u, face_below = carry
            above = src[z + 2, rows]
            face_above = self.v[z + 1, rows]
            e = self.e[z, rows]
            n = self.n[z, rows]
            use(z, u, (
                roll(e * u, 1, 0)
                + e * roll(u, -1, 0)
                + roll(n * u, 1, 1)
                + n * roll(u, -1, 1)
                + face_below * below
                + face_above * above
            ))
            return u, above, face_above

        lax.fori_loop(0, self.slabs, step, (src[0, rows], src[1, rows], self.v[0, rows]), unroll=min(unroll, self.slabs))

    def sweep(self, src, dst, unroll, rows=slice(None)):
        def use(z, u, total):
            dst[z + 1, rows] = (1.0 - OMEGA) * u + self.c[z, rows] + self.g[z, rows] * total

        self.stencil(src, unroll, use, rows)
        self.wrap(dst, rows)

    def start(self, unroll):
        def body(z):
            self.u[z + 1] = self.c[z]

        self.each(body, unroll)
        self.wrap(self.u)

    def remain(self, src, unroll, put):
        self.stencil(src, unroll, lambda z, u, total: put(z, self.d[z] * (1.25 * self.c[z] - u) + total))


def pack_edge(slabs, width, base, count):
    lane = iota(slabs[0].shape, 1)
    out = roll(slabs[0], -base, 1)
    for i in range(1, count):
        out = jnp.where(lane >= width * i, roll(slabs[i], width * i - base, 1), out)
    return out


def body(
    source_in, kappa_in, lon_in, lat_in, mask_in,
    sol, resid,
    source, kappa, lon_diff, lat_diff, mask, in_sem,
    raw0, src0, l0, raw1, l1, raw2, l2, raw3, l3, raw4, l4, t0, t1, t2, t3, t4, q1,
    a_ew, a_ns, a_rew, a_rns, a_rd,
    b_pk, b_ns, b_nc, b_rpk, b_rns, b_rnc,
    f_p, f_rp,
    k_blk, k_z, k_ev,
    p_pk, p_ns, p_nc, p_rpk, p_rns, p_rnc, q_p, q_rp, g_p, g_rp, h_blk, h_z, h_ev, h_od,
    o_ew, o_ns, o_rew, o_rns, o_rd,
    send_sem, recv_sem,
):
    mx, my = lax.axis_index("tx"), lax.axis_index("ty")
    odd = lax.rem(mx, 2) == 1
    counter = [0]
    pending = []
    places = {}

    def shifted(axis, here, shift, count):
        shift = shift % count
        if (axis, shift) not in places:
            there = here + shift
            places[axis, shift] = jnp.where(there >= count, there - count, there) if shift else here
        return places[axis, shift]

    def device(dx, dy):
        return (shifted(0, mx, dx, NTX), shifted(1, my, dy, NTY))

    def copy(src, dst, dx, dy):
        i = counter[0]
        counter[0] += 1
        made = pltpu.make_async_remote_copy(
            src_ref=src, dst_ref=dst, send_sem=send_sem.at[i], recv_sem=recv_sem.at[i],
            device_id=device(dx, dy),
            device_id_type=MESH,
        )
        made.start()
        pending.append(made)
        return made

    def arrive(copies):
        for made in copies:
            made.wait_recv()

    lev0 = Level(NZ, False, l0)
    lev1 = Level(NZ, False, l1)
    lev2 = Level(HZ, True, l2)
    lev3 = Level(HZ, True, l3)
    lev4 = Level(HZ, True, l4)

    fetched = [
        pltpu.make_async_copy(src, dst, in_sem.at[i])
        for i, (src, dst) in enumerate((
            (mask_in, mask), (lon_in, lon_diff), (lat_in, lat_diff), (kappa_in, kappa), (source_in, source)
        ))
    ]
    for made in fetched:
        made.start()

    peers = list(DIAGONALS) + [(1, 0), (-1, 0), (0, 1), (0, -1)]
    peers += [(3, 0), (-3, 0)] + [(0, d) for d in (2, 3, -2, -3)] + [(2 * k, 0) for k in range(1, 16)]
    barrier = pltpu.get_barrier_semaphore()
    for dx, dy in peers:
        pl.semaphore_signal(
            barrier, inc=1,
            device_id=device(dx, dy),
            device_id_type=MESH,
        )

    lane16 = iota((16, 128), 1)
    place = ((1, 0), (0, 0), (0, 60), (1, 60))
    edge_n = [jnp.zeros((16, 128), F32)] * 4
    edge_s = [jnp.zeros((16, 128), F32)] * 4
    own0 = (
        lambda z: kappa[z],
        lambda z: mask[z].astype(F32) * lon_diff[z],
        lambda z: mask[z].astype(F32) * lat_diff[z],
        lambda z: source[z],
    )
    for f, needed in ((1, (0, 1)), (2, (2,)), (0, (3,)), (3, (4,))):
        for i in needed:
            fetched[i].wait()
        for z in range(NZ):
            x = own0[f](z)
            raw0[f, z, 0:16, 0:128] = x
            a_ew[0, f * NZ + z] = x[0:2]
            a_ew[1, f * NZ + z] = x[14:16]
            if f == 1:
                a_ew[0, 4 * NZ + z // 2, z % 2:z % 2 + 1] = x[2:3]
                a_ew[1, 4 * NZ + z // 2, z % 2:z % 2 + 1] = x[13:14]
            start = place[f][1] + 3 * z
            edge_n[f] = jnp.where(lane16 >= start, roll(x, start - 125, 1), edge_n[f])
            edge_s[f] = jnp.where(lane16 >= start, roll(x, start, 1), edge_s[f])
    for pair, (f, g) in enumerate(((1, 2), (0, 3))):
        a_ns[0, pair] = jnp.where(lane16 < 60, edge_n[f], edge_n[g])
        a_ns[1, pair] = jnp.where(lane16 < 60, edge_s[f], edge_s[g])

    pl.semaphore_wait(barrier, len(peers))

    def send_edges(ew, ns, rew, rns, rd):
        made = [copy(ns.at[0, :, 8:16, :], rd.at[0], 1, 1)]
        made.append(copy(ns.at[0, :, 0:8, :], rd.at[1], -1, 1))
        made.append(copy(ns.at[1, :, 8:16, :], rd.at[2], 1, -1))
        made.append(copy(ns.at[1, :, 0:8, :], rd.at[3], -1, -1))
        made += [copy(ew.at[0], rew.at[0], -1, 0), copy(ew.at[1], rew.at[1], 1, 0)]
        made += [copy(ns.at[0], rns.at[0], 0, 1), copy(ns.at[1], rns.at[1], 0, -1)]
        return made

    has_s, has_n = my > 0, my < NTY - 1

    def merge_edges(f, base, rns, rd, put_rows, put_side):
        sub = iota((8, 128), 0)
        south = jnp.concatenate([rns[0, f], jnp.where(sub < 4, rd[1, f], rd[0, f])], axis=0)
        north = jnp.concatenate([rns[1, f], jnp.where(sub < 4, rd[3, f], rd[2, f])], axis=0)
        lane = iota((24, 128), 1)
        south = jnp.where(has_s, south, 0.0)
        north = jnp.where(has_n, north, 0.0)
        for z in range(NZ):
            put_rows(z)
            start = base + 3 * z
            side = jnp.where(lane < 3, roll(north, -start, 1), roll(south, 125 - start, 1))
            put_side(z, jnp.where((lane < 3) | (lane >= 125), side, 0.0))

    sent_a = send_edges(a_ew, a_ns, a_rew, a_rns, a_rd)
    for f in range(4):
        for z in range(NZ):
            raw0[f, z, 16:24, 0:128] = jnp.zeros((8, 128), F32)

    m0 = restrict_0()

    def down_0(x):
        t1[...] = mm(x.reshape(NZ * 16, 128), m0).reshape(NZ, 16, 128)
        return t1[:, pl.ds(0, 8, stride=2), :] + t1[:, pl.ds(1, 8, stride=2), :]

    def pack_1(x, f, pk, ns, nc):
        lane = iota((8, 128), 1)
        for k in range(HZ):
            pk[f * HZ + k] = jnp.where(lane < 64, roll(x[k], -32, 1), roll(x[k + HZ], 32, 1))
        for k in range(5):
            group = [x[k + 5 * j] for j in range(4)]
            for side, base in ((0, 64), (1, 32)):
                edge = pack_edge(group, 32, base, 4)
                ns[side, f * 5 + k] = edge
                nc[side, 0, f * 5 + k] = edge[0:4]
                nc[side, 1, f * 5 + k] = edge[4:8]

    def send_1(pk, ns, nc, rpk, rns, rnc):
        made = [copy(nc.at[0, 1], rnc.at[0, 1], 1, 1)]
        made.append(copy(nc.at[0, 0], rnc.at[0, 0], -1, 1))
        made.append(copy(nc.at[1, 1], rnc.at[1, 1], 1, -1))
        made.append(copy(nc.at[1, 0], rnc.at[1, 0], -1, -1))
        made += [copy(pk, rpk.at[0], -1, 0), copy(pk, rpk.at[1], 1, 0)]
        made += [copy(ns.at[0], rns.at[0], 0, 1), copy(ns.at[1], rns.at[1], 0, -1)]
        return made

    def merge_1(f, own, rpk, rns, rnc, put):
        lane = iota((8, 128), 1)
        blank = jnp.zeros((4, 128), F32)

        def edge(side, i, at):
            if i == 0:
                return rns[side, at]
            if i == 1:
                return jnp.concatenate([rnc[side, 0, at], blank], axis=0)
            return jnp.concatenate([blank, rnc[side, 1, at]], axis=0)

        for z in range(NZ):
            k, shift = (z, 32) if z < HZ else (z - HZ, -32)
            middle = (own(z), roll(rpk[0, f * HZ + k], shift, 1), roll(rpk[1, f * HZ + k], shift, 1))
            for i, start in ((0, 8), (1, 16), (2, 0)):
                south = jnp.where(has_s, roll(edge(0, i, f * 5 + z % 5), -32 * (z // 5), 1), 0.0)
                north = jnp.where(has_n, roll(edge(1, i, f * 5 + z % 5), 96 - 32 * (z // 5), 1), 0.0)
                put(z, start, jnp.where(lane < 32, south, jnp.where(lane < 96, middle[i], north)))

    own1 = [
        down_0(kappa[...]),
        0.25 * down_0(lon_diff[...]),
        0.25 * down_0(lat_diff[...]),
        (down_0(mask[...].astype(F32)) > 0.0).astype(F32),
    ]

    m1 = restrict_1()

    def down_1(x):
        pair = jnp.concatenate([x[0:HZ], x[HZ:NZ]], axis=2).reshape(HZ * 8, 256)
        t2[...] = mm(pair, m1).reshape(HZ, 8, 128)
        return t2[:, pl.ds(0, 4, stride=2), :] + t2[:, pl.ds(1, 4, stride=2), :]

    own2 = [
        down_1(own1[0]),
        0.25 * down_1(own1[1]),
        0.25 * down_1(own1[2]),
        (down_1(own1[3]) > 0.0).astype(F32),
    ]
    for f in range(4):
        g_p[f * HZ:(f + 1) * HZ] = own2[f]
        for k in range(5):
            q_p[f * 5 + k] = own2[f][k] + roll(own2[f][k + 5], 32, 1)
    sent_q = [copy(q_p, q_rp.at[0], 0, 1), copy(q_p, q_rp.at[1], 0, -1)]

    for f, x in enumerate((own1[0], own1[3] * own1[1], own1[3] * own1[2])):
        pack_1(x, f, p_pk, p_ns, p_nc)
        raw1[f, :, 8:16, :] = x
    sent_p1 = send_1(p_pk, p_ns, p_nc, p_rpk, p_rns, p_rnc)

    def send_z(blk, slots):
        slots[3] = blk[...]
        return [copy(blk, slots.at[3 - d], 0, d) for d in (3, -3, 2, -2, 1, -1)]

    def window_row(slots, count):
        row = jnp.zeros((count, 128), F32)
        for s in range(7):
            inside = (my + (s - 3) >= 0) & (my + (s - 3) < NTY)
            row = row + jnp.where(inside, roll(slots[s], 8 * (s - 3), 1), 0.0)
        return row

    def folded_window_row(slots):
        part = iota((8, 128), 1) & 63
        out = [jnp.zeros((8, 128), F32)] * 3
        for s in range(7):
            inside = (my + (s - 3) >= 0) & (my + (s - 3) < NTY)
            block = jnp.where(inside, slots[s], 0.0)
            for i in range(3):
                pick = (part >= 24 + 8 * i) & (part < 32 + 8 * i)
                out[i] = out[i] + roll(jnp.where(pick, block, 0.0), 8 * (s - 3 - i), 1)
        return jnp.concatenate(out, axis=0)

    def send_plane(row, ev, count):
        own = pl.ds(8 * count, count)
        ev[own, :] = row
        return [
            copy(ev.at[own], ev.at[pl.ds(((8 - k) % 16) * count, count)], 2 * k, 0)
            for k in (10, 6, 9, 7, 11, 5, 2, 14, 8, 3, 13, 1, 15, 4, 12)
        ]

    def send_sibling(ev, od):
        i = counter[0]
        counter[0] += 1
        made = pltpu.make_async_remote_copy(
            src_ref=ev, dst_ref=od, send_sem=send_sem.at[i], recv_sem=recv_sem.at[i],
            device_id=(mx + 1 - 2 * lax.rem(mx, 2), my), device_id_type=MESH,
        )
        made.start()
        pending.append(made)
        return [made]

    def window_slab(ev, od, index, count, put):
        put(pl.ds(0, 16, stride=2), ev[pl.ds(index, 16, stride=count), :])
        other = od[pl.ds(index, 16, stride=count), :]
        put(pl.ds(1, 16, stride=2), jnp.where(odd, roll(other, -1, 0), other))

    arrive(sent_a)
    for f in range(4):
        def put_rows(z):
            raw0[f, z, 16:18, 0:128] = a_rew[0, f * NZ + z]
            raw0[f, z, 22:24, 0:128] = a_rew[1, f * NZ + z]
            if f == 1:
                pick = slice(z % 2, z % 2 + 1)
                raw0[f, z, 18:19, 0:128] = a_rew[0, 4 * NZ + z // 2, pick]
                raw0[f, z, 21:22, 0:128] = a_rew[1, 4 * NZ + z // 2, pick]

        def put_side(z, x):
            raw0[f, z, :, 128:256] = x

        merge_edges(place[f][0], place[f][1], a_rns, a_rd, put_rows, put_side)

    def send_2(p, rp):
        return [copy(p, rp.at[3 - d], d, 0) for d in (3, -3, 2, -2, 1, -1)]

    arrive(sent_q)
    part = iota((4, 128), 1) & 63
    for f in range(4):
        for k in range(HZ):
            south = roll(q_rp[0, f * 5 + k % 5], -32 if k < 5 else -64, 1)
            north = roll(q_rp[1, f * 5 + k % 5], 32 if k < 5 else 0, 1)
            south = jnp.where(has_s, south, 0.0)
            north = jnp.where(has_n, north, 0.0)
            g_p[f * HZ + k] = jnp.where(part < 16, south, jnp.where(part < 48, g_p[f * HZ + k], north))
    sent_p2 = send_2(g_p, g_rp)

    def sea0(z):
        return (raw0[1, z] > 0.0).astype(F32)

    lev0.faces(lambda z: raw0[0, z], lambda z: raw0[1, z], lambda z: raw0[2, z], sea0, UNROLL)
    lev0.clear_ends()


    def first0(z):
        c = lev0.g[z] * raw0[3, z]
        lev0.c[z] = c
        lev0.u[z + 1] = c

    lev0.each(first0, UNROLL)
    lev0.sweep(lev0.u, lev0.w, UNROLL)

    def remain0(z, u, total):
        r = raw0[3, z] - (lev0.d[z] * u - total)
        t0[z] = r[0:16, 0:128]

    lev0.stencil(lev0.w, UNROLL, remain0)
    b1 = down_0(t0[...])

    arrive(sent_p1)
    for f in range(3):
        def put1(z, start, x):
            raw1[f, z, start:start + 8, :] = x

        merge_1(f, lambda z: raw1[f, z, 8:16, :], p_rpk, p_rns, p_rnc, put1)

    def sea_1(z):
        return (raw1[1, z] > 0.0).astype(F32)

    lev1.faces(lambda z: raw1[0, z], lambda z: raw1[1, z], lambda z: raw1[2, z], sea_1, UNROLL)
    lev1.clear_ends()
    c1 = lev1.g[:, 8:16, :] * b1
    q1[...] = c1
    pack_1(c1, 0, b_pk, b_ns, b_nc)
    sent_b = send_1(b_pk, b_ns, b_nc, b_rpk, b_rns, b_rnc)

    edge_n = jnp.zeros((16, 128), F32)
    edge_s = jnp.zeros((16, 128), F32)
    for z in range(NZ):
        x = lev0.w[z + 1, 0:16, 0:128]
        o_ew[0, z] = x[0:4]
        o_ew[1, z] = x[12:16]
        edge_n = jnp.where(lane16 >= 3 * z, roll(x, 3 * z - 125, 1), edge_n)
        edge_s = jnp.where(lane16 >= 3 * z, roll(x, 3 * z, 1), edge_s)
    o_ns[0, 0] = edge_n
    o_ns[1, 0] = edge_s

    mall = restrict_all()

    def down_all(x):
        pair = jnp.concatenate([x[0:HZ], x[HZ:NZ]], axis=2).reshape(HZ * 16, 256)
        return jnp.sum(mm(pair, mall).reshape(HZ, 16, 128), axis=1)

    sea4 = (down_all(mask[...].astype(F32)) > 0.0).astype(F32)
    h_blk[0:10, :] = down_all(kappa[...])
    h_blk[10:20, :] = sea4 * (down_all(lon_diff[...]) * (1.0 / 256))
    h_blk[20:30, :] = sea4 * (down_all(lat_diff[...]) * (1.0 / 256))
    h_blk[30:32, :] = jnp.zeros((2, 128), F32)

    arrive(sent_p2)
    for f in range(4):
        for s in range(7):
            piece = g_p if s == 3 else g_rp.at[s]
            raw2[f, :, 4 * s:4 * s + 4, :] = piece[f * HZ:(f + 1) * HZ]
        raw2[f, :, 28:32, :] = jnp.zeros((HZ, 4, 128), F32)
    lev2.faces(lambda z: raw2[0, z], lambda z: raw2[1, z], lambda z: raw2[2, z], lambda z: raw2[3, z], UNROLL)

    m2 = restrict_2()

    def down_2(x):
        t3[...] = mm(x.reshape(HZ * 32, 128), m2).reshape(HZ, 32, 128)
        return t3[:, pl.ds(0, 16, stride=2), :] + t3[:, pl.ds(1, 16, stride=2), :]

    raw3[0] = down_2(raw2[0])
    raw3[1] = 0.25 * down_2(raw2[1])
    raw3[2] = 0.25 * down_2(raw2[2])
    raw3[3] = (down_2(raw2[3]) > 0.0).astype(F32)
    lev3.faces(lambda z: raw3[0, z], lambda z: raw3[1, z], lambda z: raw3[2, z], lambda z: raw3[3, z], UNROLL)

    arrive(sent_b)
    sent_hz = send_z(h_blk, h_z)

    def put1c(z, start, x):
        lev1.c[z, start:start + 8, :] = x
        lev1.u[z + 1, start:start + 8, :] = x

    merge_1(0, lambda z: q1[z], b_rpk, b_rns, b_rnc, put1c)
    lev1.sweep(lev1.u, lev1.w, UNROLL)

    def remain1(z, r):
        q1[z] = r[8:16]

    lev1.remain(lev1.w, UNROLL, remain1)
    b2 = down_1(q1[...])

    f_p[...] = lev2.g[:, 12:16, :] * b2
    sent_c = send_2(f_p, f_rp)

    arrive(sent_hz)
    row_h = window_row(h_z, 32)
    arrive(sent_c)
    sent_hp = send_plane(row_h, h_ev, 32)
    sent_o = send_edges(o_ew, o_ns, o_rew, o_rns, o_rd)
    for s in range(7):
        piece = f_p if s == 3 else f_rp.at[s]
        lev2.c[:, 4 * s:4 * s + 4, :] = piece[...]
    lev2.c[:, 28:32, :] = jnp.zeros((HZ, 4, 128), F32)
    lev2.start(UNROLL)
    lev2.sweep(lev2.u, lev2.w, UNROLL)

    def remain2(z, r):
        t4[z] = r

    lev2.remain(lev2.w, UNROLL, remain2)

    lev3.c[...] = lev3.g[...] * down_2(t4[...])
    lev3.start(UNROLL)
    lev3.sweep(lev3.u, lev3.w, UNROLL)

    def remain3(z, r):
        t3[z, 0:16, :] = r

    lev3.remain(lev3.w, UNROLL, remain3)
    m3 = restrict_3()
    t3[:, 0:16, :] = mm(t3[:, 0:16, :].reshape(HZ * 16, 128), m3).reshape(HZ, 16, 128)
    for z in range(8):
        row = t3[z, 6:7, :] + t3[z, 7:8, :] + roll(t3[z, 8:9, :] + t3[z, 9:10, :], 8, 1)
        if z < 4:
            at = 6 if z < 2 else 8
            last = t3[8 + z % 2, at:at + 1, :] + t3[8 + z % 2, at + 1:at + 2, :]
            row = row + roll(last, 16, 1)
        k_blk[z:z + 1, :] = row
    sent_kz = send_z(k_blk, k_z)

    arrive(sent_hp)
    sent_hs = send_sibling(h_ev, h_od)

    arrive(sent_kz)
    sent_kp = send_plane(folded_window_row(k_z), k_ev, 24)

    arrive(sent_hs)
    for f in range(3):
        for z in range(HZ):
            def put4(rows, x):
                raw4[f, z, rows, :] = x

            window_slab(h_ev, h_od, f * HZ + z, 32, put4)

    def sea_4(z):
        return (raw4[1, z] > 0.0).astype(F32)

    lev4.faces(lambda z: raw4[0, z], lambda z: raw4[1, z], lambda z: raw4[2, z], sea_4, UNROLL)

    arrive(sent_kp)
    for z in range(HZ):
        for i in range(2):
            at = 8 * i + z if z < 8 else 16 + 2 * i + z - 8
            lev4.c[z, pl.ds(i, 16, stride=2), :] = k_ev[pl.ds(at, 16, stride=24), :]
    for z in range(HZ):
        lev4.c[z] = lev4.g[z] * lev4.c[z]
    lev4.start(UNROLL)

    def two(step, carry):
        lev4.sweep(lev4.u, lev4.w, UNROLL)
        lev4.sweep(lev4.w, lev4.u, UNROLL)
        return carry

    lax.fori_loop(0, 7, two, 0)
    middle = slice(8, 24)
    for src, dst in ((lev4.u, lev4.w), (lev4.w, lev4.u)) * 2 + ((lev4.u, lev4.w),):
        lev4.sweep(src, dst, UNROLL, middle)

    up = mm(lev4.w[1:HZ + 1, 13:21, :].reshape(HZ * 8, 128), prolong_3()).reshape(HZ, 8, 128)
    for start in range(2):
        t3[:, pl.ds(start, 8, stride=2), :] = up

    def add3(z):
        lev3.w[z + 1] = lev3.w[z + 1] + t3[z, 0:16, :]

    lev3.each(add3, UNROLL)
    lev3.wrap(lev3.w)
    lev3.sweep(lev3.w, lev3.u, UNROLL)
    lev3.sweep(lev3.u, lev3.w, UNROLL)

    up = mm(lev3.w[1:HZ + 1].reshape(HZ * 16, 128), prolong_2()).reshape(HZ, 16, 128)
    for start in range(2):
        t3[:, pl.ds(start, 16, stride=2), :] = up

    def add2(z):
        lev2.w[z + 1] = lev2.w[z + 1] + t3[z]

    lev2.each(add2, UNROLL)
    lev2.wrap(lev2.w)
    lev2.sweep(lev2.w, lev2.u, UNROLL)
    lev2.sweep(lev2.u, lev2.w, UNROLL)

    t3[:, 0:16, :] = lev2.w[1:HZ + 1, 8:24, :]
    up = mm(t3[:, 0:16, :].reshape(HZ * 16, 128), prolong_1()).reshape(HZ, 16, 256)
    for start in range(2):
        t1[0:HZ, :, :] = up[:, :, 0:128]
        t1[HZ:NZ, :, :] = up[:, :, 128:256]
    for z in range(NZ):
        for start in range(2):
            q = pl.ds(start, 12, stride=2)
            raw1[0, z, q, :] = t1[z, 0:12, :]

    def add1(z):
        lev1.w[z + 1] = lev1.w[z + 1] + raw1[0, z]

    lev1.each(add1, UNROLL)
    lev1.sweep(lev1.w, lev1.u, UNROLL)
    lev1.sweep(lev1.u, lev1.w, UNROLL)

    arrive(sent_o)

    def put_rows0(z):
        lev0.w[z + 1, 16:20, 0:128] = o_rew[0, z]
        lev0.w[z + 1, 20:24, 0:128] = o_rew[1, z]

    def put_side0(z, x):
        lev0.w[z + 1, :, 128:256] = x

    merge_edges(0, 0, o_rns, o_rd, put_rows0, put_side0)
    for z in range(NZ):
        t1[z, 0:8, :] = lev1.w[z + 1, 8:16, :]
        t1[z, 8:10, :] = lev1.w[z + 1, 16:18, :]
        t1[z, 10:12, :] = lev1.w[z + 1, 6:8, :]
        t1[z, 12:16, :] = jnp.zeros((4, 128), F32)
    up = mm(t1[...].reshape(NZ * 16, 128), prolong_0()).reshape(NZ, 16, 256)
    for z in range(NZ):
        for half in range(2):
            part = up[z, 0:12, 128 * half:128 * half + 128]
            for start in range(2):
                raw1[half, z, pl.ds(start, 12, stride=2), :] = part

    def add0(z):
        for half in range(2):
            lanes = slice(128 * half, 128 * half + 128)
            lev0.w[z + 1, :, lanes] = lev0.w[z + 1, :, lanes] + raw1[half, z]

    lev0.each(add0, UNROLL)
    lev0.sweep(lev0.w, lev0.u, UNROLL)
    lev0.sweep(lev0.u, lev0.w, UNROLL)

    def last0(z, u, total):
        r = raw0[3, z] - (lev0.d[z] * u - total)
        sol[z] = u[0:16, 0:128]
        resid[z] = r[0:16, 0:128]

    lev0.stencil(lev0.w, UNROLL, last0)

    for made in pending:
        made.wait_send()


def level_scratch(slabs, rows, lanes):
    def vmem(count):
        return pltpu.VMEM((count, rows, lanes), F32)

    return [vmem(slabs), vmem(slabs), vmem(slabs + 1), vmem(slabs), vmem(slabs), vmem(slabs), vmem(slabs + 2), vmem(slabs + 2)]


def shards(source, kappa_sq, lon_diff, lat_diff, sea_mask):
    def vmem(*shape):
        return pltpu.VMEM(shape, F32)

    scratch = [
        vmem(NZ, 16, 128), vmem(NZ, 16, 128), vmem(NZ, 16, 128), vmem(NZ, 16, 128),
        pltpu.VMEM((NZ, 16, 128), jnp.int32), pltpu.SemaphoreType.DMA((5,)),
        vmem(4, NZ, 24, 256), vmem(8, 128), level_scratch(NZ, 24, 256),
        vmem(3, NZ, 24, 128), level_scratch(NZ, 24, 128),
        vmem(4, HZ, 32, 128), level_scratch(HZ, 32, 128),
        vmem(4, HZ, 16, 128), level_scratch(HZ, 16, 128),
        vmem(3, HZ, 32, 128), level_scratch(HZ, 32, 128),
        vmem(NZ, 16, 128), vmem(NZ, 16, 128), vmem(HZ, 8, 128), vmem(HZ, 32, 128), vmem(HZ, 32, 128), vmem(NZ, 8, 128),
        vmem(2, 4 * NZ + HZ, 2, 128), vmem(2, 2, 16, 128), vmem(2, 4 * NZ + HZ, 2, 128), vmem(2, 2, 16, 128), vmem(4, 2, 8, 128),
        vmem(HZ, 8, 128), vmem(2, 5, 8, 128), vmem(2, 2, 5, 4, 128),
        vmem(2, HZ, 8, 128), vmem(2, 5, 8, 128), vmem(2, 2, 5, 4, 128),
        vmem(HZ, 4, 128), vmem(7, HZ, 4, 128),
        vmem(8, 128), vmem(7, 8, 128), vmem(16 * 24, 128),
        vmem(3 * HZ, 8, 128), vmem(2, 15, 8, 128), vmem(2, 2, 15, 4, 128),
        vmem(2, 3 * HZ, 8, 128), vmem(2, 15, 8, 128), vmem(2, 2, 15, 4, 128),
        vmem(20, 4, 128), vmem(2, 20, 4, 128),
        vmem(4 * HZ, 4, 128), vmem(7, 4 * HZ, 4, 128),
        vmem(32, 128), vmem(7, 32, 128), vmem(16 * 32, 128), vmem(16 * 32, 128),
        vmem(2, NZ, 4, 128), vmem(2, 1, 16, 128), vmem(2, NZ, 4, 128), vmem(2, 1, 16, 128), vmem(4, 1, 8, 128),
        pltpu.SemaphoreType.DMA((96,)), pltpu.SemaphoreType.DMA((96,)),
    ]
    shape = jax.ShapeDtypeStruct(source.shape, F32)
    anywhere = pl.BlockSpec(memory_space=pl.ANY)
    return pl.pallas_call(
        body,
        out_shape=(shape, shape),
        in_specs=[anywhere] * 5,
        out_specs=[pl.BlockSpec(memory_space=pltpu.VMEM)] * 2,
        scratch_shapes=scratch,
        compiler_params=pltpu.CompilerParams(
            collective_id=0, has_side_effects=True, vmem_limit_bytes=54848 * 1024
        ),
    )(source, kappa_sq, lon_diff, lat_diff, sea_mask)

def solution(mesh):
    spec = P(None, "tx", "ty")
    return jax.shard_map(
        shards, mesh=mesh, in_specs=(spec,) * 5, out_specs=(spec, spec), check_vma=False
    )
```

```python
import jax
import jax.numpy as jnp
from jax import lax
from jax.experimental import pallas as pl
from jax.experimental.pallas import tpu as pltpu
from jax.sharding import PartitionSpec as P

NZ = 20
HZ = 10
NTX = 32
NTY = 16
OMEGA = 0.8
UNROLL = 20
MESH = pl.DeviceIdType.MESH
F32 = jnp.float32

DIAGONALS = ((1, 1), (-1, 1), (1, -1), (-1, -1))


def iota(shape, dim):
    return lax.broadcasted_iota(jnp.int32, shape, dim)


def mm(x, m):
    high = x.astype(jnp.bfloat16)
    low = (x - high.astype(F32)).astype(jnp.bfloat16)
    m = m.astype(jnp.bfloat16)
    return lax.dot_general(
        jnp.concatenate([high, low], axis=1), jnp.concatenate([m, m], axis=0),
        (((1,), (0,)), ((), ())), preferred_element_type=F32,
    )


def roll(x, shift, axis):
    shift = shift % x.shape[axis]
    return x if shift == 0 else pltpu.roll(x, shift, axis)


def one_hot(shape, hit, value=1.0):
    row, col = iota(shape, 0), iota(shape, 1)
    return jnp.where(hit(row, col), F32(value), F32(0.0))


def restrict_0():
    return one_hot((128, 128), lambda n, m: m == 32 + (n >> 1), 0.25)


def restrict_1():
    return one_hot((256, 128), lambda n, m: m == n >> 1, 0.25)


def restrict_2():
    return one_hot((128, 128), lambda n, m: m == (n & 64) + 8 + ((n & 63) >> 1), 0.25)


def restrict_3():
    def hit(n, m):
        q = n & 63
        return (m == (n & 64) + 16 + (q >> 1)) & (q >= 16) & (q < 32)

    return one_hot((128, 128), hit, 0.25)


def restrict_all():
    return one_hot((256, 128), lambda n, m: m == ((n & 128) >> 1) + 24 + ((n & 127) >> 4), 1.0 / 256)


def prolong_3():
    return one_hot((128, 128), lambda m, n: m == (n & 64) + 16 + ((n & 63) >> 1))


def prolong_2():
    return one_hot((128, 128), lambda m, n: m == (n & 64) + 8 + ((n & 63) >> 1))


def prolong_1():
    return one_hot((128, 256), lambda m, n: m == n >> 1)


def prolong_0():
    def hit(m, n):
        rel = jnp.where(n >= 192, n - 256, n)
        return (m == 32 + (rel >> 1)) & (rel < 132) & (rel >= -4)

    return one_hot((128, 256), hit)


class Level:
    def __init__(self, slabs, folded, refs):
        self.slabs = slabs
        self.folded = folded
        self.e, self.n, self.v, self.g, self.d, self.c, self.u, self.w = refs

    def each(self, body, unroll):
        def step(z, carry):
            body(z)
            return carry

        lax.fori_loop(0, self.slabs, step, 0, unroll=min(unroll, self.slabs))

    def wrap(self, ref, rows=slice(None)):
        if self.folded:
            ref[0, rows] = roll(ref[self.slabs, rows], 64, 1)
            ref[self.slabs + 1, rows] = roll(ref[1, rows], 64, 1)

    def clear_ends(self):
        if not self.folded:
            for ref in (self.u, self.w):
                ref[0] = jnp.zeros_like(ref[0])
                ref[self.slabs + 1] = jnp.zeros_like(ref[0])

    def faces(self, kap, lond, latd, sea, unroll):
        top = self.slabs - 1

        def vertical(z):
            here = sea(z)
            self.v[z + 1] = here * sea(z + 1)

        lax.fori_loop(0, top, lambda z, c: (vertical(z), c)[1], 0, unroll=min(unroll, top))
        if self.folded:
            low = iota(self.v.shape[1:], 1) < 64
            self.v[self.slabs] = jnp.where(low, sea(top) * roll(sea(0), 64, 1), 0.0)
            self.v[0] = roll(self.v[self.slabs], 64, 1)
        else:
            self.v[0] = jnp.zeros_like(self.v[0])
            self.v[self.slabs] = jnp.zeros_like(self.v[0])

        def horizontal(z):
            s = sea(z)
            lw = s * lond(z)
            tw = s * latd(z)
            east = 0.5 * (lw * roll(s, -1, 0) + s * roll(lw, -1, 0))
            north = 0.5 * (tw * roll(s, -1, 1) + s * roll(tw, -1, 1))
            west = roll(east, 1, 0)
            south = roll(north, 1, 1)
            diag = s * kap(z) + (west + east + south + north + self.v[z] + self.v[z + 1]) + (1.0 - s)
            self.e[z] = east
            self.n[z] = north
            self.d[z] = diag
            self.g[z] = OMEGA / diag

        self.each(horizontal, unroll)

    def stencil(self, src, unroll, use, rows=slice(None)):
        def step(z, carry):
            below, u, face_below = carry
            above = src[z + 2, rows]
            face_above = self.v[z + 1, rows]
            e = self.e[z, rows]
            n = self.n[z, rows]
            use(z, u, (
                roll(e * u, 1, 0)
                + e * roll(u, -1, 0)
                + roll(n * u, 1, 1)
                + n * roll(u, -1, 1)
                + face_below * below
                + face_above * above
            ))
            return u, above, face_above

        lax.fori_loop(0, self.slabs, step, (src[0, rows], src[1, rows], self.v[0, rows]), unroll=min(unroll, self.slabs))

    def sweep(self, src, dst, unroll, rows=slice(None)):
        def use(z, u, total):
            dst[z + 1, rows] = (1.0 - OMEGA) * u + self.c[z, rows] + self.g[z, rows] * total

        self.stencil(src, unroll, use, rows)
        self.wrap(dst, rows)

    def start(self, unroll):
        def body(z):
            self.u[z + 1] = self.c[z]

        self.each(body, unroll)
        self.wrap(self.u)

    def remain(self, src, unroll, put):
        self.stencil(src, unroll, lambda z, u, total: put(z, self.d[z] * (1.25 * self.c[z] - u) + total))


def pack_edge(slabs, width, base, count):
    lane = iota(slabs[0].shape, 1)
    out = roll(slabs[0], -base, 1)
    for i in range(1, count):
        out = jnp.where(lane >= width * i, roll(slabs[i], width * i - base, 1), out)
    return out


def body(
    source_in, kappa_in, lon_in, lat_in, mask_in,
    sol, resid,
    source, kappa, lon_diff, lat_diff, mask, in_sem,
    raw0, src0, l0, raw1, l1, raw2, l2, raw3, l3, raw4, l4, t0, t1, t2, t3, t4, q1,
    a_ew, a_ns, a_rew, a_rns, a_rd,
    b_pk, b_ns, b_nc, b_rpk, b_rns, b_rnc,
    f_p, f_rp,
    k_blk, k_z, k_ev,
    p_pk, p_ns, p_nc, p_rpk, p_rns, p_rnc, q_p, q_rp, g_p, g_rp, h_blk, h_z, h_ev, h_od,
    o_ew, o_ns, o_rew, o_rns, o_rd,
    send_sem, recv_sem,
):
    mx, my = lax.axis_index("tx"), lax.axis_index("ty")
    odd = lax.rem(mx, 2) == 1
    counter = [0]
    pending = []
    places = {}

    def shifted(axis, here, shift, count):
        shift = shift % count
        if (axis, shift) not in places:
            there = here + shift
            places[axis, shift] = jnp.where(there >= count, there - count, there) if shift else here
        return places[axis, shift]

    def device(dx, dy):
        return (shifted(0, mx, dx, NTX), shifted(1, my, dy, NTY))

    def copy(src, dst, dx, dy):
        i = counter[0]
        counter[0] += 1
        made = pltpu.make_async_remote_copy(
            src_ref=src, dst_ref=dst, send_sem=send_sem.at[i], recv_sem=recv_sem.at[i],
            device_id=device(dx, dy),
            device_id_type=MESH,
        )
        made.start()
        pending.append(made)
        return made

    def arrive(copies):
        for made in copies:
            made.wait_recv()

    lev0 = Level(NZ, False, l0)
    lev1 = Level(NZ, False, l1)
    lev2 = Level(HZ, True, l2)
    lev3 = Level(HZ, True, l3)
    lev4 = Level(HZ, True, l4)

    fetched = [
        pltpu.make_async_copy(src, dst, in_sem.at[i])
        for i, (src, dst) in enumerate((
            (mask_in, mask), (lon_in, lon_diff), (lat_in, lat_diff), (kappa_in, kappa), (source_in, source)
        ))
    ]
    for made in fetched:
        made.start()

    peers = [(2 * k, 0) for k in range(1, 16)] + [(1, 0), (-1, 0), (3, 0), (-3, 0)]
    peers += [(0, d) for d in (1, 2, 3, -1, -2, -3)] + list(DIAGONALS)
    barrier = pltpu.get_barrier_semaphore()
    for dx, dy in peers:
        pl.semaphore_signal(
            barrier, inc=1,
            device_id=device(dx, dy),
            device_id_type=MESH,
        )

    lane16 = iota((16, 128), 1)
    place = ((1, 0), (0, 0), (0, 60), (1, 60))
    edge_n = [jnp.zeros((16, 128), F32)] * 4
    edge_s = [jnp.zeros((16, 128), F32)] * 4
    own0 = (
        lambda z: kappa[z],
        lambda z: mask[z].astype(F32) * lon_diff[z],
        lambda z: mask[z].astype(F32) * lat_diff[z],
        lambda z: source[z],
    )
    for f, needed in ((1, (0, 1)), (2, (2,)), (0, (3,)), (3, (4,))):
        for i in needed:
            fetched[i].wait()
        for z in range(NZ):
            x = own0[f](z)
            raw0[f, z, 0:16, 0:128] = x
            a_ew[0, f * NZ + z] = x[0:2]
            a_ew[1, f * NZ + z] = x[14:16]
            if f == 1:
                a_ew[0, 4 * NZ + z // 2, z % 2:z % 2 + 1] = x[2:3]
                a_ew[1, 4 * NZ + z // 2, z % 2:z % 2 + 1] = x[13:14]
            start = place[f][1] + 3 * z
            edge_n[f] = jnp.where(lane16 >= start, roll(x, start - 125, 1), edge_n[f])
            edge_s[f] = jnp.where(lane16 >= start, roll(x, start, 1), edge_s[f])
    for pair, (f, g) in enumerate(((1, 2), (0, 3))):
        a_ns[0, pair] = jnp.where(lane16 < 60, edge_n[f], edge_n[g])
        a_ns[1, pair] = jnp.where(lane16 < 60, edge_s[f], edge_s[g])

    pl.semaphore_wait(barrier, len(peers))

    def send_edges(ew, ns, rew, rns, rd):
        made = [copy(ns.at[0, :, 8:16, :], rd.at[0], 1, 1)]
        made.append(copy(ns.at[0, :, 0:8, :], rd.at[1], -1, 1))
        made.append(copy(ns.at[1, :, 8:16, :], rd.at[2], 1, -1))
        made.append(copy(ns.at[1, :, 0:8, :], rd.at[3], -1, -1))
        made += [copy(ew.at[0], rew.at[0], -1, 0), copy(ew.at[1], rew.at[1], 1, 0)]
        made += [copy(ns.at[0], rns.at[0], 0, 1), copy(ns.at[1], rns.at[1], 0, -1)]
        return made

    has_s, has_n = my > 0, my < NTY - 1

    def merge_edges(f, base, rns, rd, put_rows, put_side):
        sub = iota((8, 128), 0)
        south = jnp.concatenate([rns[0, f], jnp.where(sub < 4, rd[1, f], rd[0, f])], axis=0)
        north = jnp.concatenate([rns[1, f], jnp.where(sub < 4, rd[3, f], rd[2, f])], axis=0)
        lane = iota((24, 128), 1)
        south = jnp.where(has_s, south, 0.0)
        north = jnp.where(has_n, north, 0.0)
        for z in range(NZ):
            put_rows(z)
            start = base + 3 * z
            side = jnp.where(lane < 3, roll(north, -start, 1), roll(south, 125 - start, 1))
            put_side(z, jnp.where((lane < 3) | (lane >= 125), side, 0.0))

    sent_a = send_edges(a_ew, a_ns, a_rew, a_rns, a_rd)
    for f in range(4):
        for z in range(NZ):
            raw0[f, z, 16:24, 0:128] = jnp.zeros((8, 128), F32)

    m0 = restrict_0()

    def down_0(x):
        t1[...] = mm(x.reshape(NZ * 16, 128), m0).reshape(NZ, 16, 128)
        return t1[:, pl.ds(0, 8, stride=2), :] + t1[:, pl.ds(1, 8, stride=2), :]

    def pack_1(x, f, pk, ns, nc):
        lane = iota((8, 128), 1)
        for k in range(HZ):
            pk[f * HZ + k] = jnp.where(lane < 64, roll(x[k], -32, 1), roll(x[k + HZ], 32, 1))
        for k in range(5):
            group = [x[k + 5 * j] for j in range(4)]
            for side, base in ((0, 64), (1, 32)):
                edge = pack_edge(group, 32, base, 4)
                ns[side, f * 5 + k] = edge
                nc[side, 0, f * 5 + k] = edge[0:4]
                nc[side, 1, f * 5 + k] = edge[4:8]

    def send_1(pk, ns, nc, rpk, rns, rnc):
        made = [copy(nc.at[0, 1], rnc.at[0, 1], 1, 1)]
        made.append(copy(nc.at[0, 0], rnc.at[0, 0], -1, 1))
        made.append(copy(nc.at[1, 1], rnc.at[1, 1], 1, -1))
        made.append(copy(nc.at[1, 0], rnc.at[1, 0], -1, -1))
        made += [copy(pk, rpk.at[0], -1, 0), copy(pk, rpk.at[1], 1, 0)]
        made += [copy(ns.at[0], rns.at[0], 0, 1), copy(ns.at[1], rns.at[1], 0, -1)]
        return made

    def merge_1(f, own, rpk, rns, rnc, put):
        lane = iota((8, 128), 1)
        blank = jnp.zeros((4, 128), F32)

        def edge(side, i, at):
            if i == 0:
                return rns[side, at]
            if i == 1:
                return jnp.concatenate([rnc[side, 0, at], blank], axis=0)
            return jnp.concatenate([blank, rnc[side, 1, at]], axis=0)

        for z in range(NZ):
            k, shift = (z, 32) if z < HZ else (z - HZ, -32)
            middle = (own(z), roll(rpk[0, f * HZ + k], shift, 1), roll(rpk[1, f * HZ + k], shift, 1))
            for i, start in ((0, 8), (1, 16), (2, 0)):
                south = jnp.where(has_s, roll(edge(0, i, f * 5 + z % 5), -32 * (z // 5), 1), 0.0)
                north = jnp.where(has_n, roll(edge(1, i, f * 5 + z % 5), 96 - 32 * (z // 5), 1), 0.0)
                put(z, start, jnp.where(lane < 32, south, jnp.where(lane < 96, middle[i], north)))

    own1 = [
        down_0(kappa[...]),
        0.25 * down_0(lon_diff[...]),
        0.25 * down_0(lat_diff[...]),
        (down_0(mask[...].astype(F32)) > 0.0).astype(F32),
    ]

    m1 = restrict_1()

    def down_1(x):
        pair = jnp.concatenate([x[0:HZ], x[HZ:NZ]], axis=2).reshape(HZ * 8, 256)
        t2[...] = mm(pair, m1).reshape(HZ, 8, 128)
        return t2[:, pl.ds(0, 4, stride=2), :] + t2[:, pl.ds(1, 4, stride=2), :]

    own2 = [
        down_1(own1[0]),
        0.25 * down_1(own1[1]),
        0.25 * down_1(own1[2]),
        (down_1(own1[3]) > 0.0).astype(F32),
    ]
    for f in range(4):
        g_p[f * HZ:(f + 1) * HZ] = own2[f]
        for k in range(5):
            q_p[f * 5 + k] = own2[f][k] + roll(own2[f][k + 5], 32, 1)
    sent_q = [copy(q_p, q_rp.at[0], 0, 1), copy(q_p, q_rp.at[1], 0, -1)]

    for f, x in enumerate((own1[0], own1[3] * own1[1], own1[3] * own1[2])):
        pack_1(x, f, p_pk, p_ns, p_nc)
        raw1[f, :, 8:16, :] = x
    sent_p1 = send_1(p_pk, p_ns, p_nc, p_rpk, p_rns, p_rnc)

    def send_z(blk, slots):
        slots[3] = blk[...]
        return [copy(blk, slots.at[3 - d], 0, d) for d in (3, -3, 2, -2, 1, -1)]

    def window_row(slots, count):
        row = jnp.zeros((count, 128), F32)
        for s in range(7):
            inside = (my + (s - 3) >= 0) & (my + (s - 3) < NTY)
            row = row + jnp.where(inside, roll(slots[s], 8 * (s - 3), 1), 0.0)
        return row

    def folded_window_row(slots):
        part = iota((8, 128), 1) & 63
        out = [jnp.zeros((8, 128), F32)] * 3
        for s in range(7):
            inside = (my + (s - 3) >= 0) & (my + (s - 3) < NTY)
            block = jnp.where(inside, slots[s], 0.0)
            for i in range(3):
                pick = (part >= 24 + 8 * i) & (part < 32 + 8 * i)
                out[i] = out[i] + roll(jnp.where(pick, block, 0.0), 8 * (s - 3 - i), 1)
        return jnp.concatenate(out, axis=0)

    def send_plane(row, ev, count):
        own = pl.ds(8 * count, count)
        ev[own, :] = row
        return [
            copy(ev.at[own], ev.at[pl.ds(((8 - k) % 16) * count, count)], 2 * k, 0)
            for k in (10, 6, 9, 7, 11, 5, 2, 14, 8, 3, 13, 1, 15, 4, 12)
        ]

    def send_sibling(ev, od):
        i = counter[0]
        counter[0] += 1
        made = pltpu.make_async_remote_copy(
            src_ref=ev, dst_ref=od, send_sem=send_sem.at[i], recv_sem=recv_sem.at[i],
            device_id=(mx + 1 - 2 * lax.rem(mx, 2), my), device_id_type=MESH,
        )
        made.start()
        pending.append(made)
        return [made]

    def window_slab(ev, od, index, count, put):
        put(pl.ds(0, 16, stride=2), ev[pl.ds(index, 16, stride=count), :])
        other = od[pl.ds(index, 16, stride=count), :]
        put(pl.ds(1, 16, stride=2), jnp.where(odd, roll(other, -1, 0), other))

    arrive(sent_a)
    for f in range(4):
        def put_rows(z):
            raw0[f, z, 16:18, 0:128] = a_rew[0, f * NZ + z]
            raw0[f, z, 22:24, 0:128] = a_rew[1, f * NZ + z]
            if f == 1:
                pick = slice(z % 2, z % 2 + 1)
                raw0[f, z, 18:19, 0:128] = a_rew[0, 4 * NZ + z // 2, pick]
                raw0[f, z, 21:22, 0:128] = a_rew[1, 4 * NZ + z // 2, pick]

        def put_side(z, x):
            raw0[f, z, :, 128:256] = x

        merge_edges(place[f][0], place[f][1], a_rns, a_rd, put_rows, put_side)

    def send_2(p, rp):
        return [copy(p, rp.at[3 - d], d, 0) for d in (3, -3, 2, -2, 1, -1)]

    arrive(sent_q)
    part = iota((4, 128), 1) & 63
    for f in range(4):
        for k in range(HZ):
            south = roll(q_rp[0, f * 5 + k % 5], -32 if k < 5 else -64, 1)
            north = roll(q_rp[1, f * 5 + k % 5], 32 if k < 5 else 0, 1)
            south = jnp.where(has_s, south, 0.0)
            north = jnp.where(has_n, north, 0.0)
            g_p[f * HZ + k] = jnp.where(part < 16, south, jnp.where(part < 48, g_p[f * HZ + k], north))
    sent_p2 = send_2(g_p, g_rp)

    def sea0(z):
        return (raw0[1, z] > 0.0).astype(F32)

    lev0.faces(lambda z: raw0[0, z], lambda z: raw0[1, z], lambda z: raw0[2, z], sea0, UNROLL)
    lev0.clear_ends()


    def first0(z):
        c = lev0.g[z] * raw0[3, z]
        lev0.c[z] = c
        lev0.u[z + 1] = c

    lev0.each(first0, UNROLL)
    lev0.sweep(lev0.u, lev0.w, UNROLL)

    def remain0(z, u, total):
        r = raw0[3, z] - (lev0.d[z] * u - total)
        t0[z] = r[0:16, 0:128]

    lev0.stencil(lev0.w, UNROLL, remain0)
    b1 = down_0(t0[...])

    arrive(sent_p1)
    for f in range(3):
        def put1(z, start, x):
            raw1[f, z, start:start + 8, :] = x

        merge_1(f, lambda z: raw1[f, z, 8:16, :], p_rpk, p_rns, p_rnc, put1)

    def sea_1(z):
        return (raw1[1, z] > 0.0).astype(F32)

    lev1.faces(lambda z: raw1[0, z], lambda z: raw1[1, z], lambda z: raw1[2, z], sea_1, UNROLL)
    lev1.clear_ends()
    c1 = lev1.g[:, 8:16, :] * b1
    q1[...] = c1
    pack_1(c1, 0, b_pk, b_ns, b_nc)
    sent_b = send_1(b_pk, b_ns, b_nc, b_rpk, b_rns, b_rnc)

    edge_n = jnp.zeros((16, 128), F32)
    edge_s = jnp.zeros((16, 128), F32)
    for z in range(NZ):
        x = lev0.w[z + 1, 0:16, 0:128]
        o_ew[0, z] = x[0:4]
        o_ew[1, z] = x[12:16]
        edge_n = jnp.where(lane16 >= 3 * z, roll(x, 3 * z - 125, 1), edge_n)
        edge_s = jnp.where(lane16 >= 3 * z, roll(x, 3 * z, 1), edge_s)
    o_ns[0, 0] = edge_n
    o_ns[1, 0] = edge_s

    mall = restrict_all()

    def down_all(x):
        pair = jnp.concatenate([x[0:HZ], x[HZ:NZ]], axis=2).reshape(HZ * 16, 256)
        return jnp.sum(mm(pair, mall).reshape(HZ, 16, 128), axis=1)

    sea4 = (down_all(mask[...].astype(F32)) > 0.0).astype(F32)
    h_blk[0:10, :] = down_all(kappa[...])
    h_blk[10:20, :] = sea4 * (down_all(lon_diff[...]) * (1.0 / 256))
    h_blk[20:30, :] = sea4 * (down_all(lat_diff[...]) * (1.0 / 256))
    h_blk[30:32, :] = jnp.zeros((2, 128), F32)

    arrive(sent_p2)
    for f in range(4):
        for s in range(7):
            piece = g_p if s == 3 else g_rp.at[s]
            raw2[f, :, 4 * s:4 * s + 4, :] = piece[f * HZ:(f + 1) * HZ]
        raw2[f, :, 28:32, :] = jnp.zeros((HZ, 4, 128), F32)
    lev2.faces(lambda z: raw2[0, z], lambda z: raw2[1, z], lambda z: raw2[2, z], lambda z: raw2[3, z], UNROLL)

    m2 = restrict_2()

    def down_2(x):
        t3[...] = mm(x.reshape(HZ * 32, 128), m2).reshape(HZ, 32, 128)
        return t3[:, pl.ds(0, 16, stride=2), :] + t3[:, pl.ds(1, 16, stride=2), :]

    raw3[0] = down_2(raw2[0])
    raw3[1] = 0.25 * down_2(raw2[1])
    raw3[2] = 0.25 * down_2(raw2[2])
    raw3[3] = (down_2(raw2[3]) > 0.0).astype(F32)
    lev3.faces(lambda z: raw3[0, z], lambda z: raw3[1, z], lambda z: raw3[2, z], lambda z: raw3[3, z], UNROLL)

    arrive(sent_b)
    sent_hz = send_z(h_blk, h_z)

    def put1c(z, start, x):
        lev1.c[z, start:start + 8, :] = x
        lev1.u[z + 1, start:start + 8, :] = x

    merge_1(0, lambda z: q1[z], b_rpk, b_rns, b_rnc, put1c)
    lev1.sweep(lev1.u, lev1.w, UNROLL)

    def remain1(z, r):
        q1[z] = r[8:16]

    lev1.remain(lev1.w, UNROLL, remain1)
    b2 = down_1(q1[...])

    f_p[...] = lev2.g[:, 12:16, :] * b2
    sent_c = send_2(f_p, f_rp)

    arrive(sent_hz)
    row_h = window_row(h_z, 32)
    arrive(sent_c)
    sent_hp = send_plane(row_h, h_ev, 32)
    sent_o = send_edges(o_ew, o_ns, o_rew, o_rns, o_rd)
    for s in range(7):
        piece = f_p if s == 3 else f_rp.at[s]
        lev2.c[:, 4 * s:4 * s + 4, :] = piece[...]
    lev2.c[:, 28:32, :] = jnp.zeros((HZ, 4, 128), F32)
    lev2.start(UNROLL)
    lev2.sweep(lev2.u, lev2.w, UNROLL)

    def remain2(z, r):
        t4[z] = r

    lev2.remain(lev2.w, UNROLL, remain2)

    lev3.c[...] = lev3.g[...] * down_2(t4[...])
    lev3.start(UNROLL)
    lev3.sweep(lev3.u, lev3.w, UNROLL)

    def remain3(z, r):
        t3[z, 0:16, :] = r

    lev3.remain(lev3.w, UNROLL, remain3)
    m3 = restrict_3()
    t3[:, 0:16, :] = mm(t3[:, 0:16, :].reshape(HZ * 16, 128), m3).reshape(HZ, 16, 128)
    for z in range(8):
        row = t3[z, 6:7, :] + t3[z, 7:8, :] + roll(t3[z, 8:9, :] + t3[z, 9:10, :], 8, 1)
        if z < 4:
            at = 6 if z < 2 else 8
            last = t3[8 + z % 2, at:at + 1, :] + t3[8 + z % 2, at + 1:at + 2, :]
            row = row + roll(last, 16, 1)
        k_blk[z:z + 1, :] = row
    sent_kz = send_z(k_blk, k_z)

    arrive(sent_hp)
    sent_hs = send_sibling(h_ev, h_od)

    arrive(sent_kz)
    sent_kp = send_plane(folded_window_row(k_z), k_ev, 24)

    arrive(sent_hs)
    for f in range(3):
        for z in range(HZ):
            def put4(rows, x):
                raw4[f, z, rows, :] = x

            window_slab(h_ev, h_od, f * HZ + z, 32, put4)

    def sea_4(z):
        return (raw4[1, z] > 0.0).astype(F32)

    lev4.faces(lambda z: raw4[0, z], lambda z: raw4[1, z], lambda z: raw4[2, z], sea_4, UNROLL)

    arrive(sent_kp)
    for z in range(HZ):
        for i in range(2):
            at = 8 * i + z if z < 8 else 16 + 2 * i + z - 8
            lev4.c[z, pl.ds(i, 16, stride=2), :] = k_ev[pl.ds(at, 16, stride=24), :]
    for z in range(HZ):
        lev4.c[z] = lev4.g[z] * lev4.c[z]
    lev4.start(UNROLL)

    def two(step, carry):
        lev4.sweep(lev4.u, lev4.w, UNROLL)
        lev4.sweep(lev4.w, lev4.u, UNROLL)
        return carry

    lax.fori_loop(0, 7, two, 0)
    middle = slice(8, 24)
    for src, dst in ((lev4.u, lev4.w), (lev4.w, lev4.u)) * 2 + ((lev4.u, lev4.w),):
        lev4.sweep(src, dst, UNROLL, middle)

    up = mm(lev4.w[1:HZ + 1, 13:21, :].reshape(HZ * 8, 128), prolong_3()).reshape(HZ, 8, 128)
    for start in range(2):
        t3[:, pl.ds(start, 8, stride=2), :] = up

    def add3(z):
        lev3.w[z + 1] = lev3.w[z + 1] + t3[z, 0:16, :]

    lev3.each(add3, UNROLL)
    lev3.wrap(lev3.w)
    lev3.sweep(lev3.w, lev3.u, UNROLL)
    lev3.sweep(lev3.u, lev3.w, UNROLL)

    up = mm(lev3.w[1:HZ + 1].reshape(HZ * 16, 128), prolong_2()).reshape(HZ, 16, 128)
    for start in range(2):
        t3[:, pl.ds(start, 16, stride=2), :] = up

    def add2(z):
        lev2.w[z + 1] = lev2.w[z + 1] + t3[z]

    lev2.each(add2, UNROLL)
    lev2.wrap(lev2.w)
    lev2.sweep(lev2.w, lev2.u, UNROLL)
    lev2.sweep(lev2.u, lev2.w, UNROLL)

    t3[:, 0:16, :] = lev2.w[1:HZ + 1, 8:24, :]
    up = mm(t3[:, 0:16, :].reshape(HZ * 16, 128), prolong_1()).reshape(HZ, 16, 256)
    for start in range(2):
        t1[0:HZ, :, :] = up[:, :, 0:128]
        t1[HZ:NZ, :, :] = up[:, :, 128:256]
    for z in range(NZ):
        for start in range(2):
            q = pl.ds(start, 12, stride=2)
            raw1[0, z, q, :] = t1[z, 0:12, :]

    def add1(z):
        lev1.w[z + 1] = lev1.w[z + 1] + raw1[0, z]

    lev1.each(add1, UNROLL)
    lev1.sweep(lev1.w, lev1.u, UNROLL)
    lev1.sweep(lev1.u, lev1.w, UNROLL)

    arrive(sent_o)

    def put_rows0(z):
        lev0.w[z + 1, 16:20, 0:128] = o_rew[0, z]
        lev0.w[z + 1, 20:24, 0:128] = o_rew[1, z]

    def put_side0(z, x):
        lev0.w[z + 1, :, 128:256] = x

    merge_edges(0, 0, o_rns, o_rd, put_rows0, put_side0)
    for z in range(NZ):
        t1[z, 0:8, :] = lev1.w[z + 1, 8:16, :]
        t1[z, 8:10, :] = lev1.w[z + 1, 16:18, :]
        t1[z, 10:12, :] = lev1.w[z + 1, 6:8, :]
        t1[z, 12:16, :] = jnp.zeros((4, 128), F32)
    up = mm(t1[...].reshape(NZ * 16, 128), prolong_0()).reshape(NZ, 16, 256)
    for z in range(NZ):
        for half in range(2):
            part = up[z, 0:12, 128 * half:128 * half + 128]
            for start in range(2):
                raw1[half, z, pl.ds(start, 12, stride=2), :] = part

    def add0(z):
        for half in range(2):
            lanes = slice(128 * half, 128 * half + 128)
            lev0.w[z + 1, :, lanes] = lev0.w[z + 1, :, lanes] + raw1[half, z]

    lev0.each(add0, UNROLL)
    lev0.sweep(lev0.w, lev0.u, UNROLL)
    lev0.sweep(lev0.u, lev0.w, UNROLL)

    def last0(z, u, total):
        r = raw0[3, z] - (lev0.d[z] * u - total)
        sol[z] = u[0:16, 0:128]
        resid[z] = r[0:16, 0:128]

    lev0.stencil(lev0.w, UNROLL, last0)

    for made in pending:
        made.wait_send()


def deliver(sol_in, resid_in, sol_out, resid_out, sem):
    copies = [
        pltpu.make_async_copy(sol_in, sol_out, sem.at[0]),
        pltpu.make_async_copy(resid_in, resid_out, sem.at[1]),
    ]
    for made in copies:
        made.start()
    for made in copies:
        made.wait()


def level_scratch(slabs, rows, lanes):
    def vmem(count):
        return pltpu.VMEM((count, rows, lanes), F32)

    return [vmem(slabs), vmem(slabs), vmem(slabs + 1), vmem(slabs), vmem(slabs), vmem(slabs), vmem(slabs + 2), vmem(slabs + 2)]


def shards(source, kappa_sq, lon_diff, lat_diff, sea_mask):
    def vmem(*shape):
        return pltpu.VMEM(shape, F32)

    scratch = [
        vmem(NZ, 16, 128), vmem(NZ, 16, 128), vmem(NZ, 16, 128), vmem(NZ, 16, 128),
        pltpu.VMEM((NZ, 16, 128), jnp.int32), pltpu.SemaphoreType.DMA((5,)),
        vmem(4, NZ, 24, 256), vmem(8, 128), level_scratch(NZ, 24, 256),
        vmem(3, NZ, 24, 128), level_scratch(NZ, 24, 128),
        vmem(4, HZ, 32, 128), level_scratch(HZ, 32, 128),
        vmem(4, HZ, 16, 128), level_scratch(HZ, 16, 128),
        vmem(3, HZ, 32, 128), level_scratch(HZ, 32, 128),
        vmem(NZ, 16, 128), vmem(NZ, 16, 128), vmem(HZ, 8, 128), vmem(HZ, 32, 128), vmem(HZ, 32, 128), vmem(NZ, 8, 128),
        vmem(2, 4 * NZ + HZ, 2, 128), vmem(2, 2, 16, 128), vmem(2, 4 * NZ + HZ, 2, 128), vmem(2, 2, 16, 128), vmem(4, 2, 8, 128),
        vmem(HZ, 8, 128), vmem(2, 5, 8, 128), vmem(2, 2, 5, 4, 128),
        vmem(2, HZ, 8, 128), vmem(2, 5, 8, 128), vmem(2, 2, 5, 4, 128),
        vmem(HZ, 4, 128), vmem(7, HZ, 4, 128),
        vmem(8, 128), vmem(7, 8, 128), vmem(16 * 24, 128),
        vmem(3 * HZ, 8, 128), vmem(2, 15, 8, 128), vmem(2, 2, 15, 4, 128),
        vmem(2, 3 * HZ, 8, 128), vmem(2, 15, 8, 128), vmem(2, 2, 15, 4, 128),
        vmem(20, 4, 128), vmem(2, 20, 4, 128),
        vmem(4 * HZ, 4, 128), vmem(7, 4 * HZ, 4, 128),
        vmem(32, 128), vmem(7, 32, 128), vmem(16 * 32, 128), vmem(16 * 32, 128),
        vmem(2, NZ, 4, 128), vmem(2, 1, 16, 128), vmem(2, NZ, 4, 128), vmem(2, 1, 16, 128), vmem(4, 1, 8, 128),
        pltpu.SemaphoreType.DMA((96,)), pltpu.SemaphoreType.DMA((96,)),
    ]
    shape = jax.ShapeDtypeStruct(source.shape, F32)
    anywhere = pl.BlockSpec(memory_space=pl.ANY)
    found = pl.pallas_call(
        body,
        out_shape=(shape, shape),
        in_specs=[anywhere] * 5,
        out_specs=[pl.BlockSpec(memory_space=pltpu.VMEM)] * 2,
        scratch_shapes=scratch,
        compiler_params=pltpu.CompilerParams(
            collective_id=0, has_side_effects=True, vmem_limit_bytes=54848 * 1024
        ),
    )(source, kappa_sq, lon_diff, lat_diff, sea_mask)
    return pl.pallas_call(
        deliver,
        out_shape=(shape, shape),
        in_specs=[pl.BlockSpec(memory_space=pltpu.VMEM)] * 2,
        out_specs=[anywhere] * 2,
        scratch_shapes=[pltpu.SemaphoreType.DMA((2,))],
    )(*found)

def solution(mesh):
    spec = P(None, "tx", "ty")
    return jax.shard_map(
        shards, mesh=mesh, in_specs=(spec,) * 5, out_specs=(spec, spec), check_vma=False
    )
```
